128 devices in a mesh: gx: 8 (over y_hi, z), gy: 16 (over x, y_lo, core).
Axes of the slice: x: 4, y: 4 (y_hi: 2, y_lo: 2; y = y_hi * 2 + y_lo), z: 4, core: 2. Of those that a mesh axis runs over, the one named last changes fastest.
Arguments:
- well_cell: int32 [65536], P(('gx', 'gy')), may hold values from 0 to 4194303, as said below
- well_test: int32 [65536], P(('gx', 'gy')), may hold values from 0 to 3
- well_value: float32 [65536], P(('gx', 'gy')), may hold values from -6 to 6
- cond_class: int32 [32, 64, 2048], P('gx', None, 'gy'), may hold values from 0 to 15
- class_value: float32 [16], replicated, may hold values from 0.1 to 3
- zone_id: int32 [32, 64, 2048], P('gx', None, 'gy'), may hold values from 0 to 98303
- drawdown: bfloat16 [4, 32, 64, 2048], P(None, 'gx', None, 'gy'), may hold values from -6 to 6
- centroid: float32 [3, 98304], replicated, may hold values from 0 to 1
Outputs:
- prior_product: bfloat16 [4, 98304], P(None, ('gx', 'gy'))
The draws below stay inside these ranges and needn't reach their ends.
Inputs may be any that keep to these rules, and one draw needn't show every extreme that they name: `well_cell`: rows s * 512 to (s + 1) * 512 - 1 belong to device s (gx first). At most 16 of one device's rows lie in the cells of any one device, and in every draw some device holds 16 rows of every device's block.
All inputs are finite; a program needn't handle non-finite values.
Results may differ from the reference program's by a relative error of at most 0.0065.
Values may be sent and summed in bfloat16 or wider, within the bound.
A program may use at most 192 MiB of HBM per device.

```python
import math
import jax
import jax.numpy as jnp
from jax import lax

TESTS = 4
CX = 4
CY = 128
NZ = 64
SWEEPS = 12
NCLASS = 16
ZONES = 98304
WELL_DEV = 512
CAP = 16
NX = 32
NY = 2048
WELLS = 65536
N_GX = 8
N_GY = 16


def draw_well_cell(key, part):
    key = jax.random.fold_in(key, 11)
    devices = N_GX * N_GY
    keys = jax.random.split(key, 6)
    hottest = jax.random.randint(keys[0], (), 0, devices)
    picked = jax.vmap(lambda sub_key: jax.random.permutation(sub_key, (devices - 1) * CAP)[:WELL_DEV - CAP])(jax.random.split(keys[1], devices))
    others = picked // CAP
    others = others + (others >= hottest).astype(others.dtype)
    owners = jnp.concatenate([jnp.full((devices, CAP), hottest, others.dtype), others], axis=1)
    shuffle = jax.vmap(lambda sub_key: jax.random.permutation(sub_key, WELL_DEV))(jax.random.split(keys[2], devices))
    owners = jnp.take_along_axis(owners, shuffle, axis=1)
    local_x = jax.random.randint(keys[3], (devices, WELL_DEV), 0, CX)
    local_z = jax.random.randint(keys[4], (devices, WELL_DEV), 0, NZ)
    local_y = jax.random.randint(keys[5], (devices, WELL_DEV), 0, CY)
    glob_x = owners // N_GY * CX + local_x
    glob_y = owners % N_GY * CY + local_y
    cells = (glob_x * NZ + local_z) * (CY * N_GY) + glob_y
    return cells.reshape(-1).astype(jnp.int32)


def with_ends(values, key, smallest, top_value):
    longest = values.shape.index(max(values.shape))
    spots = []
    for shift in (0, 1):
        where = [jax.random.randint(jax.random.fold_in(key, axis), (), 0, length) for axis, length in enumerate(values.shape)]
        where[longest] = (where[longest] + shift) % values.shape[longest]
        spots.append(tuple(where))
    return values.at[spots[0]].set(smallest).at[spots[1]].set(top_value)


def block_scale(key, shape, shards, least, top_value):
    def one(axis_at, parts):
        draws = jax.random.uniform(jax.random.fold_in(jax.random.fold_in(key, 6), axis_at), (parts,), jnp.float32, least / len(shards), top_value / len(shards))
        return jnp.repeat(jnp.exp(draws), shape[axis_at] // parts).reshape((-1,) + (1,) * (len(shape) - axis_at - 1))

    level = one(*shards[0])
    for cut in shards[1:]:
        level = level * one(*cut)
    return level


def bell_draw(rng, extent, width, limit, cuts=(), held_as=jnp.bfloat16):
    entries = jax.random.normal(rng, extent, jnp.float32) * width
    if len(cuts) > 0:
        entries = block_scale(rng, extent, cuts, -0.22, 0.18) * entries
    return jnp.clip(entries, min=-limit, max=limit).astype(held_as)


def setup_inputs(seed: int = 0) -> dict:
    splits = jax.random.split(jax.random.key(seed), 9)
    return {
        "well_cell": draw_well_cell(jax.random.fold_in(splits[8], 71), 0),
        "well_test": with_ends(jax.random.randint(splits[1], (WELLS,), 0, TESTS), jax.random.fold_in(splits[1], 1), 0, TESTS - 1).astype(jnp.int32),
        "well_value": bell_draw(splits[2], (WELLS,), 1.0, 6.0, ((0, 128),), jnp.float32),
        "cond_class": with_ends(jax.random.randint(splits[3], (NX, NZ, NY), 0, NCLASS), jax.random.fold_in(splits[3], 1), 0, NCLASS - 1).astype(jnp.int32),
        "class_value": jnp.clip(jnp.exp(jax.random.uniform(splits[4], (NCLASS,), jnp.float32, math.log(0.1), math.log(3.0))), 0.1, 3.0),
        "zone_id": with_ends(jax.random.randint(splits[5], (NX, NZ, NY), 0, ZONES), jax.random.fold_in(splits[5], 1), 0, ZONES - 1).astype(jnp.int32),
        "drawdown": bell_draw(splits[6], (TESTS, NX, NZ, NY), 1.0, 6.0, ((1, 8), (3, 16))),
        "centroid": jnp.clip(jax.random.uniform(splits[7], (3, ZONES), jnp.float32, 0.0, 1.0), 0.0, 1.0),
    }


storage = 0.02
lam_low = 0.02
lam_high = 36.02
corr_len = 0.1

def cheb_setup():
    middle = 0.5 * (lam_high + lam_low)
    spread = 0.5 * (lam_high - lam_low)
    ratio_mid = middle / spread
    current = 1.0 / ratio_mid
    factors = []
    for counter in range(SWEEPS - 1):
        updated = 1.0 / (2.0 * ratio_mid - current)
        factors.append((updated * current, 2.0 * updated / spread))
        current = updated
    return (middle, factors)

def apply_operator(padded, cond_pad):
    centre = padded[..., 1:-1, 1:-1, 1:-1]
    cond_mid = cond_pad[..., 1:-1, 1:-1, 1:-1]
    result = storage * centre
    pairs = [(padded[..., 2:, 1:-1, 1:-1], cond_pad[..., 2:, 1:-1, 1:-1]), (padded[..., :-2, 1:-1, 1:-1], cond_pad[..., :-2, 1:-1, 1:-1]), (padded[..., 1:-1, 2:, 1:-1], cond_pad[..., 1:-1, 2:, 1:-1]), (padded[..., 1:-1, :-2, 1:-1], cond_pad[..., 1:-1, :-2, 1:-1]), (padded[..., 1:-1, 1:-1, 2:], cond_pad[..., 1:-1, 1:-1, 2:]), (padded[..., 1:-1, 1:-1, :-2], cond_pad[..., 1:-1, 1:-1, :-2])]
    for beside, cond_side in pairs:
        result = result + 0.5 * (cond_mid + cond_side) * (centre - beside)
    return result

def chebyshev(source, conduct):
    middle, factors = cheb_setup()
    cond_pad = jnp.pad(conduct, 1)
    residual = source
    direction = residual / middle
    solution = jnp.zeros_like(source)
    for counter in range(SWEEPS):
        applied = apply_operator(jnp.pad(direction, 1), cond_pad)
        solution = solution + direction
        residual = residual - applied
        if counter < SWEEPS - 1:
            keep_part, new_part = factors[counter]
            direction = keep_part * direction + new_part * residual
    return solution

def covariance(col_pts, row_pts):
    squared = (col_pts[0][:, None] - row_pts[0][None, :]) ** 2
    squared = squared + (col_pts[1][:, None] - row_pts[1][None, :]) ** 2
    squared = squared + (col_pts[2][:, None] - row_pts[2][None, :]) ** 2
    return jnp.exp(-jnp.sqrt(squared) / corr_len).astype(jnp.bfloat16)

def reference(well_cell, well_test, well_value, cond_class, class_value, zone_id, drawdown, centroid):
    conduct = class_value[cond_class]
    total_cells = NX * NZ * NY
    zone_flat = zone_id.reshape(-1)

    def one_test(test_no):
        weights = jnp.where(well_test == test_no, well_value, 0.0)
        source = jnp.zeros((total_cells,), jnp.float32).at[well_cell].add(weights).reshape(NX, NZ, NY)
        adjoint = chebyshev(source, conduct)
        sensitive = conduct * drawdown[test_no].astype(jnp.float32) * adjoint
        return jax.ops.segment_sum(sensitive.reshape(-1), zone_flat, num_segments=ZONES)
    partial_value = lax.map(one_test, jnp.arange(TESTS, dtype=jnp.int32))
    zone_sums = partial_value.astype(jnp.bfloat16)
    block_len = min(1024, ZONES)

    def tile_product(start):
        rows_pts = lax.dynamic_slice_in_dim(centroid, start, block_len, 1)
        return jnp.dot(zone_sums, covariance(centroid, rows_pts), preferred_element_type=jnp.float32)
    pieces = lax.map(tile_product, jnp.arange(ZONES // block_len, dtype=jnp.int32) * block_len)
    return jnp.moveaxis(pieces, 0, 1).reshape(TESTS, ZONES).astype(jnp.bfloat16)
```

```python
import functools

import jax
import jax.numpy as jnp
from jax import lax
from jax.experimental import pallas as pl
from jax.experimental.pallas import tpu as pltpu
from jax.sharding import PartitionSpec as P

MESH = pl.DeviceIdType.MESH
NT = (((1,), (1,)), ((), ()))
VMEM = pl.BlockSpec(memory_space=pltpu.VMEM)
F32 = jnp.float32
BF16 = jnp.bfloat16
MIB = 2**20

SWEEPS = 12
TESTS = 4
CX, NZ, CY = 4, 64, 128
N_GX, N_GY = 8, 16
DEVICES = N_GX * N_GY
NCLASS = 16
CAP = 16
ZONES = 98304
SHARE = ZONES // DEVICES
GROUPS = 16
MEMBERS = DEVICES // GROUPS
GROUP = ZONES // GROUPS
PLANES = TESTS * CX

storage = 0.02
lam_low = 0.02
lam_high = 36.02
corr_len = 0.1
LOG2E = 1.4426950408889634


def cheb_setup():
    middle = 0.5 * (lam_high + lam_low)
    spread = 0.5 * (lam_high - lam_low)
    ratio_mid = middle / spread
    current = 1.0 / ratio_mid
    factors = []
    for counter in range(SWEEPS - 1):
        updated = 1.0 / (2.0 * ratio_mid - current)
        factors.append((updated * current, 2.0 * updated / spread))
        current = updated
    return (middle, factors)


def my_index():
    return lax.axis_index("gx") * N_GY + lax.axis_index("gy")


def coords(dev):
    return (dev // N_GY, dev % N_GY)


def greet(devs):
    barrier = pltpu.get_barrier_semaphore()
    for dev in devs:
        pl.semaphore_signal(barrier, inc=1, device_id=dev, device_id_type=MESH)
    pl.semaphore_wait(barrier, len(devs))


def greet_all(me):
    barrier = pltpu.get_barrier_semaphore()

    def each(k, _):
        dev = lax.rem(me + k, DEVICES)
        pl.semaphore_signal(barrier, inc=1, device_id=coords(dev), device_id_type=MESH)
        return 0

    lax.fori_loop(1, DEVICES, each, 0)
    pl.semaphore_wait(barrier, DEVICES - 1)


def send_to_all(me, send, recv, send_sem, recv_sem):
    def each(k, _):
        dev = lax.rem(me + k, DEVICES)
        pltpu.make_async_remote_copy(
            src_ref=send.at[dev],
            dst_ref=recv.at[me],
            send_sem=send_sem,
            recv_sem=recv_sem,
            device_id=coords(dev),
            device_id_type=MESH,
        ).start()
        return 0

    lax.fori_loop(1, DEVICES, each, 0)
    recv[me] = send[me]
    rest = pl.ds(0, DEVICES - 1)
    pltpu.make_async_copy(recv.at[rest], recv.at[rest], recv_sem).wait()
    pltpu.make_async_copy(send.at[rest], send.at[rest], send_sem).wait()


def wells_kernel(cell_ref, test_ref, value_ref, src_ref, rows, send, recv, send_sem, recv_sem):
    me = my_index()
    cell, test, value = cell_ref[...], test_ref[...], value_ref[...]
    n_rows = cell.shape[1]
    y = cell % (CY * N_GY)
    z = cell // (CY * N_GY) % NZ
    x = cell // (CY * N_GY * NZ)
    owner = x // CX * N_GY + y // CY
    z_row = z % 8 * 8 + z // 8
    high = (test * CX + x % CX) * 32 + z_row % 32
    code = (high * 256 + z_row // 32 * CY + y % CY).astype(F32)
    hot = jnp.where(
        lax.broadcasted_iota(jnp.int32, (DEVICES, n_rows), 0) == owner, 1.0, 0.0
    )
    earlier = jnp.where(
        lax.broadcasted_iota(jnp.int32, (n_rows, n_rows), 0)
        < lax.broadcasted_iota(jnp.int32, (n_rows, n_rows), 1),
        1.0,
        0.0,
    )
    hot16 = hot.astype(BF16)
    count = jnp.dot(hot16, earlier.astype(BF16), preferred_element_type=F32)
    rank = jnp.sum(hot * count, axis=0, keepdims=True).astype(jnp.int32)
    slot = lax.broadcasted_iota(jnp.int32, (128, n_rows), 0)
    part = jnp.where(slot == rank, code, jnp.where(slot == rank + CAP, value, 0.0))
    part = jnp.where(rank < CAP, part, 0.0)
    total = None
    for _ in range(3):
        piece = part.astype(BF16)
        part = part - piece.astype(F32)
        term = lax.dot_general(hot16, piece, NT, preferred_element_type=F32)
        total = term if total is None else total + term
    rows[...] = total
    for dev in range(DEVICES):
        send[dev] = rows[dev : dev + 1, :]

    greet_all(me)
    send_to_all(me, send, recv, send_sem, recv_sem)

    for dev in range(DEVICES):
        rows[dev : dev + 1, :] = recv[dev]
    lane = lax.broadcasted_iota(jnp.int32, (16, 128), 1)
    codes = jnp.zeros((16, 128), F32)
    values = jnp.zeros((16, 128), F32)
    for g in range(8):
        block = rows[16 * g : 16 * g + 16, :]
        here = lane // CAP == g
        codes = jnp.where(here, pltpu.roll(block, CAP * g, 1) if g else block, codes)
        values = jnp.where(here, pltpu.roll(block, (CAP * g - CAP) % 128, 1), values)
    codes = codes.astype(jnp.int32)
    highs, lows = codes // 256, codes % 256
    first = values.astype(BF16).astype(F32)
    second = values - first
    row_high = lax.broadcasted_iota(jnp.int32, (512, 128), 0)
    row_low = lax.broadcasted_iota(jnp.int32, (256, 128), 0)
    left, right_a, right_b = [], [], []
    for r in range(16):
        left.append(jnp.where(row_high == highs[r : r + 1], 1.0, 0.0).astype(BF16))
        same = row_low == lows[r : r + 1]
        right_a.append(jnp.where(same, first[r : r + 1], 0.0).astype(BF16))
        right_b.append(jnp.where(same, second[r : r + 1], 0.0).astype(BF16))
    left = jnp.concatenate(left, axis=1)
    acc = lax.dot_general(
        left, jnp.concatenate(right_a, axis=1), NT, preferred_element_type=F32
    ) + lax.dot_general(left, jnp.concatenate(right_b, axis=1), NT, preferred_element_type=F32)
    for p in range(PLANES):
        for half in range(2):
            src_ref[p, 32 * half : 32 * half + 32, :] = acc[
                32 * p : 32 * p + 32, 128 * half : 128 * half + 128
            ]


def wells_call(cell, test, value):
    return pl.pallas_call(
        wells_kernel,
        out_shape=jax.ShapeDtypeStruct((PLANES, NZ, CY), F32),
        in_specs=[VMEM] * 3,
        out_specs=VMEM,
        scratch_shapes=[
            pltpu.VMEM((DEVICES, 128), F32),
            pltpu.VMEM((DEVICES, 1, 128), F32),
            pltpu.VMEM((DEVICES, 1, 128), F32),
            pltpu.SemaphoreType.DMA,
            pltpu.SemaphoreType.DMA,
        ],
        compiler_params=pltpu.CompilerParams(
            collective_id=0, has_side_effects=True, vmem_limit_bytes=48 * MIB
        ),
    )(cell, test, value)


def roll_to(value, shift):
    shift = shift % 128
    return pltpu.roll(value, shift, 1) if shift else value


def sweeps_kernel(
    class_ref,
    class_value_ref,
    src_ref,
    draw_ref,
    out_ref,
    cond_nat,
    cond,
    coef,
    dirs,
    resid,
    sol,
    cx_recv,
    cy_send,
    cy_recv,
    dx_send,
    dx_recv,
    dy_send,
    dy_recv,
    cond_send_sem,
    cond_recv_sem,
    send_sem,
    recv_sem,
):
    gx, gy = lax.axis_index("gx"), lax.axis_index("gy")
    x_down, x_up = (lax.rem(gx + N_GX - 1, N_GX), gy), (lax.rem(gx + 1, N_GX), gy)
    y_down, y_up = (gx, lax.rem(gy + N_GY - 1, N_GY)), (gx, lax.rem(gy + 1, N_GY))
    lane = lax.broadcasted_iota(jnp.int32, (8, 128), 1)
    sub = lax.broadcasted_iota(jnp.int32, (8, 128), 0)
    first_lane, last_lane = lane == 0, lane == 127

    def tile(j):
        return slice(8 * j, 8 * j + 8)

    for x in range(CX):
        cls = class_ref[x]
        acc = jnp.zeros((NZ, CY), F32)
        for k in range(NCLASS):
            acc = jnp.where(cls == k, class_value_ref[k], acc)
        cond_nat[x] = acc
    for x in range(CX):
        for j in range(8):
            cond[x, tile(j), :] = cond_nat[x, pl.ds(j, 8, stride=8), :]

    def packed(get):
        parts = [jnp.zeros((8, 128), F32)] * 2
        for x in range(CX):
            for j in range(8):
                q = 2 * x + 32 * (j % 4)
                here = (lane == q) | (lane == q + 1)
                parts[j // 4] = jnp.where(here, roll_to(get(x, j), q + 1), parts[j // 4])
        return parts

    def met(low, high):
        return jnp.where(lane % 2 == 1, high, roll_to(low, 2))

    greet([x_down, x_up, y_down, y_up])

    def exchange(x_src, x_dst, y_src, y_dst, s_sem, r_sem):
        out = []
        for n, (src, dst, dev) in enumerate(
            (
                (x_src(0), x_dst(1), x_down),
                (x_src(1), x_dst(0), x_up),
                (y_src, y_dst(1), y_down),
                (y_src, y_dst(0), y_up),
            )
        ):
            out.append(
                pltpu.make_async_remote_copy(
                    src_ref=src,
                    dst_ref=dst,
                    send_sem=s_sem(n),
                    recv_sem=r_sem(n),
                    device_id=dev,
                    device_id_type=MESH,
                )
            )
        return out

    pack = packed(lambda x, j: cond[x, tile(j), :])
    for half in range(2):
        cy_send[half] = pack[half]
    cond_copies = exchange(
        lambda side: cond.at[side * (CX - 1)],
        lambda side: cx_recv.at[side],
        cy_send,
        lambda side: cy_recv.at[side],
        lambda n: cond_send_sem.at[n],
        lambda n: cond_recv_sem.at[n],
    )
    for copy in cond_copies:
        copy.start()

    def copies(par):
        return exchange(
            lambda side: dx_send.at[par, side],
            lambda side: dx_recv.at[par, side],
            dy_send.at[par],
            lambda side: dy_recv.at[par, side],
            lambda n: send_sem.at[par, n],
            lambda n: recv_sem.at[par, n],
        )

    middle, factors = cheb_setup()

    def stage(par, t, get):
        for side, x in ((0, 0), (1, CX - 1)):
            for j in range(0, 8, 2):
                both = jnp.concatenate([get(x, j), get(x, j + 1)], axis=0)
                dx_send[par, side, t, 8 * j : 8 * j + 16, :] = both.astype(BF16)
        parts = packed(get)
        for half in range(2):
            old = dy_send[par, half]
            dy_send[par, half] = jnp.where(
                lane % 32 // 8 == t, pltpu.roll(parts[half], 8 * t, 1), old
            )

    for par in range(2):
        for half in range(2):
            dy_send[par, half] = jnp.zeros((8, 128), F32)

    def begin(t, _):
        for x in range(CX):
            p = CX * t + x
            value = src_ref[p]
            resid[p] = value
            dirs[0, p] = value / middle
            sol[p] = jnp.zeros((NZ, CY), F32)
        stage(0, t, lambda x, j: dirs[0, CX * t + x, tile(j), :])
        return 0

    lax.fori_loop(0, TESTS, begin, 0)
    for copy in copies(0):
        copy.start()
    for copy in cond_copies:
        copy.wait()

    beside = [met(cy_recv[0, half], cy_recv[1, half]) for half in range(2)]
    for x in range(CX):
        for j in range(8):
            c = cond[x, tile(j), :]
            q = 2 * x + 32 * (j % 4)
            halo = roll_to(beside[j // 4], -(q + 2))
            zero = jnp.zeros((8, 128), F32)
            off_y_up = last_lane & (gy == N_GY - 1)
            off_y_down = first_lane & (gy == 0)
            sides = []
            if x < CX - 1:
                sides.append((cond[x + 1, tile(j), :], None))
            else:
                sides.append((cx_recv[1, tile(j), :], (lane >= 0) & (gx == N_GX - 1)))
            if x > 0:
                sides.append((cond[x - 1, tile(j), :], None))
            else:
                sides.append((cx_recv[0, tile(j), :], (lane >= 0) & (gx == 0)))
            if j < 7:
                sides.append((cond[x, tile(j + 1), :], None))
            else:
                sides.append((pltpu.roll(cond[x, tile(0), :], 7, 0), sub == 7))
            if j > 0:
                sides.append((cond[x, tile(j - 1), :], None))
            else:
                sides.append((pltpu.roll(cond[x, tile(7), :], 1, 0), sub == 0))
            sides.append((jnp.where(last_lane, halo, roll_to(c, 127)), off_y_up))
            sides.append((jnp.where(first_lane, halo, roll_to(c, 1)), off_y_down))
            diag = storage
            for n, (near, off) in enumerate(sides):
                if off is not None:
                    near = jnp.where(off, zero, near)
                face = 0.5 * (c + near)
                diag = diag + face
                coef[n, x, tile(j), :] = face if off is None else jnp.where(off, zero, face)
            coef[6, x, tile(j), :] = diag

    keeps = [pair[0] for pair in factors]
    news = [pair[1] for pair in factors]

    def sweep(k, _):
        par = lax.rem(k, 2)
        nxt = 1 - par
        keep, new = jnp.float32(keeps[0]), jnp.float32(news[0])
        for n in range(1, SWEEPS - 1):
            keep = jnp.where(k == n, jnp.float32(keeps[n]), keep)
            new = jnp.where(k == n, jnp.float32(news[n]), new)
        for copy in copies(par):
            copy.wait()
        near_y = [met(dy_recv[par, 0, half], dy_recv[par, 1, half]) for half in range(2)]

        def one_test(t, _):
            halos = [pltpu.roll(near_y[half], lax.rem(128 - 8 * t, 128), 1) for half in range(2)]
            made = {}
            low = [dx_recv[par, 0, t, 8 * j : 8 * j + 16, :].astype(F32) for j in range(0, 8, 2)]
            high = [dx_recv[par, 1, t, 8 * j : 8 * j + 16, :].astype(F32) for j in range(0, 8, 2)]
            for x in range(CX):
                p = CX * t + x
                v = [dirs[par, p, tile(j), :] for j in range(8)]
                for j in range(8):
                    q = 2 * x + 32 * (j % 4)
                    halo = roll_to(halos[j // 4], -(q + 2))
                    half = slice(8 * (j % 2), 8 * (j % 2) + 8)
                    near = [
                        dirs[par, p + 1, tile(j), :] if x < CX - 1 else high[j // 2][half],
                        dirs[par, p - 1, tile(j), :] if x > 0 else low[j // 2][half],
                        v[j + 1] if j < 7 else pltpu.roll(v[0], 7, 0),
                        v[j - 1] if j > 0 else pltpu.roll(v[7], 1, 0),
                        jnp.where(last_lane, halo, roll_to(v[j], 127)),
                        jnp.where(first_lane, halo, roll_to(v[j], 1)),
                    ]
                    applied = coef[6, x, tile(j), :] * v[j]
                    for n in range(6):
                        applied = applied - coef[n, x, tile(j), :] * near[n]
                    left = resid[p, tile(j), :] - applied
                    resid[p, tile(j), :] = left
                    sol[p, tile(j), :] += v[j]
                    fresh = keep * v[j] + new * left
                    dirs[nxt, p, tile(j), :] = fresh
                    made[x, j] = fresh
            stage(nxt, t, lambda x, j: made[x, j])
            return 0

        lax.fori_loop(0, TESTS, one_test, 0)

        @pl.when(k < SWEEPS - 2)
        def _():
            for copy in copies(nxt):
                copy.start()

        return 0

    lax.fori_loop(0, SWEEPS - 1, sweep, 0)
    last = (SWEEPS - 1) % 2

    def finish(p, _):
        for j in range(8):
            resid[p, pl.ds(j, 8, stride=8), :] = sol[p, tile(j), :] + dirs[last, p, tile(j), :]
        x = lax.rem(p, CX)
        out_ref[p] = cond_nat[x] * draw_ref[p].astype(F32) * resid[p]
        return 0

    lax.fori_loop(0, PLANES, finish, 0)


def sweeps_call(classes, class_value, source, drawdown):
    block = (PLANES, NZ, CY)
    return pl.pallas_call(
        sweeps_kernel,
        out_shape=jax.ShapeDtypeStruct(block, F32),
        in_specs=[VMEM, pl.BlockSpec(memory_space=pltpu.SMEM), VMEM, VMEM],
        out_specs=VMEM,
        scratch_shapes=[
            pltpu.VMEM((CX, NZ, CY), F32),
            pltpu.VMEM((CX, NZ, CY), F32),
            pltpu.VMEM((7, CX, NZ, CY), F32),
            pltpu.VMEM((2,) + block, F32),
            pltpu.VMEM(block, F32),
            pltpu.VMEM(block, F32),
            pltpu.VMEM((2, NZ, CY), F32),
            pltpu.VMEM((2, 8, 128), F32),
            pltpu.VMEM((2, 2, 8, 128), F32),
            pltpu.VMEM((2, 2, TESTS, NZ, CY), BF16),
            pltpu.VMEM((2, 2, TESTS, NZ, CY), BF16),
            pltpu.VMEM((2, 2, 8, 128), F32),
            pltpu.VMEM((2, 2, 2, 8, 128), F32),
            pltpu.SemaphoreType.DMA((4,)),
            pltpu.SemaphoreType.DMA((4,)),
            pltpu.SemaphoreType.DMA((2, 4)),
            pltpu.SemaphoreType.DMA((2, 4)),
        ],
        compiler_params=pltpu.CompilerParams(
            collective_id=1, has_side_effects=True, vmem_limit_bytes=48 * MIB
        ),
    )(classes, class_value, source, drawdown)


def groups_of(gx, gy):
    tail = gx == N_GX - 1
    low = jnp.where(tail, gy % 8, gy)
    high = jnp.where(tail, gy % 8 + 8, (gy + gx + 1) % GROUPS)
    return low, high, tail & (gy >= 8)


def takers_of(group):
    out = []
    for k in range(N_GX - 1):
        out.append(((k, group), 0))
        out.append(((k, (group + GROUPS - k - 1) % GROUPS), 1))
    place = group // 8
    out.append(((N_GX - 1, group % 8), place))
    out.append(((N_GX - 1, group % 8 + 8), place))
    return out


ROWS_STEP = 8


def zones_kernel(
    zone_ref, sens_ref, out_ref, owner_of, left, right, acc, send, recv, mine, sem, got_sem, put_sem
):
    me = my_index()
    gx, gy = lax.axis_index("gx"), lax.axis_index("gy")
    owner_of[...] = (
        (lax.broadcasted_iota(jnp.int32, (TESTS * DEVICES, 128), 0) // TESTS)
        .astype(F32)
        .astype(BF16)
    )
    acc[...] = jnp.zeros_like(acc)
    inner = lax.broadcasted_iota(jnp.int32, (256, 128), 0).astype(F32).astype(BF16)
    sub = lax.broadcasted_iota(jnp.int32, (8, 128), 0) % TESTS

    def spread(row, times):
        return jnp.concatenate([jnp.broadcast_to(row, (16, 128)).astype(BF16)] * times, axis=0)

    def step(i, _):
        at = pl.ds(pl.multiple_of(i * ROWS_STEP, ROWS_STEP), ROWS_STEP)
        zone = zone_ref[at, :].astype(F32)
        owner = ((zone + 0.5) * (1.0 / SHARE)).astype(jnp.int32).astype(F32)
        place = zone - owner * SHARE
        values = [sens_ref[t, at, :] for t in range(TESTS)]
        for r in range(ROWS_STEP):
            row = slice(r, r + 1)
            four = jnp.broadcast_to(values[0][row], (8, 128))
            for t in range(1, TESTS):
                four = jnp.where(sub == t, jnp.broadcast_to(values[t][row], (8, 128)), four)
            four = jnp.concatenate([four, four], axis=0).astype(BF16)
            cols = slice(128 * r, 128 * r + 128)
            left[:, cols] = jnp.where(
                owner_of[...] == spread(owner[row], TESTS * DEVICES // 16),
                jnp.concatenate([four] * (TESTS * DEVICES // 16), axis=0),
                jnp.zeros((), BF16),
            )
            for part in range(SHARE // 256):
                right[256 * part : 256 * part + 256, cols] = jnp.where(
                    inner == spread(place[row] - 256.0 * part, 16),
                    jnp.ones((), BF16),
                    jnp.zeros((), BF16),
                )
        acc[...] += lax.dot_general(left[...], right[...], NT, preferred_element_type=F32)
        return 0

    lax.fori_loop(0, CX * NZ // ROWS_STEP, step, 0)
    for dev in range(DEVICES):
        send[dev] = acc[TESTS * dev : TESTS * dev + TESTS, :]

    greet_all(me)
    send_to_all(me, send, recv, sem.at[0], sem.at[1])

    def add(s, total):
        for n in range(8):
            total = total + recv[8 * s + n]
        return total

    total = lax.fori_loop(0, DEVICES // 8, add, jnp.zeros((TESTS, SHARE), F32))
    mine[...] = total.astype(BF16).astype(F32)

    group, member = me // MEMBERS, me % MEMBERS

    def put(n, dev, place):
        return pltpu.make_async_remote_copy(
            src_ref=mine,
            dst_ref=out_ref.at[place, member],
            send_sem=put_sem.at[n],
            recv_sem=got_sem.at[place, member],
            device_id=dev,
            device_id_type=MESH,
        )

    takers = takers_of(group)
    for n, (dev, place) in enumerate(takers):
        self_here = dev[0] * N_GY + dev[1] == me

        @pl.when(jnp.logical_not(self_here))
        def _():
            put(n, dev, place).start()

        @pl.when(self_here)
        def _():
            out_ref[place, member] = mine[...]

    low, high, _ = groups_of(gx, gy)
    for place, held in ((0, low), (1, high)):
        for m in range(MEMBERS):

            @pl.when(held * MEMBERS + m != me)
            def _():
                pltpu.make_async_copy(
                    out_ref.at[place, m], out_ref.at[place, m], got_sem.at[place, m]
                ).wait()

    for n, (dev, place) in enumerate(takers):

        @pl.when(dev[0] * N_GY + dev[1] != me)
        def _():
            put(n, dev, place).wait_send()


def zones_call(zone, sens):
    rows = TESTS * DEVICES
    width = ROWS_STEP * 128
    return pl.pallas_call(
        zones_kernel,
        out_shape=jax.ShapeDtypeStruct((2, MEMBERS, TESTS, SHARE), F32),
        in_specs=[VMEM] * 2,
        out_specs=VMEM,
        scratch_shapes=[
            pltpu.VMEM((rows, 128), BF16),
            pltpu.VMEM((rows, width), BF16),
            pltpu.VMEM((SHARE, width), BF16),
            pltpu.VMEM((rows, SHARE), F32),
            pltpu.VMEM((DEVICES, TESTS, SHARE), F32),
            pltpu.VMEM((DEVICES, TESTS, SHARE), F32),
            pltpu.VMEM((TESTS, SHARE), F32),
            pltpu.SemaphoreType.DMA((2,)),
            pltpu.SemaphoreType.DMA((2, MEMBERS)),
            pltpu.SemaphoreType.DMA((16,)),
        ],
        compiler_params=pltpu.CompilerParams(
            collective_id=2, has_side_effects=True, vmem_limit_bytes=48 * MIB
        ),
    )(zone, sens)


BLOCK = 1024
STRIP = 64


def cov_kernel(diag_ref, pts_ref, sums_ref, out_ref, z_ref, rows_ref, tile_ref):
    blocks = GROUP // BLOCK
    diag = diag_ref[0]
    out_ref[...] = jnp.zeros_like(out_ref)
    for g in range(2):
        for m in range(MEMBERS):
            both = jnp.concatenate([sums_ref[g, m], jnp.zeros((TESTS, SHARE), F32)], axis=0)
            z_ref[g, :, SHARE * m : SHARE * m + SHARE] = both.astype(BF16)

    def tile(cg, c):
        cols = [pts_ref[cg, k : k + 1, pl.ds(pl.multiple_of(c * BLOCK, BLOCK), BLOCK)] for k in range(3)]

        def body(i, _):
            r0 = pl.multiple_of(i * STRIP, STRIP)
            squared = None
            for k in range(3):
                near = jnp.concatenate([rows_ref[k, pl.ds(r0, STRIP), :]] * (BLOCK // 128), axis=1)
                gap = near - cols[k]
                squared = gap * gap if squared is None else squared + gap * gap
            squared = jnp.maximum(squared, 1e-30)
            dist = squared * lax.rsqrt(squared)
            tile_ref[pl.ds(r0, STRIP), :] = jnp.exp2(-dist).astype(BF16)
            return 0

        lax.fori_loop(0, BLOCK // STRIP, body, 0, unroll=True)

    def phase(rg, _):
        cg = jnp.where(diag == 1, rg, 1)

        def row_block(r, _):
            rs = pl.ds(pl.multiple_of(r * BLOCK, BLOCK), BLOCK)
            for k in range(3):
                rows_ref[k] = jnp.broadcast_to(pts_ref[rg, k : k + 1, rs], (128, BLOCK)).T
            near = z_ref[rg, :, rs]

            def col_block(c, acc):
                tile(cg, c)
                cs = pl.ds(pl.multiple_of(c * BLOCK, BLOCK), BLOCK)
                acc = acc + lax.dot_general(
                    z_ref[cg, :, cs], tile_ref[...], NT, preferred_element_type=F32
                )

                @pl.when(jnp.logical_not((diag == 1) & (c == r)))
                def _():
                    out_ref[cg, :, cs] += jnp.dot(near, tile_ref[...], preferred_element_type=F32)

                return acc

            first = jnp.where(diag == 1, r, 0)
            acc = lax.fori_loop(first, blocks, col_block, jnp.zeros((8, BLOCK), F32))
            out_ref[rg, :, rs] += acc
            return 0

        lax.fori_loop(0, blocks, row_block, 0)
        return 0

    lax.fori_loop(0, 1 + diag, phase, 0)


def cov_call(diag, pts, sums):
    return pl.pallas_call(
        cov_kernel,
        out_shape=jax.ShapeDtypeStruct((2, 8, GROUP), F32),
        in_specs=[pl.BlockSpec(memory_space=pltpu.SMEM), VMEM, VMEM],
        out_specs=VMEM,
        scratch_shapes=[
            pltpu.VMEM((2, 8, GROUP), BF16),
            pltpu.VMEM((3, BLOCK, 128), F32),
            pltpu.VMEM((BLOCK, BLOCK), BF16),
        ],
        compiler_params=pltpu.CompilerParams(vmem_limit_bytes=48 * MIB),
    )(diag, pts, sums)


def reduce_kernel(part_ref, out_ref, send, recv, send_sem, recv_sem):
    me = my_index()
    gx, gy = lax.axis_index("gx"), lax.axis_index("gy")
    low, high, diag = groups_of(gx, gy)
    group, member = me // MEMBERS, me % MEMBERS
    for g in range(2):
        for m in range(MEMBERS):
            send[g, m] = part_ref[g, 0:TESTS, SHARE * m : SHARE * m + SHARE]

    takers = takers_of(group)
    barrier = pltpu.get_barrier_semaphore()
    for place, held in ((0, low), (1, high)):
        for m in range(MEMBERS):
            owner = held * MEMBERS + m

            @pl.when(owner != me)
            def _():
                pl.semaphore_signal(barrier, inc=1, device_id=coords(owner), device_id_type=MESH)

    for dev, _ in takers:

        @pl.when(dev[0] * N_GY + dev[1] != me)
        def _():
            pl.semaphore_signal(barrier, inc=1, device_id=dev, device_id_type=MESH)

    self_here = (low == group) | (high == group)
    pl.semaphore_wait(barrier, 32 - 2 * self_here.astype(jnp.int32))

    def put(place, m, held, slot):
        return pltpu.make_async_remote_copy(
            src_ref=send.at[place, m],
            dst_ref=recv.at[slot],
            send_sem=send_sem.at[place, m],
            recv_sem=recv_sem.at[slot],
            device_id=coords(held * MEMBERS + m),
            device_id_type=MESH,
        )

    sides = (
        (0, low, jnp.where(diag, low, high)),
        (1, high, jnp.where(diag, high, low)),
    )
    for place, held, slot in sides:
        for m in range(MEMBERS):

            @pl.when(held * MEMBERS + m != me)
            def _():
                put(place, m, held, slot).start()

            @pl.when(held * MEMBERS + m == me)
            def _():
                recv[slot] = send[place, m]

    own_slot = jnp.where(
        low == group, jnp.where(diag, low, high), jnp.where(diag, high, low)
    )
    for slot in range(GROUPS):

        @pl.when(jnp.logical_not(self_here & (own_slot == slot)))
        def _():
            pltpu.make_async_copy(recv.at[slot], recv.at[slot], recv_sem.at[slot]).wait()

    total = recv[0]
    for slot in range(1, GROUPS):
        total = total + recv[slot]
    out_ref[...] = total.astype(BF16)
    for place, held, slot in sides:
        for m in range(MEMBERS):

            @pl.when(held * MEMBERS + m != me)
            def _():
                put(place, m, held, slot).wait_send()


def reduce_call(parts):
    return pl.pallas_call(
        reduce_kernel,
        out_shape=jax.ShapeDtypeStruct((TESTS, SHARE), BF16),
        in_specs=[VMEM],
        out_specs=VMEM,
        scratch_shapes=[
            pltpu.VMEM((2, MEMBERS, TESTS, SHARE), F32),
            pltpu.VMEM((GROUPS, TESTS, SHARE), F32),
            pltpu.SemaphoreType.DMA((2, MEMBERS)),
            pltpu.SemaphoreType.DMA((GROUPS,)),
        ],
        compiler_params=pltpu.CompilerParams(
            collective_id=3, has_side_effects=True, vmem_limit_bytes=32 * MIB
        ),
    )(parts)


def per_device(
    well_cell, well_test, well_value, cond_class, class_value, zone_id, drawdown, centroid
):
    gx, gy = lax.axis_index("gx"), lax.axis_index("gy")
    low, high, diag = groups_of(gx, gy)
    pts = jnp.stack(
        [lax.dynamic_slice_in_dim(centroid, held * GROUP, GROUP, 1) for held in (low, high)]
    ) * (LOG2E / corr_len)
    source = wells_call(well_cell[None], well_test[None], well_value[None])
    sens = sweeps_call(cond_class, class_value, source, drawdown.reshape(PLANES, NZ, CY))
    sums = zones_call(zone_id.reshape(CX * NZ, CY), sens.reshape(TESTS, CX * NZ, CY))
    parts = cov_call(diag.astype(jnp.int32)[None], pts, sums)
    return reduce_call(parts)


def solution(mesh):
    return jax.shard_map(
        per_device,
        mesh=mesh,
        in_specs=(
            P(("gx", "gy")),
            P(("gx", "gy")),
            P(("gx", "gy")),
            P("gx", None, "gy"),
            P(),
            P("gx", None, "gy"),
            P(None, "gx", None, "gy"),
            P(),
        ),
        out_specs=P(None, ("gx", "gy")),
        check_vma=False,
    )
```

```python
import functools

import jax
import jax.numpy as jnp
from jax import lax
from jax.experimental import pallas as pl
from jax.experimental.pallas import tpu as pltpu
from jax.sharding import PartitionSpec as P

MESH = pl.DeviceIdType.MESH
NT = (((1,), (1,)), ((), ()))
VMEM = pl.BlockSpec(memory_space=pltpu.VMEM)
F32 = jnp.float32
BF16 = jnp.bfloat16
MIB = 2**20

SWEEPS = 12
TESTS = 4
CX, NZ, CY = 4, 64, 128
N_GX, N_GY = 8, 16
DEVICES = N_GX * N_GY
NCLASS = 16
CAP = 16
ZONES = 98304
SHARE = ZONES // DEVICES
GROUPS = 16
MEMBERS = DEVICES // GROUPS
GROUP = ZONES // GROUPS
HALF = CY // 2
RIM = 16
XL, YL = 8, 3
HIGHS = 4 * YL * NZ
SLOTS = 16 * CAP

storage = 0.02
lam_low = 0.02
lam_high = 36.02
corr_len = 0.1
LOG2E = 1.4426950408889634


def cheb_setup():
    middle = 0.5 * (lam_high + lam_low)
    spread = 0.5 * (lam_high - lam_low)
    ratio_mid = middle / spread
    current = 1.0 / ratio_mid
    factors = []
    for counter in range(SWEEPS - 1):
        updated = 1.0 / (2.0 * ratio_mid - current)
        factors.append((updated * current, 2.0 * updated / spread))
        current = updated
    return (middle, factors)


def my_index():
    return lax.axis_index("gx") * N_GY + lax.axis_index("gy")


def coords(dev):
    return (dev // N_GY, dev % N_GY)


def greet(devs):
    barrier = pltpu.get_barrier_semaphore()
    for dev in devs:
        pl.semaphore_signal(barrier, inc=1, device_id=dev, device_id_type=MESH)
    pl.semaphore_wait(barrier, len(devs))


def greet_all(me):
    barrier = pltpu.get_barrier_semaphore()

    def each(k, _):
        dev = lax.rem(me + k, DEVICES)
        pl.semaphore_signal(barrier, inc=1, device_id=coords(dev), device_id_type=MESH)
        return 0

    lax.fori_loop(1, DEVICES, each, 0)
    pl.semaphore_wait(barrier, DEVICES - 1)


def send_to_all(me, send, recv, send_sem, recv_sem):
    def each(k, _):
        dev = lax.rem(me + k, DEVICES)
        pltpu.make_async_remote_copy(
            src_ref=send.at[dev],
            dst_ref=recv.at[me],
            send_sem=send_sem,
            recv_sem=recv_sem,
            device_id=coords(dev),
            device_id_type=MESH,
        ).start()
        return 0

    lax.fori_loop(1, DEVICES, each, 0)
    recv[me] = send[me]
    rest = pl.ds(0, DEVICES - 1)
    pltpu.make_async_copy(recv.at[rest], recv.at[rest], recv_sem).wait()
    pltpu.make_async_copy(send.at[rest], send.at[rest], send_sem).wait()


def share_kernel(
    cell_ref,
    test_ref,
    value_ref,
    class_ref,
    wells_ref,
    cls_ref,
    edge_ref,
    rows,
    send,
    mine,
    edges,
    wells_sem,
    cls_sem,
    edge_sem,
):
    me = my_index()
    gx, gy = lax.axis_index("gx"), lax.axis_index("gy")
    lane = lax.broadcasted_iota(jnp.int32, (32, 128), 1)
    classes = class_ref[...].reshape(CX * NZ, CY).astype(F32)
    mine[...] = classes.astype(BF16)
    for side, first in ((0, 0), (1, CY - RIM)):
        pack = jnp.zeros((32, 128), F32)
        for g in range(8):
            here = (lane >= RIM * g) & (lane < RIM * g + RIM)
            pack = jnp.where(here, roll_to(classes[32 * g : 32 * g + 32], RIM * g - first), pack)
        edges[side] = pack.astype(BF16)
    edge_ref[...] = jnp.zeros_like(edge_ref)

    cell, test, value = cell_ref[...], test_ref[...], value_ref[...]
    n_rows = 2 * cell.shape[1]
    y = cell % (CY * N_GY)
    z = cell // (CY * N_GY) % NZ
    x = cell // (CY * N_GY * NZ)
    block = y // HALF
    within = y % HALF
    step = jnp.where(within < RIM, -1, jnp.where(within >= HALF - RIM, 1, 0))
    other = block + step
    valid = (step != 0) & (other >= 0) & (other < 2 * N_GY)

    def twice(first, second):
        return jnp.concatenate([first, second], axis=1)

    block, y, z, x = twice(block, other), twice(y, y), twice(z, z), twice(x, x)
    test, value = twice(test, test), twice(value, value)
    owner = (block % 2 * 4 + test) * N_GY + block // 2
    owner = twice(owner[:, : n_rows // 2], jnp.where(valid, owner[:, n_rows // 2 :], -1))
    y_loc = y - (block * HALF - RIM)
    x_low = x % XL
    high = ((x_low % 4 * YL + y_loc % YL) * 8 + z % 8) * 8 + z // 8
    low = x_low // 4 * 128 + x // XL * 32 + y_loc // YL
    code = (high * 256 + low).astype(F32)
    hot = jnp.where(
        lax.broadcasted_iota(jnp.int32, (DEVICES, n_rows), 0) == owner, 1.0, 0.0
    )
    earlier = jnp.where(
        lax.broadcasted_iota(jnp.int32, (n_rows, n_rows), 0)
        < lax.broadcasted_iota(jnp.int32, (n_rows, n_rows), 1),
        1.0,
        0.0,
    )
    hot16 = hot.astype(BF16)
    count = jnp.dot(hot16, earlier.astype(BF16), preferred_element_type=F32)
    rank = jnp.sum(hot * count, axis=0, keepdims=True).astype(jnp.int32)
    slot = lax.broadcasted_iota(jnp.int32, (SLOTS, n_rows), 0)
    part = jnp.concatenate(
        [jnp.where(slot == rank, code, 0.0), jnp.where(slot == rank, value, 0.0)], axis=0
    )
    total = None
    for _ in range(3):
        piece = part.astype(BF16)
        part = part - piece.astype(F32)
        term = lax.dot_general(hot16, piece, NT, preferred_element_type=F32)
        total = term if total is None else total + term
    for k in range(4):
        rows[k] = total[:, 128 * k : 128 * k + 128]
    for dev in range(DEVICES):
        for k in range(4):
            send[dev, k : k + 1, :] = rows[k, dev : dev + 1, :]

    greet_all(me)

    def cls_copy(k):
        return pltpu.make_async_remote_copy(
            src_ref=mine,
            dst_ref=cls_ref.at[gx],
            send_sem=cls_sem.at[0],
            recv_sem=cls_sem.at[1],
            device_id=(lax.rem(gx + k, N_GX), gy),
            device_id_type=MESH,
        )

    for k in range(1, N_GX):
        cls_copy(k).start()

    def edge_copy(side, k):
        return pltpu.make_async_remote_copy(
            src_ref=edges.at[side],
            dst_ref=edge_ref.at[gx],
            send_sem=edge_sem.at[side],
            recv_sem=edge_sem.at[2],
            device_id=(k + 4 * (1 - side), lax.rem(gy + N_GY - 1 + 2 * side, N_GY)),
            device_id_type=MESH,
        )

    @pl.when(gy > 0)
    def _():
        for k in range(4):
            edge_copy(0, k).start()

    @pl.when(gy < N_GY - 1)
    def _():
        for k in range(4):
            edge_copy(1, k).start()

    cls_ref[gx] = mine[...]
    send_to_all(me, send, wells_ref, wells_sem.at[0], wells_sem.at[1])
    seven = pl.ds(0, N_GX - 1)
    pltpu.make_async_copy(cls_ref.at[seven], cls_ref.at[seven], cls_sem.at[1]).wait()
    pltpu.make_async_copy(cls_ref.at[seven], cls_ref.at[seven], cls_sem.at[0]).wait()
    four = pl.ds(0, 4)

    @pl.when(gy > 0)
    def _():
        pltpu.make_async_copy(edge_ref.at[four], edge_ref.at[four], edge_sem.at[0]).wait()

    @pl.when(gy < N_GY - 1)
    def _():
        pltpu.make_async_copy(edge_ref.at[four], edge_ref.at[four], edge_sem.at[1]).wait()

    upper = gx >= 4

    @pl.when((upper & (gy < N_GY - 1)) | (jnp.logical_not(upper) & (gy > 0)))
    def _():
        pltpu.make_async_copy(edge_ref, edge_ref, edge_sem.at[2]).wait()


def share_call(cell, test, value, classes):
    return pl.pallas_call(
        share_kernel,
        out_shape=(
            jax.ShapeDtypeStruct((DEVICES, 4, 128), F32),
            jax.ShapeDtypeStruct((N_GX, CX * NZ, CY), BF16),
            jax.ShapeDtypeStruct((N_GX, 32, 128), BF16),
        ),
        in_specs=[VMEM] * 4,
        out_specs=(VMEM,) * 3,
        scratch_shapes=[
            pltpu.VMEM((4, DEVICES, 128), F32),
            pltpu.VMEM((DEVICES, 4, 128), F32),
            pltpu.VMEM((CX * NZ, CY), BF16),
            pltpu.VMEM((2, 32, 128), BF16),
            pltpu.SemaphoreType.DMA((2,)),
            pltpu.SemaphoreType.DMA((2,)),
            pltpu.SemaphoreType.DMA((3,)),
        ],
        compiler_params=pltpu.CompilerParams(
            collective_id=0, has_side_effects=True, vmem_limit_bytes=48 * MIB
        ),
    )(cell, test, value, classes)


def roll_to(value, shift):
    shift = shift % 128
    return pltpu.roll(value, shift, 1) if shift else value


def sweeps_kernel(
    wells_ref,
    cls_ref,
    edge_ref,
    class_value_ref,
    out_ref,
    rows,
    plane,
    cond,
    face_x,
    face_y,
    face_z,
    extra,
    dirs,
    resid,
    sol,
    flux,
    acc,
):
    gx, gy = lax.axis_index("gx"), lax.axis_index("gy")
    half = gx // 4
    lane = lax.broadcasted_iota(jnp.int32, (8, 128), 1)
    sub = lax.broadcasted_iota(jnp.int32, (8, 128), 0)
    x_high, y_high = lane // 32, lane % 32

    def tile(j):
        return slice(8 * j, 8 * j + 8)

    from_lane = lax.broadcasted_iota(jnp.int32, (128, 128), 0)
    to_lane = lax.broadcasted_iota(jnp.int32, (128, 128), 1)
    local = (from_lane + jnp.where(half == 0, RIM, HALF + RIM)) % 128
    picks = [
        jnp.where(local == YL * (to_lane % 32) + low, 1.0, 0.0).astype(BF16) for low in range(YL)
    ]
    lane32 = lax.broadcasted_iota(jnp.int32, (32, 128), 1)
    rim_at = jnp.where(half == 0, CY - RIM, 0)
    in_rim = (lane32 >= rim_at) & (lane32 < rim_at + RIM)
    group64 = lax.broadcasted_iota(jnp.int32, (NZ, 128), 1) // 32

    def whole(x):
        o = x // CX
        own = cls_ref[o, NZ * (x % CX) : NZ * (x % CX) + NZ, :].astype(F32)
        side = edge_ref[o].astype(F32)
        parts = []
        for g in (2 * (x % CX), 2 * (x % CX) + 1):
            moved = pltpu.roll(side, lax.rem(rim_at + 128 - RIM * g, 128), 1)
            parts.append(jnp.where(in_rim, moved, own[32 * (g % 2) : 32 * (g % 2) + 32]))
        return jnp.concatenate(parts, axis=0).astype(BF16)

    for x_low in range(XL):
        blocks = jnp.concatenate([whole(XL * h + x_low) for h in range(4)], axis=0)
        for y_low in range(YL):
            moved = jnp.dot(blocks, picks[y_low], preferred_element_type=F32)
            merged = moved[0:NZ]
            for h in range(1, 4):
                merged = jnp.where(group64 == h, moved[NZ * h : NZ * h + NZ], merged)
            value = jnp.zeros((NZ, 128), F32)
            for k in range(NCLASS):
                value = jnp.where(merged == float(k), class_value_ref[k], value)
            plane[...] = value
            for j in range(8):
                cond[x_low, y_low, tile(j), :] = plane[pl.ds(j, 8, stride=8), :]

    zero = jnp.zeros((8, 128), F32)
    first_y = jnp.where((gy == 0) & (half == 0), RIM, -1)
    last_y = jnp.where((gy == N_GY - 1) & (half == 1), RIM + HALF - 1, -2)

    def faces(x_low, _):
        for y_low in range(YL):
            y_loc = YL * y_high + y_low
            for j in range(8):
                c = cond[x_low, y_low, tile(j), :]
                more = jnp.full((8, 128), storage, F32)
                end = x_low == XL - 1
                near = cond[jnp.where(end, 0, x_low + 1), y_low, tile(j), :]
                near = jnp.where(end, pltpu.roll(near, 96, 1), near)
                off = end & (x_high == 3)
                face_x[x_low, y_low, tile(j), :] = jnp.where(off, zero, 0.5 * (c + near))
                more = more + jnp.where(off, 0.5 * c, zero)
                more = more + jnp.where((x_low == 0) & (x_high == 0), 0.5 * c, zero)
                if y_low < YL - 1:
                    near = cond[x_low, y_low + 1, tile(j), :]
                    off = y_loc + 1 == first_y
                else:
                    near = pltpu.roll(cond[x_low, 0, tile(j), :], 127, 1)
                    off = (y_loc + 1 == first_y) | (y_high == 31)
                off = off | (y_loc == last_y)
                face_y[x_low, y_low, tile(j), :] = jnp.where(off, zero, 0.5 * (c + near))
                more = more + jnp.where((y_loc == first_y) | (y_loc == last_y), 0.5 * c, zero)
                if j < 7:
                    face_z[x_low, y_low, tile(j), :] = 0.5 * (c + cond[x_low, y_low, tile(j + 1), :])
                else:
                    near = pltpu.roll(cond[x_low, y_low, tile(0), :], 7, 0)
                    face_z[x_low, y_low, tile(j), :] = jnp.where(sub == 7, zero, 0.5 * (c + near))
                    more = more + jnp.where(sub == 7, 0.5 * c, zero)
                if j == 0:
                    more = more + jnp.where(sub == 0, 0.5 * c, zero)
                extra[x_low, y_low, tile(j), :] = more
        return 0

    lax.fori_loop(0, XL, faces, 0)

    for dev in range(DEVICES):
        for k in range(4):
            rows[k, dev : dev + 1, :] = wells_ref[dev, k : k + 1, :]
    lane16 = lax.broadcasted_iota(jnp.int32, (16, 128), 1)
    row_high = lax.broadcasted_iota(jnp.int32, (HIGHS, 128), 0)
    row_low = lax.broadcasted_iota(jnp.int32, (256, 128), 0)
    acc[...] = jnp.zeros_like(acc)

    def level(n, _):
        row, at = n // 8, n % 8 * CAP
        codes = jnp.zeros((16, 128), F32)
        values = jnp.zeros((16, 128), F32)
        for g in range(8):
            here = lane16 // CAP == g
            turn = lax.rem(CAP * g + 128 - at, 128)
            block = rows[row, 16 * g : 16 * g + 16, :]
            codes = jnp.where(here, pltpu.roll(block, turn, 1), codes)
            block = rows[2 + row, 16 * g : 16 * g + 16, :]
            values = jnp.where(here, pltpu.roll(block, turn, 1), values)

        @pl.when(jnp.max(jnp.abs(values)) > 0.0)
        def _():
            whole_codes = codes.astype(jnp.int32)
            highs, lows = whole_codes // 256, whole_codes % 256
            first = values.astype(BF16).astype(F32)
            second = values - first
            left, right_a, right_b = [], [], []
            for r in range(16):
                left.append(jnp.where(row_high == highs[r : r + 1], 1.0, 0.0).astype(BF16))
                same = row_low == lows[r : r + 1]
                right_a.append(jnp.where(same, first[r : r + 1], 0.0).astype(BF16))
                right_b.append(jnp.where(same, second[r : r + 1], 0.0).astype(BF16))
            left = jnp.concatenate(left, axis=1)
            acc[...] += lax.dot_general(
                left, jnp.concatenate(right_a, axis=1), NT, preferred_element_type=F32
            ) + lax.dot_general(
                left, jnp.concatenate(right_b, axis=1), NT, preferred_element_type=F32
            )

        return 0

    lax.fori_loop(0, SLOTS // CAP, level, 0)

    middle, factors = cheb_setup()
    for x_low in range(XL):
        for y_low in range(YL):
            at = NZ * (x_low % 4 * YL + y_low)
            value = acc[at : at + NZ, x_low // 4 * 128 : x_low // 4 * 128 + 128]
            resid[x_low, y_low] = value
            dirs[0, x_low, y_low] = value / middle
            sol[x_low, y_low] = jnp.zeros((NZ, 128), F32)

    keeps = [pair[0] for pair in factors]
    news = [pair[1] for pair in factors]

    def sweep(k, _):
        par = lax.rem(k, 2)
        nxt = 1 - par
        keep, new = jnp.float32(keeps[0]), jnp.float32(news[0])
        for n in range(1, SWEEPS - 1):
            keep = jnp.where(k == n, jnp.float32(keeps[n]), keep)
            new = jnp.where(k == n, jnp.float32(news[n]), new)
        for y_low in range(YL):
            for j in range(8):
                over = face_x[XL - 1, y_low, tile(j), :] * (
                    pltpu.roll(dirs[par, 0, y_low, tile(j), :], 96, 1)
                    - dirs[par, XL - 1, y_low, tile(j), :]
                )
                flux[XL - 1, y_low, tile(j), :] = over
                flux[XL, y_low, tile(j), :] = pltpu.roll(over, 32, 1)
        for x_low in range(XL):
            behind = XL if x_low == 0 else x_low - 1
            v = [[dirs[par, x_low, y_low, tile(j), :] for y_low in range(YL)] for j in range(8)]
            z_old = []
            for y_low in range(YL):
                z_old.append(
                    pltpu.roll(
                        face_z[x_low, y_low, tile(7), :]
                        * (pltpu.roll(v[0][y_low], 7, 0) - v[7][y_low]),
                        1,
                        0,
                    )
                )
            for j in range(8):
                fy = [
                    face_y[x_low, y_low, tile(j), :]
                    * (
                        (v[j][y_low + 1] if y_low < YL - 1 else pltpu.roll(v[j][0], 127, 1))
                        - v[j][y_low]
                    )
                    for y_low in range(YL)
                ]
                for y_low in range(YL):
                    here = v[j][y_low]
                    at = (x_low, y_low, tile(j))
                    if x_low < XL - 1:
                        fx = face_x[at] * (dirs[par, x_low + 1, y_low, tile(j), :] - here)
                        flux[at] = fx
                    else:
                        fx = flux[at]
                    above = v[j + 1][y_low] if j < 7 else pltpu.roll(v[0][y_low], 7, 0)
                    fz = face_z[at] * (above - here)
                    fy_old = fy[y_low - 1] if y_low else pltpu.roll(fy[YL - 1], 1, 1)
                    gain = (fx - flux[behind, y_low, tile(j), :]) + (fy[y_low] - fy_old)
                    gain = gain + (fz - z_old[y_low])
                    z_old[y_low] = fz
                    left = resid[at] + (gain - extra[at] * here)
                    resid[at] = left
                    sol[at] = sol[at] + here
                    dirs[nxt, x_low, y_low, tile(j), :] = keep * here + new * left
        return 0

    lax.fori_loop(0, SWEEPS - 1, sweep, 0)
    last = (SWEEPS - 1) % 2

    row = lax.broadcasted_iota(jnp.int32, (YL * 128, 256), 0)
    col = lax.broadcasted_iota(jnp.int32, (YL * 128, 256), 1)
    put = jnp.where(
        (row % 128 // 32 == col // HALF)
        & (YL * (row % 32) + row // 128 == col % HALF + RIM),
        1.0,
        0.0,
    ).astype(BF16)
    left_half = lax.broadcasted_iota(jnp.int32, (NZ, 128), 1) < HALF
    for odd in range(2):
        wide = []
        for x_low in range(4 * odd, 4 * odd + 4):
            field = jnp.concatenate(
                [sol[x_low, y_low] + dirs[last, x_low, y_low] for y_low in range(YL)], axis=1
            )
            first = field.astype(BF16)
            second = (field - first.astype(F32)).astype(BF16)
            wide.append(
                jnp.dot(first, put, preferred_element_type=F32)
                + jnp.dot(second, put, preferred_element_type=F32)
            )
        for h in range(4):
            lanes = slice(128 * (h // 2), 128 * (h // 2) + 128)
            for n in range(2):
                a, b = wide[n][:, lanes], wide[n + 2][:, lanes]
                if h % 2 == 0:
                    both = jnp.where(left_half, a, pltpu.roll(b, 64, 1))
                else:
                    both = jnp.where(left_half, pltpu.roll(a, 64, 1), b)
                for j in range(8):
                    out_ref[2 * h + odd, pl.ds(NZ * n + j, 8, stride=8), :] = both[tile(j)]


def sweeps_call(wells, classes, edges, class_value):
    block = (XL, YL, NZ, 128)
    return pl.pallas_call(
        sweeps_kernel,
        out_shape=jax.ShapeDtypeStruct((N_GX, 2 * NZ, 128), F32),
        in_specs=[VMEM] * 3 + [pl.BlockSpec(memory_space=pltpu.SMEM)],
        out_specs=VMEM,
        scratch_shapes=[
            pltpu.VMEM((4, DEVICES, 128), F32),
            pltpu.VMEM((NZ, 128), F32),
            pltpu.VMEM(block, F32),
            pltpu.VMEM(block, F32),
            pltpu.VMEM(block, F32),
            pltpu.VMEM(block, F32),
            pltpu.VMEM(block, F32),
            pltpu.VMEM((2,) + block, F32),
            pltpu.VMEM(block, F32),
            pltpu.VMEM(block, F32),
            pltpu.VMEM((XL + 1, YL, NZ, 128), F32),
            pltpu.VMEM((HIGHS, 256), F32),
        ],
        compiler_params=pltpu.CompilerParams(vmem_limit_bytes=48 * MIB),
    )(wells, classes, edges, class_value)


def groups_of(gx, gy):
    tail = gx == N_GX - 1
    low = jnp.where(tail, gy % 8, gy)
    high = jnp.where(tail, gy % 8 + 8, (gy + gx + 1) % GROUPS)
    return low, high, tail & (gy >= 8)


def takers_of(group):
    out = []
    for k in range(N_GX - 1):
        out.append(((k, group), 0))
        out.append(((k, (group + GROUPS - k - 1) % GROUPS), 1))
    place = group // 8
    out.append(((N_GX - 1, group % 8), place))
    out.append(((N_GX - 1, group % 8 + 8), place))
    return out


ROWS_STEP = 8


def zones_kernel(
    zone_ref,
    adj_ref,
    class_ref,
    class_value_ref,
    draw_ref,
    out_ref,
    adj,
    sens_ref,
    owner_of,
    left,
    right,
    acc,
    send,
    recv,
    mine,
    sem,
    got_sem,
    put_sem,
    adj_sem,
):
    me = my_index()
    gx, gy = lax.axis_index("gx"), lax.axis_index("gy")
    greet_all(me)

    def back(k):
        dev = lax.rem(gx + k, N_GX)
        return pltpu.make_async_remote_copy(
            src_ref=adj_ref.at[dev],
            dst_ref=adj.at[gx],
            send_sem=adj_sem.at[0],
            recv_sem=adj_sem.at[1],
            device_id=(dev, gy),
            device_id_type=MESH,
        )

    for k in range(1, N_GX):
        back(k).start()
    adj[gx] = adj_ref[gx]
    left_half = lax.broadcasted_iota(jnp.int32, (NZ, 128), 1) < HALF
    owner_of[...] = (
        (lax.broadcasted_iota(jnp.int32, (TESTS * DEVICES, 128), 0) // TESTS)
        .astype(F32)
        .astype(BF16)
    )
    acc[...] = jnp.zeros_like(acc)
    inner = lax.broadcasted_iota(jnp.int32, (256, 128), 0).astype(F32).astype(BF16)
    sub = lax.broadcasted_iota(jnp.int32, (8, 128), 0) % TESTS
    conduct = []
    for x in range(CX):
        cls = class_ref[NZ * x : NZ * x + NZ, :]
        value = jnp.zeros((NZ, CY), F32)
        for k in range(NCLASS):
            value = jnp.where(cls == k, class_value_ref[k], value)
        conduct.append(value)
    seven = pl.ds(0, N_GX - 1)
    pltpu.make_async_copy(adj.at[seven], adj.at[seven], adj_sem.at[1]).wait()
    for t in range(TESTS):
        for n in range(2):
            a, b = adj[t, NZ * n : NZ * n + NZ, :], adj[4 + t, NZ * n : NZ * n + NZ, :]
            for x, field in (
                (n, jnp.where(left_half, a, pltpu.roll(b, 64, 1))),
                (n + 2, jnp.where(left_half, pltpu.roll(a, 64, 1), b)),
            ):
                at = slice(NZ * x, NZ * x + NZ)
                sens_ref[t, at, :] = conduct[x] * draw_ref[t, at, :].astype(F32) * field

    def spread(row, times):
        return jnp.concatenate([jnp.broadcast_to(row, (16, 128)).astype(BF16)] * times, axis=0)

    def step(i, _):
        at = pl.ds(pl.multiple_of(i * ROWS_STEP, ROWS_STEP), ROWS_STEP)
        zone = zone_ref[at, :].astype(F32)
        owner = ((zone + 0.5) * (1.0 / SHARE)).astype(jnp.int32).astype(F32)
        place = zone - owner * SHARE
        values = [sens_ref[t, at, :] for t in range(TESTS)]
        for r in range(ROWS_STEP):
            row = slice(r, r + 1)
            four = jnp.broadcast_to(values[0][row], (8, 128))
            for t in range(1, TESTS):
                four = jnp.where(sub == t, jnp.broadcast_to(values[t][row], (8, 128)), four)
            four = jnp.concatenate([four, four], axis=0).astype(BF16)
            cols = slice(128 * r, 128 * r + 128)
            left[:, cols] = jnp.where(
                owner_of[...] == spread(owner[row], TESTS * DEVICES // 16),
                jnp.concatenate([four] * (TESTS * DEVICES // 16), axis=0),
                jnp.zeros((), BF16),
            )
            for part in range(SHARE // 256):
                right[256 * part : 256 * part + 256, cols] = jnp.where(
                    inner == spread(place[row] - 256.0 * part, 16),
                    jnp.ones((), BF16),
                    jnp.zeros((), BF16),
                )
        acc[...] += lax.dot_general(left[...], right[...], NT, preferred_element_type=F32)
        return 0

    lax.fori_loop(0, CX * NZ // ROWS_STEP, step, 0)
    for dev in range(DEVICES):
        send[dev] = acc[TESTS * dev : TESTS * dev + TESTS, :]

    send_to_all(me, send, recv, sem.at[0], sem.at[1])
    pltpu.make_async_copy(adj.at[seven], adj.at[seven], adj_sem.at[0]).wait()

    def add(s, total):
        for n in range(8):
            total = total + recv[8 * s + n]
        return total

    total = lax.fori_loop(0, DEVICES // 8, add, jnp.zeros((TESTS, SHARE), F32))
    mine[...] = total.astype(BF16).astype(F32)

    group, member = me // MEMBERS, me % MEMBERS

    def put(n, dev, place):
        return pltpu.make_async_remote_copy(
            src_ref=mine,
            dst_ref=out_ref.at[place, member],
            send_sem=put_sem.at[n],
            recv_sem=got_sem.at[place, member],
            device_id=dev,
            device_id_type=MESH,
        )

    takers = takers_of(group)
    for n, (dev, place) in enumerate(takers):
        self_here = dev[0] * N_GY + dev[1] == me

        @pl.when(jnp.logical_not(self_here))
        def _():
            put(n, dev, place).start()

        @pl.when(self_here)
        def _():
            out_ref[place, member] = mine[...]

    low, high, _ = groups_of(gx, gy)
    for place, held in ((0, low), (1, high)):
        for m in range(MEMBERS):

            @pl.when(held * MEMBERS + m != me)
            def _():
                pltpu.make_async_copy(
                    out_ref.at[place, m], out_ref.at[place, m], got_sem.at[place, m]
                ).wait()

    for n, (dev, place) in enumerate(takers):

        @pl.when(dev[0] * N_GY + dev[1] != me)
        def _():
            put(n, dev, place).wait_send()


def zones_call(zone, adjoint, classes, class_value, drawdown):
    rows = TESTS * DEVICES
    width = ROWS_STEP * 128
    return pl.pallas_call(
        zones_kernel,
        out_shape=jax.ShapeDtypeStruct((2, MEMBERS, TESTS, SHARE), F32),
        in_specs=[VMEM] * 3 + [pl.BlockSpec(memory_space=pltpu.SMEM), VMEM],
        out_specs=VMEM,
        scratch_shapes=[
            pltpu.VMEM((N_GX, 2 * NZ, 128), F32),
            pltpu.VMEM((TESTS, CX * NZ, CY), F32),
            pltpu.VMEM((rows, 128), BF16),
            pltpu.VMEM((rows, width), BF16),
            pltpu.VMEM((SHARE, width), BF16),
            pltpu.VMEM((rows, SHARE), F32),
            pltpu.VMEM((DEVICES, TESTS, SHARE), F32),
            pltpu.VMEM((DEVICES, TESTS, SHARE), F32),
            pltpu.VMEM((TESTS, SHARE), F32),
            pltpu.SemaphoreType.DMA((2,)),
            pltpu.SemaphoreType.DMA((2, MEMBERS)),
            pltpu.SemaphoreType.DMA((16,)),
            pltpu.SemaphoreType.DMA((2,)),
        ],
        compiler_params=pltpu.CompilerParams(
            collective_id=2, has_side_effects=True, vmem_limit_bytes=48 * MIB
        ),
    )(zone, adjoint, classes, class_value, drawdown)


BLOCK = 1024
STRIP = 64


def cov_kernel(diag_ref, pts_ref, sums_ref, out_ref, z_ref, rows_ref, tile_ref):
    blocks = GROUP // BLOCK
    diag = diag_ref[0]
    out_ref[...] = jnp.zeros_like(out_ref)
    for g in range(2):
        for m in range(MEMBERS):
            both = jnp.concatenate([sums_ref[g, m], jnp.zeros((TESTS, SHARE), F32)], axis=0)
            z_ref[g, :, SHARE * m : SHARE * m + SHARE] = both.astype(BF16)

    def tile(cg, c):
        cols = [pts_ref[cg, k : k + 1, pl.ds(pl.multiple_of(c * BLOCK, BLOCK), BLOCK)] for k in range(3)]

        def body(i, _):
            r0 = pl.multiple_of(i * STRIP, STRIP)
            squared = None
            for k in range(3):
                near = jnp.concatenate([rows_ref[k, pl.ds(r0, STRIP), :]] * (BLOCK // 128), axis=1)
                gap = near - cols[k]
                squared = gap * gap if squared is None else squared + gap * gap
            squared = jnp.maximum(squared, 1e-30)
            dist = squared * lax.rsqrt(squared)
            tile_ref[pl.ds(r0, STRIP), :] = jnp.exp2(-dist).astype(BF16)
            return 0

        lax.fori_loop(0, BLOCK // STRIP, body, 0, unroll=True)

    def phase(rg, _):
        cg = jnp.where(diag == 1, rg, 1)

        def row_block(r, _):
            rs = pl.ds(pl.multiple_of(r * BLOCK, BLOCK), BLOCK)
            for k in range(3):
                rows_ref[k] = jnp.broadcast_to(pts_ref[rg, k : k + 1, rs], (128, BLOCK)).T
            near = z_ref[rg, :, rs]

            def col_block(c, acc):
                tile(cg, c)
                cs = pl.ds(pl.multiple_of(c * BLOCK, BLOCK), BLOCK)
                acc = acc + lax.dot_general(
                    z_ref[cg, :, cs], tile_ref[...], NT, preferred_element_type=F32
                )

                @pl.when(jnp.logical_not((diag == 1) & (c == r)))
                def _():
                    out_ref[cg, :, cs] += jnp.dot(near, tile_ref[...], preferred_element_type=F32)

                return acc

            first = jnp.where(diag == 1, r, 0)
            acc = lax.fori_loop(first, blocks, col_block, jnp.zeros((8, BLOCK), F32))
            out_ref[rg, :, rs] += acc
            return 0

        lax.fori_loop(0, blocks, row_block, 0)
        return 0

    lax.fori_loop(0, 1 + diag, phase, 0)


def cov_call(diag, pts, sums):
    return pl.pallas_call(
        cov_kernel,
        out_shape=jax.ShapeDtypeStruct((2, 8, GROUP), F32),
        in_specs=[pl.BlockSpec(memory_space=pltpu.SMEM), VMEM, VMEM],
        out_specs=VMEM,
        scratch_shapes=[
            pltpu.VMEM((2, 8, GROUP), BF16),
            pltpu.VMEM((3, BLOCK, 128), F32),
            pltpu.VMEM((BLOCK, BLOCK), BF16),
        ],
        compiler_params=pltpu.CompilerParams(vmem_limit_bytes=48 * MIB),
    )(diag, pts, sums)


def reduce_kernel(part_ref, out_ref, send, recv, send_sem, recv_sem):
    me = my_index()
    gx, gy = lax.axis_index("gx"), lax.axis_index("gy")
    low, high, diag = groups_of(gx, gy)
    group, member = me // MEMBERS, me % MEMBERS
    for g in range(2):
        for m in range(MEMBERS):
            send[g, m] = part_ref[g, 0:TESTS, SHARE * m : SHARE * m + SHARE]

    takers = takers_of(group)
    barrier = pltpu.get_barrier_semaphore()
    for place, held in ((0, low), (1, high)):
        for m in range(MEMBERS):
            owner = held * MEMBERS + m

            @pl.when(owner != me)
            def _():
                pl.semaphore_signal(barrier, inc=1, device_id=coords(owner), device_id_type=MESH)

    for dev, _ in takers:

        @pl.when(dev[0] * N_GY + dev[1] != me)
        def _():
            pl.semaphore_signal(barrier, inc=1, device_id=dev, device_id_type=MESH)

    self_here = (low == group) | (high == group)
    pl.semaphore_wait(barrier, 32 - 2 * self_here.astype(jnp.int32))

    def put(place, m, held, slot):
        return pltpu.make_async_remote_copy(
            src_ref=send.at[place, m],
            dst_ref=recv.at[slot],
            send_sem=send_sem.at[place, m],
            recv_sem=recv_sem.at[slot],
            device_id=coords(held * MEMBERS + m),
            device_id_type=MESH,
        )

    sides = (
        (0, low, jnp.where(diag, low, high)),
        (1, high, jnp.where(diag, high, low)),
    )
    for place, held, slot in sides:
        for m in range(MEMBERS):

            @pl.when(held * MEMBERS + m != me)
            def _():
                put(place, m, held, slot).start()

            @pl.when(held * MEMBERS + m == me)
            def _():
                recv[slot] = send[place, m]

    own_slot = jnp.where(
        low == group, jnp.where(diag, low, high), jnp.where(diag, high, low)
    )
    for slot in range(GROUPS):

        @pl.when(jnp.logical_not(self_here & (own_slot == slot)))
        def _():
            pltpu.make_async_copy(recv.at[slot], recv.at[slot], recv_sem.at[slot]).wait()

    total = recv[0]
    for slot in range(1, GROUPS):
        total = total + recv[slot]
    out_ref[...] = total.astype(BF16)
    for place, held, slot in sides:
        for m in range(MEMBERS):

            @pl.when(held * MEMBERS + m != me)
            def _():
                put(place, m, held, slot).wait_send()


def reduce_call(parts):
    return pl.pallas_call(
        reduce_kernel,
        out_shape=jax.ShapeDtypeStruct((TESTS, SHARE), BF16),
        in_specs=[VMEM],
        out_specs=VMEM,
        scratch_shapes=[
            pltpu.VMEM((2, MEMBERS, TESTS, SHARE), F32),
            pltpu.VMEM((GROUPS, TESTS, SHARE), F32),
            pltpu.SemaphoreType.DMA((2, MEMBERS)),
            pltpu.SemaphoreType.DMA((GROUPS,)),
        ],
        compiler_params=pltpu.CompilerParams(
            collective_id=3, has_side_effects=True, vmem_limit_bytes=32 * MIB
        ),
    )(parts)


def per_device(
    well_cell, well_test, well_value, cond_class, class_value, zone_id, drawdown, centroid
):
    gx, gy = lax.axis_index("gx"), lax.axis_index("gy")
    low, high, diag = groups_of(gx, gy)
    pts = jnp.stack(
        [lax.dynamic_slice_in_dim(centroid, held * GROUP, GROUP, 1) for held in (low, high)]
    ) * (LOG2E / corr_len)
    wells, classes, edges = share_call(
        well_cell[None], well_test[None], well_value[None], cond_class
    )
    adjoint = sweeps_call(wells, classes, edges, class_value)
    rows = CX * NZ
    sums = zones_call(
        zone_id.reshape(rows, CY),
        adjoint,
        cond_class.reshape(rows, CY),
        class_value,
        drawdown.reshape(TESTS, rows, CY),
    )
    parts = cov_call(diag.astype(jnp.int32)[None], pts, sums)
    return reduce_call(parts)


def solution(mesh):
    return jax.shard_map(
        per_device,
        mesh=mesh,
        in_specs=(
            P(("gx", "gy")),
            P(("gx", "gy")),
            P(("gx", "gy")),
            P("gx", None, "gy"),
            P(),
            P("gx", None, "gy"),
            P(None, "gx", None, "gy"),
            P(),
        ),
        out_specs=P(None, ("gx", "gy")),
        check_vma=False,
    )
```

```python
import functools

import jax
import jax.numpy as jnp
from jax import lax
from jax.experimental import pallas as pl
from jax.experimental.pallas import tpu as pltpu
from jax.sharding import PartitionSpec as P

MESH = pl.DeviceIdType.MESH
NT = (((1,), (1,)), ((), ()))
VMEM = pl.BlockSpec(memory_space=pltpu.VMEM)
F32 = jnp.float32
BF16 = jnp.bfloat16
MIB = 2**20

SWEEPS = 12
TESTS = 4
CX, NZ, CY = 4, 64, 128
N_GX, N_GY = 8, 16
DEVICES = N_GX * N_GY
NCLASS = 16
CAP = 16
ZONES = 98304
SHARE = ZONES // DEVICES
GROUPS = 16
MEMBERS = DEVICES // GROUPS
GROUP = ZONES // GROUPS
HALF = CY // 2
RIM = 16
XL, YL = 8, 3
HIGHS = 4 * YL * NZ
SLOTS = 16 * CAP

storage = 0.02
lam_low = 0.02
lam_high = 36.02
corr_len = 0.1
LOG2E = 1.4426950408889634


def cheb_setup():
    middle = 0.5 * (lam_high + lam_low)
    spread = 0.5 * (lam_high - lam_low)
    ratio_mid = middle / spread
    current = 1.0 / ratio_mid
    factors = []
    for counter in range(SWEEPS - 1):
        updated = 1.0 / (2.0 * ratio_mid - current)
        factors.append((updated * current, 2.0 * updated / spread))
        current = updated
    return (middle, factors)


def my_index():
    return lax.axis_index("gx") * N_GY + lax.axis_index("gy")


def coords(dev):
    return (dev // N_GY, dev % N_GY)


def greet(devs):
    barrier = pltpu.get_barrier_semaphore()
    for dev in devs:
        pl.semaphore_signal(barrier, inc=1, device_id=dev, device_id_type=MESH)
    pl.semaphore_wait(barrier, len(devs))


def greet_all(me):
    barrier = pltpu.get_barrier_semaphore()

    def each(k, _):
        dev = lax.rem(me + k, DEVICES)
        pl.semaphore_signal(barrier, inc=1, device_id=coords(dev), device_id_type=MESH)
        return 0

    lax.fori_loop(1, DEVICES, each, 0)
    pl.semaphore_wait(barrier, DEVICES - 1)


def send_to_all(me, send, recv, send_sem, recv_sem):
    def each(k, _):
        dev = lax.rem(me + k, DEVICES)
        pltpu.make_async_remote_copy(
            src_ref=send.at[dev],
            dst_ref=recv.at[me],
            send_sem=send_sem,
            recv_sem=recv_sem,
            device_id=coords(dev),
            device_id_type=MESH,
        ).start()
        return 0

    lax.fori_loop(1, DEVICES, each, 0)
    recv[me] = send[me]
    rest = pl.ds(0, DEVICES - 1)
    pltpu.make_async_copy(recv.at[rest], recv.at[rest], recv_sem).wait()
    pltpu.make_async_copy(send.at[rest], send.at[rest], send_sem).wait()


def share_kernel(
    cell_ref,
    test_ref,
    value_ref,
    class_ref,
    wells_ref,
    cls_ref,
    edge_ref,
    rows,
    send,
    mine,
    edges,
    wells_sem,
    cls_sem,
    edge_sem,
):
    me = my_index()
    gx, gy = lax.axis_index("gx"), lax.axis_index("gy")
    lane = lax.broadcasted_iota(jnp.int32, (32, 128), 1)
    classes = class_ref[...].reshape(CX * NZ, CY).astype(F32)
    mine[...] = classes.astype(BF16)
    for side, first in ((0, 0), (1, CY - RIM)):
        pack = jnp.zeros((32, 128), F32)
        for g in range(8):
            here = (lane >= RIM * g) & (lane < RIM * g + RIM)
            pack = jnp.where(here, roll_to(classes[32 * g : 32 * g + 32], RIM * g - first), pack)
        edges[side] = pack.astype(BF16)
    edge_ref[...] = jnp.zeros_like(edge_ref)

    cell, test, value = cell_ref[...], test_ref[...], value_ref[...]
    n_rows = 2 * cell.shape[1]
    y = cell % (CY * N_GY)
    z = cell // (CY * N_GY) % NZ
    x = cell // (CY * N_GY * NZ)
    block = y // HALF
    within = y % HALF
    step = jnp.where(within < RIM, -1, jnp.where(within >= HALF - RIM, 1, 0))
    other = block + step
    valid = (step != 0) & (other >= 0) & (other < 2 * N_GY)

    def twice(first, second):
        return jnp.concatenate([first, second], axis=1)

    block, y, z, x = twice(block, other), twice(y, y), twice(z, z), twice(x, x)
    test, value = twice(test, test), twice(value, value)
    owner = (block % 2 * 4 + test) * N_GY + block // 2
    owner = twice(owner[:, : n_rows // 2], jnp.where(valid, owner[:, n_rows // 2 :], -1))
    y_loc = y - (block * HALF - RIM)
    x_low = x % XL
    high = ((x_low % 4 * YL + y_loc % YL) * 8 + z % 8) * 8 + z // 8
    low = x_low // 4 * 128 + x // XL * 32 + y_loc // YL
    code = (high * 256 + low).astype(F32)
    hot = jnp.where(
        lax.broadcasted_iota(jnp.int32, (DEVICES, n_rows), 0) == owner, 1.0, 0.0
    )
    earlier = jnp.where(
        lax.broadcasted_iota(jnp.int32, (n_rows, n_rows), 0)
        < lax.broadcasted_iota(jnp.int32, (n_rows, n_rows), 1),
        1.0,
        0.0,
    )
    hot16 = hot.astype(BF16)
    count = jnp.dot(hot16, earlier.astype(BF16), preferred_element_type=F32)
    rank = jnp.sum(hot * count, axis=0, keepdims=True).astype(jnp.int32)
    slot = lax.broadcasted_iota(jnp.int32, (SLOTS, n_rows), 0)
    part = jnp.concatenate(
        [jnp.where(slot == rank, code, 0.0), jnp.where(slot == rank, value, 0.0)], axis=0
    )
    total = None
    for _ in range(3):
        piece = part.astype(BF16)
        part = part - piece.astype(F32)
        term = lax.dot_general(hot16, piece, NT, preferred_element_type=F32)
        total = term if total is None else total + term
    for k in range(4):
        rows[k] = total[:, 128 * k : 128 * k + 128]
    for dev in range(DEVICES):
        for k in range(4):
            send[dev, k : k + 1, :] = rows[k, dev : dev + 1, :]

    greet_all(me)

    def cls_copy(k):
        return pltpu.make_async_remote_copy(
            src_ref=mine,
            dst_ref=cls_ref.at[gx],
            send_sem=cls_sem.at[0],
            recv_sem=cls_sem.at[1],
            device_id=(lax.rem(gx + k, N_GX), gy),
            device_id_type=MESH,
        )

    for k in range(1, N_GX):
        cls_copy(k).start()

    def edge_copy(side, k):
        return pltpu.make_async_remote_copy(
            src_ref=edges.at[side],
            dst_ref=edge_ref.at[gx],
            send_sem=edge_sem.at[side],
            recv_sem=edge_sem.at[2],
            device_id=(k + 4 * (1 - side), lax.rem(gy + N_GY - 1 + 2 * side, N_GY)),
            device_id_type=MESH,
        )

    @pl.when(gy > 0)
    def _():
        for k in range(4):
            edge_copy(0, k).start()

    @pl.when(gy < N_GY - 1)
    def _():
        for k in range(4):
            edge_copy(1, k).start()

    cls_ref[gx] = mine[...]
    send_to_all(me, send, wells_ref, wells_sem.at[0], wells_sem.at[1])
    seven = pl.ds(0, N_GX - 1)
    pltpu.make_async_copy(cls_ref.at[seven], cls_ref.at[seven], cls_sem.at[1]).wait()
    pltpu.make_async_copy(cls_ref.at[seven], cls_ref.at[seven], cls_sem.at[0]).wait()
    four = pl.ds(0, 4)

    @pl.when(gy > 0)
    def _():
        pltpu.make_async_copy(edge_ref.at[four], edge_ref.at[four], edge_sem.at[0]).wait()

    @pl.when(gy < N_GY - 1)
    def _():
        pltpu.make_async_copy(edge_ref.at[four], edge_ref.at[four], edge_sem.at[1]).wait()

    upper = gx >= 4

    @pl.when((upper & (gy < N_GY - 1)) | (jnp.logical_not(upper) & (gy > 0)))
    def _():
        pltpu.make_async_copy(edge_ref, edge_ref, edge_sem.at[2]).wait()


def share_call(cell, test, value, classes):
    return pl.pallas_call(
        share_kernel,
        out_shape=(
            jax.ShapeDtypeStruct((DEVICES, 4, 128), F32),
            jax.ShapeDtypeStruct((N_GX, CX * NZ, CY), BF16),
            jax.ShapeDtypeStruct((N_GX, 32, 128), BF16),
        ),
        in_specs=[VMEM] * 4,
        out_specs=(VMEM,) * 3,
        scratch_shapes=[
            pltpu.VMEM((4, DEVICES, 128), F32),
            pltpu.VMEM((DEVICES, 4, 128), F32),
            pltpu.VMEM((CX * NZ, CY), BF16),
            pltpu.VMEM((2, 32, 128), BF16),
            pltpu.SemaphoreType.DMA((2,)),
            pltpu.SemaphoreType.DMA((2,)),
            pltpu.SemaphoreType.DMA((3,)),
        ],
        compiler_params=pltpu.CompilerParams(
            collective_id=0, has_side_effects=True, vmem_limit_bytes=48 * MIB
        ),
    )(cell, test, value, classes)


def roll_to(value, shift):
    shift = shift % 128
    return pltpu.roll(value, shift, 1) if shift else value


def tile(j):
    return slice(8 * j, 8 * j + 8)


def source_kernel(
    wells_ref, cls_ref, edge_ref, class_value_ref, cond, src_ref, rows, plane, acc
):
    half = lax.axis_index("gx") // 4

    from_lane = lax.broadcasted_iota(jnp.int32, (128, 128), 0)
    to_lane = lax.broadcasted_iota(jnp.int32, (128, 128), 1)
    local = (from_lane + jnp.where(half == 0, RIM, HALF + RIM)) % 128
    picks = [
        jnp.where(local == YL * (to_lane % 32) + low, 1.0, 0.0).astype(BF16) for low in range(YL)
    ]
    lane32 = lax.broadcasted_iota(jnp.int32, (32, 128), 1)
    rim_at = jnp.where(half == 0, CY - RIM, 0)
    in_rim = (lane32 >= rim_at) & (lane32 < rim_at + RIM)
    group64 = lax.broadcasted_iota(jnp.int32, (NZ, 128), 1) // 32

    def whole(x):
        o = x // CX
        own = cls_ref[o, NZ * (x % CX) : NZ * (x % CX) + NZ, :].astype(F32)
        side = edge_ref[o].astype(F32)
        parts = []
        for g in (2 * (x % CX), 2 * (x % CX) + 1):
            moved = pltpu.roll(side, lax.rem(rim_at + 128 - RIM * g, 128), 1)
            parts.append(jnp.where(in_rim, moved, own[32 * (g % 2) : 32 * (g % 2) + 32]))
        return jnp.concatenate(parts, axis=0).astype(BF16)

    for x_low in range(XL):
        blocks = jnp.concatenate([whole(XL * h + x_low) for h in range(4)], axis=0)
        for y_low in range(YL):
            moved = jnp.dot(blocks, picks[y_low], preferred_element_type=F32)
            merged = moved[0:NZ]
            for h in range(1, 4):
                merged = jnp.where(group64 == h, moved[NZ * h : NZ * h + NZ], merged)
            value = jnp.zeros((NZ, 128), F32)
            for k in range(NCLASS):
                value = jnp.where(merged == float(k), class_value_ref[k], value)
            plane[...] = value
            for j in range(8):
                cond[x_low, y_low, tile(j), :] = plane[pl.ds(j, 8, stride=8), :]

    for dev in range(DEVICES):
        for k in range(4):
            rows[k, dev : dev + 1, :] = wells_ref[dev, k : k + 1, :]
    lane16 = lax.broadcasted_iota(jnp.int32, (16, 128), 1)
    row_high = lax.broadcasted_iota(jnp.int32, (HIGHS, 128), 0)
    row_low = lax.broadcasted_iota(jnp.int32, (256, 128), 0)
    acc[...] = jnp.zeros_like(acc)

    def level(n, _):
        row, at = n // 8, n % 8 * CAP
        codes = jnp.zeros((16, 128), F32)
        values = jnp.zeros((16, 128), F32)
        for g in range(8):
            here = lane16 // CAP == g
            turn = lax.rem(CAP * g + 128 - at, 128)
            block = rows[row, 16 * g : 16 * g + 16, :]
            codes = jnp.where(here, pltpu.roll(block, turn, 1), codes)
            block = rows[2 + row, 16 * g : 16 * g + 16, :]
            values = jnp.where(here, pltpu.roll(block, turn, 1), values)

        @pl.when(jnp.max(jnp.abs(values)) > 0.0)
        def _():
            whole_codes = codes.astype(jnp.int32)
            highs, lows = whole_codes // 256, whole_codes % 256
            first = values.astype(BF16).astype(F32)
            second = values - first
            left, right_a, right_b = [], [], []
            for r in range(16):
                left.append(jnp.where(row_high == highs[r : r + 1], 1.0, 0.0).astype(BF16))
                same = row_low == lows[r : r + 1]
                right_a.append(jnp.where(same, first[r : r + 1], 0.0).astype(BF16))
                right_b.append(jnp.where(same, second[r : r + 1], 0.0).astype(BF16))
            left = jnp.concatenate(left, axis=1)
            acc[...] += lax.dot_general(
                left, jnp.concatenate(right_a, axis=1), NT, preferred_element_type=F32
            ) + lax.dot_general(
                left, jnp.concatenate(right_b, axis=1), NT, preferred_element_type=F32
            )

        return 0

    lax.fori_loop(0, SLOTS // CAP, level, 0)

    for x_low in range(XL):
        for y_low in range(YL):
            at = NZ * (x_low % 4 * YL + y_low)
            src_ref[x_low, y_low] = acc[at : at + NZ, x_low // 4 * 128 : x_low // 4 * 128 + 128]


FIELD = (XL, YL, NZ, 128)


def source_call(wells, classes, edges, class_value):
    return pl.pallas_call(
        source_kernel,
        out_shape=(jax.ShapeDtypeStruct(FIELD, F32),) * 2,
        in_specs=[VMEM] * 3 + [pl.BlockSpec(memory_space=pltpu.SMEM)],
        out_specs=(VMEM,) * 2,
        scratch_shapes=[
            pltpu.VMEM((4, DEVICES, 128), F32),
            pltpu.VMEM((NZ, 128), F32),
            pltpu.VMEM((HIGHS, 256), F32),
        ],
        compiler_params=pltpu.CompilerParams(vmem_limit_bytes=48 * MIB),
    )(wells, classes, edges, class_value)


def groups_of(gx, gy):
    tail = gx == N_GX - 1
    low = jnp.where(tail, gy % 8, gy)
    high = jnp.where(tail, gy % 8 + 8, (gy + gx + 1) % GROUPS)
    return low, high, tail & (gy >= 8)


def takers_of(group):
    out = []
    for k in range(N_GX - 1):
        out.append(((k, group), 0))
        out.append(((k, (group + GROUPS - k - 1) % GROUPS), 1))
    place = group // 8
    out.append(((N_GX - 1, group % 8), place))
    out.append(((N_GX - 1, group % 8 + 8), place))
    return out


STEP = 16
INNER = SHARE // 2


def main_kernel(
    cond,
    src_ref,
    zone_ref,
    draw_ref,
    out_ref,
    face_x,
    face_y,
    face_z,
    extra,
    dirs,
    resid,
    sol,
    flux,
    zone_out,
    draw_out,
    zone_in,
    draw_in,
    sens,
    left_a,
    right_a,
    left_b,
    right_b,
    acc,
    send_a,
    recv_a,
    send_b,
    recv_b,
    mine,
    zone_sem,
    draw_sem,
    a_sem,
    b_sem,
    got_sem,
    put_sem,
):
    me = my_index()
    gx, gy = lax.axis_index("gx"), lax.axis_index("gy")
    half = gx // 4
    lane = lax.broadcasted_iota(jnp.int32, (8, 128), 1)
    sub = lax.broadcasted_iota(jnp.int32, (8, 128), 0)
    x_high, y_high = lane // 32, lane % 32
    left_half = lax.broadcasted_iota(jnp.int32, (NZ, 128), 1) < HALF

    group, member = me // MEMBERS, me % MEMBERS
    low_group, high_group, _ = groups_of(gx, gy)
    takers = takers_of(group)
    barrier = pltpu.get_barrier_semaphore()
    for k in range(1, N_GX):
        pl.semaphore_signal(
            barrier, inc=1, device_id=(lax.rem(gx + k, N_GX), gy), device_id_type=MESH
        )
    for k in range(1, N_GY):
        pl.semaphore_signal(
            barrier, inc=1, device_id=(gx, lax.rem(gy + k, N_GY)), device_id_type=MESH
        )
    for held in (low_group, high_group):
        for m in range(MEMBERS):
            owner = held * MEMBERS + m

            @pl.when(owner != me)
            def _():
                pl.semaphore_signal(barrier, inc=1, device_id=coords(owner), device_id_type=MESH)

    for dev, _ in takers:

        @pl.when(dev[0] * N_GY + dev[1] != me)
        def _():
            pl.semaphore_signal(barrier, inc=1, device_id=dev, device_id_type=MESH)

    def packed(fields, side, n):
        a, b = fields[n], fields[n + 2]
        if side == 0:
            return jnp.where(left_half, a, pltpu.roll(b, HALF, 1))
        return jnp.where(left_half, pltpu.roll(a, HALF, 1), b)

    zones = [zone_ref[NZ * x : NZ * x + NZ, :].astype(F32) for x in range(CX)]
    for side in range(2):
        for n in range(2):
            zone_out[side, NZ * n : NZ * n + NZ, :] = packed(zones, side, n)
    for t in range(TESTS):
        draws = [draw_ref[t, NZ * x : NZ * x + NZ, :].astype(F32) for x in range(CX)]
        for side in range(2):
            for n in range(2):
                draw_out[TESTS * side + t, NZ * n : NZ * n + NZ, :] = packed(
                    draws, side, n
                ).astype(BF16)

    self_here = (low_group == group) | (high_group == group)
    pl.semaphore_wait(barrier, N_GX + N_GY - 2 + 32 - 2 * self_here.astype(jnp.int32))

    def to_column(k, src, dst, sems):
        dev = lax.rem(gx + k, N_GX)
        return pltpu.make_async_remote_copy(
            src_ref=src(dev),
            dst_ref=dst,
            send_sem=sems.at[0],
            recv_sem=sems.at[1],
            device_id=(dev, gy),
            device_id_type=MESH,
        )

    for k in range(1, N_GX):
        to_column(k, lambda dev: zone_out.at[dev // TESTS], zone_in.at[gx], zone_sem).start()
        to_column(k, lambda dev: draw_out.at[dev], draw_in.at[gx], draw_sem).start()
    zone_in[gx] = zone_out[half]
    draw_in[gx] = draw_out[gx]

    zero = jnp.zeros((8, 128), F32)
    first_y = jnp.where((gy == 0) & (half == 0), RIM, -1)
    last_y = jnp.where((gy == N_GY - 1) & (half == 1), RIM + HALF - 1, -2)

    def faces(x_low, _):
        for y_low in range(YL):
            y_loc = YL * y_high + y_low
            for j in range(8):
                c = cond[x_low, y_low, tile(j), :]
                more = jnp.full((8, 128), storage, F32)
                end = x_low == XL - 1
                near = cond[jnp.where(end, 0, x_low + 1), y_low, tile(j), :]
                near = jnp.where(end, pltpu.roll(near, 96, 1), near)
                off = end & (x_high == 3)
                face_x[x_low, y_low, tile(j), :] = jnp.where(off, zero, 0.5 * (c + near))
                more = more + jnp.where(off, 0.5 * c, zero)
                more = more + jnp.where((x_low == 0) & (x_high == 0), 0.5 * c, zero)
                if y_low < YL - 1:
                    near = cond[x_low, y_low + 1, tile(j), :]
                    off = y_loc + 1 == first_y
                else:
                    near = pltpu.roll(cond[x_low, 0, tile(j), :], 127, 1)
                    off = (y_loc + 1 == first_y) | (y_high == 31)
                off = off | (y_loc == last_y)
                face_y[x_low, y_low, tile(j), :] = jnp.where(off, zero, 0.5 * (c + near))
                more = more + jnp.where((y_loc == first_y) | (y_loc == last_y), 0.5 * c, zero)
                if j < 7:
                    face_z[x_low, y_low, tile(j), :] = 0.5 * (c + cond[x_low, y_low, tile(j + 1), :])
                else:
                    near = pltpu.roll(cond[x_low, y_low, tile(0), :], 7, 0)
                    face_z[x_low, y_low, tile(j), :] = jnp.where(sub == 7, zero, 0.5 * (c + near))
                    more = more + jnp.where(sub == 7, 0.5 * c, zero)
                if j == 0:
                    more = more + jnp.where(sub == 0, 0.5 * c, zero)
                extra[x_low, y_low, tile(j), :] = more
        return 0

    lax.fori_loop(0, XL, faces, 0)

    middle, factors = cheb_setup()
    for x_low in range(XL):
        for y_low in range(YL):
            value = src_ref[x_low, y_low]
            resid[x_low, y_low] = value
            dirs[0, x_low, y_low] = value / middle
            sol[x_low, y_low] = jnp.zeros((NZ, 128), F32)

    keeps = [pair[0] for pair in factors]
    news = [pair[1] for pair in factors]

    def sweep(k, _):
        par = lax.rem(k, 2)
        nxt = 1 - par
        keep, new = jnp.float32(keeps[0]), jnp.float32(news[0])
        for n in range(1, SWEEPS - 1):
            keep = jnp.where(k == n, jnp.float32(keeps[n]), keep)
            new = jnp.where(k == n, jnp.float32(news[n]), new)
        for y_low in range(YL):
            for j in range(8):
                over = face_x[XL - 1, y_low, tile(j), :] * (
                    pltpu.roll(dirs[par, 0, y_low, tile(j), :], 96, 1)
                    - dirs[par, XL - 1, y_low, tile(j), :]
                )
                flux[XL - 1, y_low, tile(j), :] = over
                flux[XL, y_low, tile(j), :] = pltpu.roll(over, 32, 1)
        for x_low in range(XL):
            behind = XL if x_low == 0 else x_low - 1
            v = [[dirs[par, x_low, y_low, tile(j), :] for y_low in range(YL)] for j in range(8)]
            z_old = []
            for y_low in range(YL):
                z_old.append(
                    pltpu.roll(
                        face_z[x_low, y_low, tile(7), :]
                        * (pltpu.roll(v[0][y_low], 7, 0) - v[7][y_low]),
                        1,
                        0,
                    )
                )
            for j in range(8):
                fy = [
                    face_y[x_low, y_low, tile(j), :]
                    * (
                        (v[j][y_low + 1] if y_low < YL - 1 else pltpu.roll(v[j][0], 127, 1))
                        - v[j][y_low]
                    )
                    for y_low in range(YL)
                ]
                for y_low in range(YL):
                    here = v[j][y_low]
                    at = (x_low, y_low, tile(j))
                    if x_low < XL - 1:
                        fx = face_x[at] * (dirs[par, x_low + 1, y_low, tile(j), :] - here)
                        flux[at] = fx
                    else:
                        fx = flux[at]
                    above = v[j + 1][y_low] if j < 7 else pltpu.roll(v[0][y_low], 7, 0)
                    fz = face_z[at] * (above - here)
                    fy_old = fy[y_low - 1] if y_low else pltpu.roll(fy[YL - 1], 1, 1)
                    gain = (fx - flux[behind, y_low, tile(j), :]) + (fy[y_low] - fy_old)
                    gain = gain + (fz - z_old[y_low])
                    z_old[y_low] = fz
                    left = resid[at] + (gain - extra[at] * here)
                    resid[at] = left
                    sol[at] = sol[at] + here
                    dirs[nxt, x_low, y_low, tile(j), :] = keep * here + new * left
        return 0

    lax.fori_loop(0, SWEEPS - 1, sweep, 0)
    last = (SWEEPS - 1) % 2

    row = lax.broadcasted_iota(jnp.int32, (YL * 128, 256), 0)
    col = lax.broadcasted_iota(jnp.int32, (YL * 128, 256), 1)
    put = jnp.where(
        (row % 128 // 32 == col // HALF)
        & (YL * (row % 32) + row // 128 == col % HALF + RIM),
        1.0,
        0.0,
    ).astype(BF16)
    for odd in range(2):
        wide = []
        for x_low in range(4 * odd, 4 * odd + 4):
            field = jnp.concatenate(
                [
                    cond[x_low, y_low] * (sol[x_low, y_low] + dirs[last, x_low, y_low])
                    for y_low in range(YL)
                ], axis=1
            )
            first = field.astype(BF16)
            second = (field - first.astype(F32)).astype(BF16)
            wide.append(
                jnp.dot(first, put, preferred_element_type=F32)
                + jnp.dot(second, put, preferred_element_type=F32)
            )
        for h in range(4):
            lanes = slice(128 * (h // 2), 128 * (h // 2) + 128)
            for n in range(2):
                a, b = wide[n][:, lanes], wide[n + 2][:, lanes]
                if h % 2 == 0:
                    both = jnp.where(left_half, a, pltpu.roll(b, 64, 1))
                else:
                    both = jnp.where(left_half, pltpu.roll(a, 64, 1), b)
                for j in range(8):
                    sens[2 * h + odd, pl.ds(NZ * n + j, 8, stride=8), :] = both[tile(j)]


    seven = pl.ds(0, N_GX - 1)
    for ref, sems in ((zone_in, zone_sem), (draw_in, draw_sem)):
        pltpu.make_async_copy(ref.at[seven], ref.at[seven], sems.at[1]).wait()
        pltpu.make_async_copy(ref.at[seven], ref.at[seven], sems.at[0]).wait()

    inner = lax.broadcasted_iota(jnp.int32, (256, 128), 0).astype(F32).astype(BF16)
    one, nil = jnp.ones((), BF16), jnp.zeros((), BF16)

    def spread(row, times):
        return jnp.concatenate([jnp.broadcast_to(row, (16, 128)).astype(BF16)] * times, axis=0)

    per = 2 * NZ // STEP

    def build(i, left, right):
        o, at = i // per, pl.ds(pl.multiple_of(i % per * STEP, STEP), STEP)
        zone = zone_in[o, at, :]
        value = sens[o, at, :] * draw_in[o, at, :].astype(F32)
        outer = ((zone + 0.5) * (1.0 / INNER)).astype(jnp.int32).astype(F32)
        place = zone - outer * INNER
        for r in range(STEP):
            row = slice(r, r + 1)
            cols = slice(128 * r, 128 * r + 128)
            right[:, cols] = jnp.where(inner == spread(outer[row], 16), spread(value[row], 16), nil)
            left[0:256, cols] = jnp.where(inner == spread(place[row], 16), one, nil)
            left[256:INNER, cols] = jnp.where(
                inner[0 : INNER - 256] == spread(place[row] - 256.0, (INNER - 256) // 16), one, nil
            )

    def add(left, right):
        for n in range(2):
            cols = slice(64 * STEP * n, 64 * STEP * n + 64 * STEP)
            acc[n] += lax.dot_general(
                left[:, cols], right[:, cols], NT, preferred_element_type=F32
            )

    steps = N_GX * per
    acc[...] = jnp.zeros_like(acc)
    build(0, left_a, right_a)

    def two(i, _):
        build(2 * i + 1, left_b, right_b)
        add(left_a, right_a)
        build(jnp.minimum(2 * i + 2, steps - 1), left_a, right_a)
        add(left_b, right_b)
        return 0

    lax.fori_loop(0, steps // 2, two, 0)

    turned = (acc[0] + acc[1]).T
    for dev in range(DEVICES):
        send_a[dev % N_GY, dev // N_GY] = turned[2 * dev : 2 * dev + 2, :]

    def row_copy(k):
        dev = lax.rem(gy + k, N_GY)
        return pltpu.make_async_remote_copy(
            src_ref=send_a.at[dev],
            dst_ref=recv_a.at[gy],
            send_sem=a_sem.at[0],
            recv_sem=a_sem.at[1],
            device_id=(gx, dev),
            device_id_type=MESH,
        )

    for k in range(1, N_GY):
        row_copy(k).start()
    recv_a[gy] = send_a[gy]
    rest = pl.ds(0, N_GY - 1)
    pltpu.make_async_copy(recv_a.at[rest], recv_a.at[rest], a_sem.at[1]).wait()
    for o in range(N_GX):
        total = recv_a[0, o]
        for n in range(1, N_GY):
            total = total + recv_a[n, o]
        send_b[o] = total
    for k in range(1, N_GX):
        to_column(k, lambda dev: send_b.at[dev], recv_b.at[gx], b_sem).start()
    recv_b[gx] = send_b[gx]
    pltpu.make_async_copy(recv_b.at[seven], recv_b.at[seven], b_sem.at[1]).wait()
    for t in range(TESTS):
        total = (recv_b[t] + recv_b[TESTS + t]).astype(BF16).astype(F32)
        for n in range(2):
            mine[t : t + 1, INNER * n : INNER * n + INNER] = total[n : n + 1]

    def put_out(n, dev, place):
        return pltpu.make_async_remote_copy(
            src_ref=mine,
            dst_ref=out_ref.at[place, member],
            send_sem=put_sem.at[n],
            recv_sem=got_sem.at[place, member],
            device_id=dev,
            device_id_type=MESH,
        )

    for n, (dev, place) in enumerate(takers):
        taker_is_me = dev[0] * N_GY + dev[1] == me

        @pl.when(jnp.logical_not(taker_is_me))
        def _():
            put_out(n, dev, place).start()

        @pl.when(taker_is_me)
        def _():
            out_ref[place, member] = mine[...]

    pltpu.make_async_copy(send_a.at[rest], send_a.at[rest], a_sem.at[0]).wait()
    pltpu.make_async_copy(send_b.at[seven], send_b.at[seven], b_sem.at[0]).wait()
    for place, held in ((0, low_group), (1, high_group)):
        for m in range(MEMBERS):

            @pl.when(held * MEMBERS + m != me)
            def _():
                pltpu.make_async_copy(
                    out_ref.at[place, m], out_ref.at[place, m], got_sem.at[place, m]
                ).wait()

    for n, (dev, place) in enumerate(takers):

        @pl.when(dev[0] * N_GY + dev[1] != me)
        def _():
            put_out(n, dev, place).wait_send()


def main_call(cond, source, zone, drawdown):
    width = STEP * 128
    return pl.pallas_call(
        main_kernel,
        out_shape=jax.ShapeDtypeStruct((2, MEMBERS, TESTS, SHARE), F32),
        in_specs=[VMEM] * 4,
        out_specs=VMEM,
        scratch_shapes=[
            pltpu.VMEM(FIELD, F32),
            pltpu.VMEM(FIELD, F32),
            pltpu.VMEM(FIELD, F32),
            pltpu.VMEM(FIELD, F32),
            pltpu.VMEM((2,) + FIELD, F32),
            pltpu.VMEM(FIELD, F32),
            pltpu.VMEM(FIELD, F32),
            pltpu.VMEM((XL + 1, YL, NZ, 128), F32),
            pltpu.VMEM((2, 2 * NZ, 128), F32),
            pltpu.VMEM((N_GX, 2 * NZ, 128), BF16),
            pltpu.VMEM((N_GX, 2 * NZ, 128), F32),
            pltpu.VMEM((N_GX, 2 * NZ, 128), BF16),
            pltpu.VMEM((N_GX, 2 * NZ, 128), F32),
            pltpu.VMEM((INNER, width), BF16),
            pltpu.VMEM((256, width), BF16),
            pltpu.VMEM((INNER, width), BF16),
            pltpu.VMEM((256, width), BF16),
            pltpu.VMEM((2, INNER, 256), F32),
            pltpu.VMEM((N_GY, N_GX, 2, INNER), F32),
            pltpu.VMEM((N_GY, N_GX, 2, INNER), F32),
            pltpu.VMEM((N_GX, 2, INNER), F32),
            pltpu.VMEM((N_GX, 2, INNER), F32),
            pltpu.VMEM((TESTS, SHARE), F32),
            pltpu.SemaphoreType.DMA((2,)),
            pltpu.SemaphoreType.DMA((2,)),
            pltpu.SemaphoreType.DMA((2,)),
            pltpu.SemaphoreType.DMA((2,)),
            pltpu.SemaphoreType.DMA((2, MEMBERS)),
            pltpu.SemaphoreType.DMA((16,)),
        ],
        compiler_params=pltpu.CompilerParams(
            collective_id=1, has_side_effects=True, vmem_limit_bytes=48 * MIB
        ),
    )(cond, source, zone, drawdown)


ROWS, COLS, STRIP = 1024, 512, 256
TERMS = 128


def pieces(value):
    out = []
    for _ in range(3):
        piece = value.astype(BF16).astype(F32)
        out.append(piece)
        value = value - piece
    return out


def terms(pts, as_rows):
    sub = lax.broadcasted_iota(jnp.int32, pts.shape, 0)
    norm = pieces(jnp.broadcast_to(jnp.sum(pts * pts, axis=0, keepdims=True), pts.shape))
    parts = pieces(pts)
    first = 0 if as_rows else 3
    rest = jnp.where((sub < 6) & ((sub >= 3) if as_rows else (sub < 3)), 1.0, 0.0)
    for n in range(3):
        rest = jnp.where(sub == first + n, norm[n], rest)
    blocks = [
        -2.0 * parts[i] if as_rows else parts[j] for i in range(3) for j in range(3)
    ]
    return jnp.concatenate(blocks + [rest], axis=0)


def cov_kernel(
    diag_ref, pts_ref, sums_ref, out_ref, z_ref, z_turned, row_terms, col_terms, near, total, ta, tb
):
    diag = diag_ref[0]
    out_ref[...] = jnp.zeros_like(out_ref)
    for g in range(2):
        for m in range(MEMBERS):
            both = jnp.concatenate([sums_ref[g, m], jnp.zeros((TESTS, SHARE), F32)], axis=0)
            z_ref[g, :, SHARE * m : SHARE * m + SHARE] = both.astype(BF16)

    def phase(rg, _):
        cg = jnp.where(diag == 1, rg, 1)
        for i in range(GROUP // ROWS):
            at = slice(ROWS * i, ROWS * i + ROWS)
            row_terms[0:80, at] = terms(pts_ref[rg, :, at], True)
            row_terms[80:TERMS, at] = jnp.zeros((TERMS - 80, ROWS), F32)
            col_terms[0:80, at] = terms(pts_ref[cg, :, at], False).astype(BF16)
            col_terms[80:TERMS, at] = jnp.zeros((TERMS - 80, ROWS), BF16)
            wide = jnp.concatenate(
                [z_ref[cg, :, at].astype(F32), jnp.zeros((120, ROWS), F32)], axis=0
            )
            z_turned[at, :] = wide.T.astype(BF16)

        def row_block(r, _):
            rs = pl.ds(pl.multiple_of(r * ROWS, ROWS), ROWS)
            near[...] = row_terms[:, rs].T.astype(BF16)
            total[...] = jnp.zeros_like(total)
            z_row = z_ref[rg, :, rs]

            def at_cols(c):
                return pl.ds(pl.multiple_of(c * COLS, COLS), COLS)

            def tile(c, out):
                cols = col_terms[:, at_cols(c)]
                for i in range(ROWS // STRIP):
                    at = slice(STRIP * i, STRIP * i + STRIP)
                    squared = jnp.dot(near[at, :], cols, preferred_element_type=F32)
                    squared = jnp.maximum(squared, 1e-30)
                    out[at, :] = jnp.exp2(squared * (-lax.rsqrt(squared))).astype(BF16)

            def for_rows(c, held):
                total[...] += jnp.dot(
                    held[...], z_turned[at_cols(c), :], preferred_element_type=F32
                )

            def both_ways(c, held):
                out_ref[cg, :, at_cols(c)] += jnp.dot(
                    z_row, held[...], preferred_element_type=F32
                )
                for_rows(c, held)

            last = GROUP // COLS // 2 - 1
            first = jnp.where(diag == 1, r + 1, 0)

            @pl.when(diag == 1)
            def _():
                tile(2 * r, ta)
                tile(2 * r + 1, tb)
                for_rows(2 * r, ta)
                for_rows(2 * r + 1, tb)

            @pl.when(first <= last)
            def _():
                tile(2 * first, ta)

                def two(p, _):
                    tile(2 * p + 1, tb)
                    both_ways(2 * p, ta)
                    tile(2 * p + 2, ta)
                    both_ways(2 * p + 1, tb)
                    return 0

                lax.fori_loop(first, last, two, 0)
                tile(2 * last + 1, tb)
                both_ways(2 * last, ta)
                both_ways(2 * last + 1, tb)

            out_ref[rg, :, rs] += total[...].T[0:8]
            return 0

        lax.fori_loop(0, GROUP // ROWS, row_block, 0)
        return 0

    lax.fori_loop(0, 1 + diag, phase, 0)


def cov_call(diag, pts, sums):
    return pl.pallas_call(
        cov_kernel,
        out_shape=jax.ShapeDtypeStruct((2, 8, GROUP), F32),
        in_specs=[pl.BlockSpec(memory_space=pltpu.SMEM), VMEM, VMEM],
        out_specs=VMEM,
        scratch_shapes=[
            pltpu.VMEM((2, 8, GROUP), BF16),
            pltpu.VMEM((GROUP, 128), BF16),
            pltpu.VMEM((TERMS, GROUP), F32),
            pltpu.VMEM((TERMS, GROUP), BF16),
            pltpu.VMEM((ROWS, TERMS), BF16),
            pltpu.VMEM((ROWS, 128), F32),
            pltpu.VMEM((ROWS, COLS), BF16),
            pltpu.VMEM((ROWS, COLS), BF16),
        ],
        compiler_params=pltpu.CompilerParams(vmem_limit_bytes=48 * MIB),
    )(diag, pts, sums)


def reduce_kernel(part_ref, out_ref, send, recv, send_sem, recv_sem):
    me = my_index()
    gx, gy = lax.axis_index("gx"), lax.axis_index("gy")
    low, high, diag = groups_of(gx, gy)
    group, member = me // MEMBERS, me % MEMBERS
    for g in range(2):
        for m in range(MEMBERS):
            send[g, m] = part_ref[g, 0:TESTS, SHARE * m : SHARE * m + SHARE]

    takers = takers_of(group)
    barrier = pltpu.get_barrier_semaphore()
    for place, held in ((0, low), (1, high)):
        for m in range(MEMBERS):
            owner = held * MEMBERS + m

            @pl.when(owner != me)
            def _():
                pl.semaphore_signal(barrier, inc=1, device_id=coords(owner), device_id_type=MESH)

    for dev, _ in takers:

        @pl.when(dev[0] * N_GY + dev[1] != me)
        def _():
            pl.semaphore_signal(barrier, inc=1, device_id=dev, device_id_type=MESH)

    self_here = (low == group) | (high == group)
    pl.semaphore_wait(barrier, 32 - 2 * self_here.astype(jnp.int32))

    def put(place, m, held, slot):
        return pltpu.make_async_remote_copy(
            src_ref=send.at[place, m],
            dst_ref=recv.at[slot],
            send_sem=send_sem.at[place, m],
            recv_sem=recv_sem.at[slot],
            device_id=coords(held * MEMBERS + m),
            device_id_type=MESH,
        )

    sides = (
        (0, low, jnp.where(diag, low, high)),
        (1, high, jnp.where(diag, high, low)),
    )
    for place, held, slot in sides:
        for m in range(MEMBERS):

            @pl.when(held * MEMBERS + m != me)
            def _():
                put(place, m, held, slot).start()

            @pl.when(held * MEMBERS + m == me)
            def _():
                recv[slot] = send[place, m]

    own_slot = jnp.where(
        low == group, jnp.where(diag, low, high), jnp.where(diag, high, low)
    )
    for slot in range(GROUPS):

        @pl.when(jnp.logical_not(self_here & (own_slot == slot)))
        def _():
            pltpu.make_async_copy(recv.at[slot], recv.at[slot], recv_sem.at[slot]).wait()

    total = recv[0]
    for slot in range(1, GROUPS):
        total = total + recv[slot]
    out_ref[...] = total.astype(BF16)
    for place, held, slot in sides:
        for m in range(MEMBERS):

            @pl.when(held * MEMBERS + m != me)
            def _():
                put(place, m, held, slot).wait_send()


def reduce_call(parts):
    return pl.pallas_call(
        reduce_kernel,
        out_shape=jax.ShapeDtypeStruct((TESTS, SHARE), BF16),
        in_specs=[VMEM],
        out_specs=VMEM,
        scratch_shapes=[
            pltpu.VMEM((2, MEMBERS, TESTS, SHARE), F32),
            pltpu.VMEM((GROUPS, TESTS, SHARE), F32),
            pltpu.SemaphoreType.DMA((2, MEMBERS)),
            pltpu.SemaphoreType.DMA((GROUPS,)),
        ],
        compiler_params=pltpu.CompilerParams(
            collective_id=2, has_side_effects=True, vmem_limit_bytes=32 * MIB
        ),
    )(parts)


def per_device(
    well_cell, well_test, well_value, cond_class, class_value, zone_id, drawdown, centroid
):
    gx, gy = lax.axis_index("gx"), lax.axis_index("gy")
    low, high, diag = groups_of(gx, gy)
    pts = jnp.stack(
        [lax.dynamic_slice_in_dim(centroid, held * GROUP, GROUP, 1) for held in (low, high)]
    )
    pts = jnp.pad((pts - 0.5) * (LOG2E / corr_len), ((0, 0), (0, 5), (0, 0)))
    wells, classes, edges = share_call(
        well_cell[None], well_test[None], well_value[None], cond_class
    )
    cond, source = source_call(wells, classes, edges, class_value)
    rows = CX * NZ
    sums = main_call(
        cond, source, zone_id.reshape(rows, CY), drawdown.reshape(TESTS, rows, CY)
    )
    parts = cov_call(diag.astype(jnp.int32)[None], pts, sums)
    return reduce_call(parts)


def solution(mesh):
    return jax.shard_map(
        per_device,
        mesh=mesh,
        in_specs=(
            P(("gx", "gy")),
            P(("gx", "gy")),
            P(("gx", "gy")),
            P("gx", None, "gy"),
            P(),
            P("gx", None, "gy"),
            P(None, "gx", None, "gy"),
            P(),
        ),
        out_specs=P(None, ("gx", "gy")),
        check_vma=False,
    )
```

```python
import functools

import jax
import jax.numpy as jnp
from jax import lax
from jax.experimental import pallas as pl
from jax.experimental.pallas import tpu as pltpu
from jax.sharding import PartitionSpec as P

MESH = pl.DeviceIdType.MESH
NT = (((1,), (1,)), ((), ()))
VMEM = pl.BlockSpec(memory_space=pltpu.VMEM)
F32 = jnp.float32
BF16 = jnp.bfloat16
MIB = 2**20

SWEEPS = 12
TESTS = 4
CX, NZ, CY = 4, 64, 128
N_GX, N_GY = 8, 16
DEVICES = N_GX * N_GY
NCLASS = 16
CAP = 16
ZONES = 98304
SHARE = ZONES // DEVICES
GROUPS = 16
MEMBERS = DEVICES // GROUPS
GROUP = ZONES // GROUPS
HALF = CY // 2
RIM = 16
XL, YL = 8, 3
HIGHS = 4 * YL * NZ
SLOTS = 16 * CAP

storage = 0.02
lam_low = 0.02
lam_high = 36.02
corr_len = 0.1
LOG2E = 1.4426950408889634


def cheb_setup():
    middle = 0.5 * (lam_high + lam_low)
    spread = 0.5 * (lam_high - lam_low)
    ratio_mid = middle / spread
    current = 1.0 / ratio_mid
    factors = []
    for counter in range(SWEEPS - 1):
        updated = 1.0 / (2.0 * ratio_mid - current)
        factors.append((updated * current, 2.0 * updated / spread))
        current = updated
    return (middle, factors)


def my_index():
    return lax.axis_index("gx") * N_GY + lax.axis_index("gy")


def coords(dev):
    return (dev // N_GY, dev % N_GY)


def greet(devs):
    barrier = pltpu.get_barrier_semaphore()
    for dev in devs:
        pl.semaphore_signal(barrier, inc=1, device_id=dev, device_id_type=MESH)
    pl.semaphore_wait(barrier, len(devs))


def greet_all(me):
    barrier = pltpu.get_barrier_semaphore()

    def each(k, _):
        dev = lax.rem(me + k, DEVICES)
        pl.semaphore_signal(barrier, inc=1, device_id=coords(dev), device_id_type=MESH)
        return 0

    lax.fori_loop(1, DEVICES, each, 0)
    pl.semaphore_wait(barrier, DEVICES - 1)


def send_to_all(me, send, recv, send_sem, recv_sem):
    def each(k, _):
        dev = lax.rem(me + k, DEVICES)
        pltpu.make_async_remote_copy(
            src_ref=send.at[dev],
            dst_ref=recv.at[me],
            send_sem=send_sem,
            recv_sem=recv_sem,
            device_id=coords(dev),
            device_id_type=MESH,
        ).start()
        return 0

    lax.fori_loop(1, DEVICES, each, 0)
    recv[me] = send[me]
    rest = pl.ds(0, DEVICES - 1)
    pltpu.make_async_copy(recv.at[rest], recv.at[rest], recv_sem).wait()
    pltpu.make_async_copy(send.at[rest], send.at[rest], send_sem).wait()


def share_kernel(
    cell_ref,
    test_ref,
    value_ref,
    class_ref,
    wells_ref,
    cls_ref,
    edge_ref,
    rows,
    send,
    mine,
    edges,
    wells_sem,
    cls_sem,
    edge_sem,
):
    me = my_index()
    gx, gy = lax.axis_index("gx"), lax.axis_index("gy")
    lane = lax.broadcasted_iota(jnp.int32, (32, 128), 1)
    classes = class_ref[...].reshape(CX * NZ, CY).astype(F32)
    mine[...] = classes.astype(BF16)
    for side, first in ((0, 0), (1, CY - RIM)):
        pack = jnp.zeros((32, 128), F32)
        for g in range(8):
            here = (lane >= RIM * g) & (lane < RIM * g + RIM)
            pack = jnp.where(here, roll_to(classes[32 * g : 32 * g + 32], RIM * g - first), pack)
        edges[side] = pack.astype(BF16)
    edge_ref[...] = jnp.zeros_like(edge_ref)

    cell, test, value = cell_ref[...], test_ref[...], value_ref[...]
    n_rows = 2 * cell.shape[1]
    y = cell % (CY * N_GY)
    z = cell // (CY * N_GY) % NZ
    x = cell // (CY * N_GY * NZ)
    block = y // HALF
    within = y % HALF
    step = jnp.where(within < RIM, -1, jnp.where(within >= HALF - RIM, 1, 0))
    other = block + step
    valid = (step != 0) & (other >= 0) & (other < 2 * N_GY)

    def twice(first, second):
        return jnp.concatenate([first, second], axis=1)

    block, y, z, x = twice(block, other), twice(y, y), twice(z, z), twice(x, x)
    test, value = twice(test, test), twice(value, value)
    owner = (block % 2 * 4 + test) * N_GY + block // 2
    owner = twice(owner[:, : n_rows // 2], jnp.where(valid, owner[:, n_rows // 2 :], -1))
    y_loc = y - (block * HALF - RIM)
    x_low = x % XL
    high = ((x_low % 4 * YL + y_loc % YL) * 8 + z % 8) * 8 + z // 8
    low = x_low // 4 * 128 + x // XL * 32 + y_loc // YL
    code = (high * 256 + low).astype(F32)
    hot = jnp.where(
        lax.broadcasted_iota(jnp.int32, (DEVICES, n_rows), 0) == owner, 1.0, 0.0
    )
    earlier = jnp.where(
        lax.broadcasted_iota(jnp.int32, (n_rows, n_rows), 0)
        < lax.broadcasted_iota(jnp.int32, (n_rows, n_rows), 1),
        1.0,
        0.0,
    )
    hot16 = hot.astype(BF16)
    count = jnp.dot(hot16, earlier.astype(BF16), preferred_element_type=F32)
    rank = jnp.sum(hot * count, axis=0, keepdims=True).astype(jnp.int32)
    slot = lax.broadcasted_iota(jnp.int32, (SLOTS, n_rows), 0)
    part = jnp.concatenate(
        [jnp.where(slot == rank, code, 0.0), jnp.where(slot == rank, value, 0.0)], axis=0
    )
    total = None
    for _ in range(3):
        piece = part.astype(BF16)
        part = part - piece.astype(F32)
        term = lax.dot_general(hot16, piece, NT, preferred_element_type=F32)
        total = term if total is None else total + term
    for k in range(4):
        rows[k] = total[:, 128 * k : 128 * k + 128]
    for dev in range(DEVICES):
        for k in range(4):
            send[dev, k : k + 1, :] = rows[k, dev : dev + 1, :]

    greet_all(me)

    def cls_copy(k):
        return pltpu.make_async_remote_copy(
            src_ref=mine,
            dst_ref=cls_ref.at[gx],
            send_sem=cls_sem.at[0],
            recv_sem=cls_sem.at[1],
            device_id=(lax.rem(gx + k, N_GX), gy),
            device_id_type=MESH,
        )

    for k in range(1, N_GX):
        cls_copy(k).start()

    def edge_copy(side, k):
        return pltpu.make_async_remote_copy(
            src_ref=edges.at[side],
            dst_ref=edge_ref.at[gx],
            send_sem=edge_sem.at[side],
            recv_sem=edge_sem.at[2],
            device_id=(k + 4 * (1 - side), lax.rem(gy + N_GY - 1 + 2 * side, N_GY)),
            device_id_type=MESH,
        )

    @pl.when(gy > 0)
    def _():
        for k in range(4):
            edge_copy(0, k).start()

    @pl.when(gy < N_GY - 1)
    def _():
        for k in range(4):
            edge_copy(1, k).start()

    cls_ref[gx] = mine[...]
    send_to_all(me, send, wells_ref, wells_sem.at[0], wells_sem.at[1])
    seven = pl.ds(0, N_GX - 1)
    pltpu.make_async_copy(cls_ref.at[seven], cls_ref.at[seven], cls_sem.at[1]).wait()
    pltpu.make_async_copy(cls_ref.at[seven], cls_ref.at[seven], cls_sem.at[0]).wait()
    four = pl.ds(0, 4)

    @pl.when(gy > 0)
    def _():
        pltpu.make_async_copy(edge_ref.at[four], edge_ref.at[four], edge_sem.at[0]).wait()

    @pl.when(gy < N_GY - 1)
    def _():
        pltpu.make_async_copy(edge_ref.at[four], edge_ref.at[four], edge_sem.at[1]).wait()

    upper = gx >= 4

    @pl.when((upper & (gy < N_GY - 1)) | (jnp.logical_not(upper) & (gy > 0)))
    def _():
        pltpu.make_async_copy(edge_ref, edge_ref, edge_sem.at[2]).wait()


def share_call(cell, test, value, classes):
    return pl.pallas_call(
        share_kernel,
        out_shape=(
            jax.ShapeDtypeStruct((DEVICES, 4, 128), F32),
            jax.ShapeDtypeStruct((N_GX, CX * NZ, CY), BF16),
            jax.ShapeDtypeStruct((N_GX, 32, 128), BF16),
        ),
        in_specs=[VMEM] * 4,
        out_specs=(VMEM,) * 3,
        scratch_shapes=[
            pltpu.VMEM((4, DEVICES, 128), F32),
            pltpu.VMEM((DEVICES, 4, 128), F32),
            pltpu.VMEM((CX * NZ, CY), BF16),
            pltpu.VMEM((2, 32, 128), BF16),
            pltpu.SemaphoreType.DMA((2,)),
            pltpu.SemaphoreType.DMA((2,)),
            pltpu.SemaphoreType.DMA((3,)),
        ],
        compiler_params=pltpu.CompilerParams(
            collective_id=0, has_side_effects=True, vmem_limit_bytes=48 * MIB
        ),
    )(cell, test, value, classes)


def roll_to(value, shift):
    shift = shift % 128
    return pltpu.roll(value, shift, 1) if shift else value


def tile(j):
    return slice(8 * j, 8 * j + 8)


def source_kernel(
    wells_ref, cls_ref, edge_ref, class_value_ref, cond, src_ref, rows, plane, acc
):
    half = lax.axis_index("gx") // 4

    from_lane = lax.broadcasted_iota(jnp.int32, (128, 128), 0)
    to_lane = lax.broadcasted_iota(jnp.int32, (128, 128), 1)
    local = (from_lane + jnp.where(half == 0, RIM, HALF + RIM)) % 128
    picks = [
        jnp.where(local == YL * (to_lane % 32) + low, 1.0, 0.0).astype(BF16) for low in range(YL)
    ]
    lane32 = lax.broadcasted_iota(jnp.int32, (32, 128), 1)
    rim_at = jnp.where(half == 0, CY - RIM, 0)
    in_rim = (lane32 >= rim_at) & (lane32 < rim_at + RIM)
    group64 = lax.broadcasted_iota(jnp.int32, (NZ, 128), 1) // 32

    def whole(x):
        o = x // CX
        own = cls_ref[o, NZ * (x % CX) : NZ * (x % CX) + NZ, :].astype(F32)
        side = edge_ref[o].astype(F32)
        parts = []
        for g in (2 * (x % CX), 2 * (x % CX) + 1):
            moved = pltpu.roll(side, lax.rem(rim_at + 128 - RIM * g, 128), 1)
            parts.append(jnp.where(in_rim, moved, own[32 * (g % 2) : 32 * (g % 2) + 32]))
        return jnp.concatenate(parts, axis=0).astype(BF16)

    for x_low in range(XL):
        blocks = jnp.concatenate([whole(XL * h + x_low) for h in range(4)], axis=0)
        for y_low in range(YL):
            moved = jnp.dot(blocks, picks[y_low], preferred_element_type=F32)
            merged = moved[0:NZ]
            for h in range(1, 4):
                merged = jnp.where(group64 == h, moved[NZ * h : NZ * h + NZ], merged)
            value = jnp.zeros((NZ, 128), F32)
            for k in range(NCLASS):
                value = jnp.where(merged == float(k), class_value_ref[k], value)
            plane[...] = value
            for j in range(8):
                cond[x_low, y_low, tile(j), :] = plane[pl.ds(j, 8, stride=8), :]

    for dev in range(DEVICES):
        for k in range(4):
            rows[k, dev : dev + 1, :] = wells_ref[dev, k : k + 1, :]
    lane16 = lax.broadcasted_iota(jnp.int32, (16, 128), 1)
    row_high = lax.broadcasted_iota(jnp.int32, (HIGHS, 128), 0)
    row_low = lax.broadcasted_iota(jnp.int32, (256, 128), 0)
    acc[...] = jnp.zeros_like(acc)

    def level(n, _):
        row, at = n // 8, n % 8 * CAP
        codes = jnp.zeros((16, 128), F32)
        values = jnp.zeros((16, 128), F32)
        for g in range(8):
            here = lane16 // CAP == g
            turn = lax.rem(CAP * g + 128 - at, 128)
            block = rows[row, 16 * g : 16 * g + 16, :]
            codes = jnp.where(here, pltpu.roll(block, turn, 1), codes)
            block = rows[2 + row, 16 * g : 16 * g + 16, :]
            values = jnp.where(here, pltpu.roll(block, turn, 1), values)

        @pl.when(jnp.max(jnp.abs(values)) > 0.0)
        def _():
            whole_codes = codes.astype(jnp.int32)
            highs, lows = whole_codes // 256, whole_codes % 256
            first = values.astype(BF16).astype(F32)
            second = values - first
            left, right_a, right_b = [], [], []
            for r in range(16):
                left.append(jnp.where(row_high == highs[r : r + 1], 1.0, 0.0).astype(BF16))
                same = row_low == lows[r : r + 1]
                right_a.append(jnp.where(same, first[r : r + 1], 0.0).astype(BF16))
                right_b.append(jnp.where(same, second[r : r + 1], 0.0).astype(BF16))
            left = jnp.concatenate(left, axis=1)
            acc[...] += lax.dot_general(
                left, jnp.concatenate(right_a, axis=1), NT, preferred_element_type=F32
            ) + lax.dot_general(
                left, jnp.concatenate(right_b, axis=1), NT, preferred_element_type=F32
            )

        return 0

    lax.fori_loop(0, SLOTS // CAP, level, 0)

    for x_low in range(XL):
        for y_low in range(YL):
            at = NZ * (x_low % 4 * YL + y_low)
            src_ref[x_low, y_low] = acc[at : at + NZ, x_low // 4 * 128 : x_low // 4 * 128 + 128]


FIELD = (XL, YL, NZ, 128)


def source_call(wells, classes, edges, class_value):
    return pl.pallas_call(
        source_kernel,
        out_shape=(jax.ShapeDtypeStruct(FIELD, F32),) * 2,
        in_specs=[VMEM] * 3 + [pl.BlockSpec(memory_space=pltpu.SMEM)],
        out_specs=(VMEM,) * 2,
        scratch_shapes=[
            pltpu.VMEM((4, DEVICES, 128), F32),
            pltpu.VMEM((NZ, 128), F32),
            pltpu.VMEM((HIGHS, 256), F32),
        ],
        compiler_params=pltpu.CompilerParams(vmem_limit_bytes=48 * MIB),
    )(wells, classes, edges, class_value)


def groups_of(gx, gy):
    tail = gx == N_GX - 1
    low = jnp.where(tail, gy % 8, gy)
    high = jnp.where(tail, gy % 8 + 8, (gy + gx + 1) % GROUPS)
    return low, high, tail & (gy >= 8)


def takers_of(group):
    out = []
    for k in range(N_GX - 1):
        out.append(((k, group), 0))
        out.append(((k, (group + GROUPS - k - 1) % GROUPS), 1))
    place = group // 8
    out.append(((N_GX - 1, group % 8), place))
    out.append(((N_GX - 1, group % 8 + 8), place))
    return out


INNER = SHARE // 2


def main_kernel(
    cond,
    src_ref,
    zone_ref,
    draw_ref,
    out_ref,
    face_x,
    face_y,
    face_z,
    extra,
    dirs,
    resid,
    sol,
    flux,
    zone_out,
    draw_out,
    zone_in,
    draw_in,
    sens,
    acc,
    send_a,
    recv_a,
    send_b,
    recv_b,
    mine,
    zone_sem,
    draw_sem,
    a_sem,
    b_sem,
    got_sem,
    put_sem,
):
    me = my_index()
    gx, gy = lax.axis_index("gx"), lax.axis_index("gy")
    half = gx // 4
    lane = lax.broadcasted_iota(jnp.int32, (8, 128), 1)
    sub = lax.broadcasted_iota(jnp.int32, (8, 128), 0)
    x_high, y_high = lane // 32, lane % 32
    left_half = lax.broadcasted_iota(jnp.int32, (NZ, 128), 1) < HALF

    group, member = me // MEMBERS, me % MEMBERS
    low_group, high_group, _ = groups_of(gx, gy)
    takers = takers_of(group)
    barrier = pltpu.get_barrier_semaphore()
    for k in range(1, N_GX):
        pl.semaphore_signal(
            barrier, inc=1, device_id=(lax.rem(gx + k, N_GX), gy), device_id_type=MESH
        )
    for k in range(1, N_GY):
        pl.semaphore_signal(
            barrier, inc=1, device_id=(gx, lax.rem(gy + k, N_GY)), device_id_type=MESH
        )
    for held in (low_group, high_group):
        for m in range(MEMBERS):
            owner = held * MEMBERS + m

            @pl.when(owner != me)
            def _():
                pl.semaphore_signal(barrier, inc=1, device_id=coords(owner), device_id_type=MESH)

    for dev, _ in takers:

        @pl.when(dev[0] * N_GY + dev[1] != me)
        def _():
            pl.semaphore_signal(barrier, inc=1, device_id=dev, device_id_type=MESH)

    def packed(fields, side, n):
        a, b = fields[n], fields[n + 2]
        if side == 0:
            return jnp.where(left_half, a, pltpu.roll(b, HALF, 1))
        return jnp.where(left_half, pltpu.roll(a, HALF, 1), b)

    zones = [zone_ref[NZ * x : NZ * x + NZ, :].astype(F32) for x in range(CX)]
    for side in range(2):
        for n in range(2):
            zone_out[side, NZ * n : NZ * n + NZ, :] = packed(zones, side, n)
    for t in range(TESTS):
        draws = [draw_ref[t, NZ * x : NZ * x + NZ, :].astype(F32) for x in range(CX)]
        for side in range(2):
            for n in range(2):
                draw_out[TESTS * side + t, NZ * n : NZ * n + NZ, :] = packed(
                    draws, side, n
                ).astype(BF16)

    self_here = (low_group == group) | (high_group == group)
    pl.semaphore_wait(barrier, N_GX + N_GY - 2 + 32 - 2 * self_here.astype(jnp.int32))

    def to_column(k, src, dst, sems):
        dev = lax.rem(gx + k, N_GX)
        return pltpu.make_async_remote_copy(
            src_ref=src(dev),
            dst_ref=dst,
            send_sem=sems.at[0],
            recv_sem=sems.at[1],
            device_id=(dev, gy),
            device_id_type=MESH,
        )

    for k in range(1, N_GX):
        to_column(k, lambda dev: zone_out.at[dev // TESTS], zone_in.at[gx], zone_sem).start()
        to_column(k, lambda dev: draw_out.at[dev], draw_in.at[gx], draw_sem).start()
    zone_in[gx] = zone_out[half]
    draw_in[gx] = draw_out[gx]

    zero = jnp.zeros((8, 128), F32)
    first_y = jnp.where((gy == 0) & (half == 0), RIM, -1)
    last_y = jnp.where((gy == N_GY - 1) & (half == 1), RIM + HALF - 1, -2)

    def faces(x_low, _):
        for y_low in range(YL):
            y_loc = YL * y_high + y_low
            for j in range(8):
                c = cond[x_low, y_low, tile(j), :]
                more = jnp.full((8, 128), storage, F32)
                end = x_low == XL - 1
                near = cond[jnp.where(end, 0, x_low + 1), y_low, tile(j), :]
                near = jnp.where(end, pltpu.roll(near, 96, 1), near)
                off = end & (x_high == 3)
                face_x[x_low, y_low, tile(j), :] = jnp.where(off, zero, 0.5 * (c + near))
                more = more + jnp.where(off, 0.5 * c, zero)
                more = more + jnp.where((x_low == 0) & (x_high == 0), 0.5 * c, zero)
                if y_low < YL - 1:
                    near = cond[x_low, y_low + 1, tile(j), :]
                    off = y_loc + 1 == first_y
                else:
                    near = pltpu.roll(cond[x_low, 0, tile(j), :], 127, 1)
                    off = (y_loc + 1 == first_y) | (y_high == 31)
                off = off | (y_loc == last_y)
                face_y[x_low, y_low, tile(j), :] = jnp.where(off, zero, 0.5 * (c + near))
                more = more + jnp.where((y_loc == first_y) | (y_loc == last_y), 0.5 * c, zero)
                if j < 7:
                    face_z[x_low, y_low, tile(j), :] = 0.5 * (c + cond[x_low, y_low, tile(j + 1), :])
                else:
                    near = pltpu.roll(cond[x_low, y_low, tile(0), :], 7, 0)
                    face_z[x_low, y_low, tile(j), :] = jnp.where(sub == 7, zero, 0.5 * (c + near))
                    more = more + jnp.where(sub == 7, 0.5 * c, zero)
                if j == 0:
                    more = more + jnp.where(sub == 0, 0.5 * c, zero)
                extra[x_low, y_low, tile(j), :] = more
        return 0

    lax.fori_loop(0, XL, faces, 0)

    middle, factors = cheb_setup()
    for x_low in range(XL):
        for y_low in range(YL):
            value = src_ref[x_low, y_low]
            resid[x_low, y_low] = value
            dirs[0, x_low, y_low] = value / middle
            sol[x_low, y_low] = jnp.zeros((NZ, 128), F32)

    keeps = [pair[0] for pair in factors]
    news = [pair[1] for pair in factors]

    def sweep(k, _):
        par = lax.rem(k, 2)
        nxt = 1 - par
        keep, new = jnp.float32(keeps[0]), jnp.float32(news[0])
        for n in range(1, SWEEPS - 1):
            keep = jnp.where(k == n, jnp.float32(keeps[n]), keep)
            new = jnp.where(k == n, jnp.float32(news[n]), new)
        for y_low in range(YL):
            for j in range(8):
                over = face_x[XL - 1, y_low, tile(j), :] * (
                    pltpu.roll(dirs[par, 0, y_low, tile(j), :], 96, 1)
                    - dirs[par, XL - 1, y_low, tile(j), :]
                )
                flux[XL - 1, y_low, tile(j), :] = over
                flux[XL, y_low, tile(j), :] = pltpu.roll(over, 32, 1)
        for x_low in range(XL):
            behind = XL if x_low == 0 else x_low - 1
            v = [[dirs[par, x_low, y_low, tile(j), :] for y_low in range(YL)] for j in range(8)]
            z_old = []
            for y_low in range(YL):
                z_old.append(
                    pltpu.roll(
                        face_z[x_low, y_low, tile(7), :]
                        * (pltpu.roll(v[0][y_low], 7, 0) - v[7][y_low]),
                        1,
                        0,
                    )
                )
            for j in range(8):
                fy = [
                    face_y[x_low, y_low, tile(j), :]
                    * (
                        (v[j][y_low + 1] if y_low < YL - 1 else pltpu.roll(v[j][0], 127, 1))
                        - v[j][y_low]
                    )
                    for y_low in range(YL)
                ]
                for y_low in range(YL):
                    here = v[j][y_low]
                    at = (x_low, y_low, tile(j))
                    if x_low < XL - 1:
                        fx = face_x[at] * (dirs[par, x_low + 1, y_low, tile(j), :] - here)
                        flux[at] = fx
                    else:
                        fx = flux[at]
                    above = v[j + 1][y_low] if j < 7 else pltpu.roll(v[0][y_low], 7, 0)
                    fz = face_z[at] * (above - here)
                    fy_old = fy[y_low - 1] if y_low else pltpu.roll(fy[YL - 1], 1, 1)
                    gain = (fx - flux[behind, y_low, tile(j), :]) + (fy[y_low] - fy_old)
                    gain = gain + (fz - z_old[y_low])
                    z_old[y_low] = fz
                    left = resid[at] + (gain - extra[at] * here)
                    resid[at] = left
                    sol[at] = sol[at] + here
                    dirs[nxt, x_low, y_low, tile(j), :] = keep * here + new * left
        return 0

    lax.fori_loop(0, SWEEPS - 1, sweep, 0)
    last = (SWEEPS - 1) % 2

    row = lax.broadcasted_iota(jnp.int32, (YL * 128, 256), 0)
    col = lax.broadcasted_iota(jnp.int32, (YL * 128, 256), 1)
    put = jnp.where(
        (row % 128 // 32 == col // HALF)
        & (YL * (row % 32) + row // 128 == col % HALF + RIM),
        1.0,
        0.0,
    ).astype(BF16)
    for odd in range(2):
        wide = []
        for x_low in range(4 * odd, 4 * odd + 4):
            field = jnp.concatenate(
                [
                    cond[x_low, y_low] * (sol[x_low, y_low] + dirs[last, x_low, y_low])
                    for y_low in range(YL)
                ], axis=1
            )
            first = field.astype(BF16)
            second = (field - first.astype(F32)).astype(BF16)
            wide.append(
                jnp.dot(first, put, preferred_element_type=F32)
                + jnp.dot(second, put, preferred_element_type=F32)
            )
        for h in range(4):
            lanes = slice(128 * (h // 2), 128 * (h // 2) + 128)
            for n in range(2):
                a, b = wide[n][:, lanes], wide[n + 2][:, lanes]
                if h % 2 == 0:
                    both = jnp.where(left_half, a, pltpu.roll(b, 64, 1))
                else:
                    both = jnp.where(left_half, pltpu.roll(a, 64, 1), b)
                for j in range(8):
                    sens[2 * h + odd, pl.ds(NZ * n + j, 8, stride=8), :] = both[tile(j)]


    seven = pl.ds(0, N_GX - 1)
    for ref, sems in ((zone_in, zone_sem), (draw_in, draw_sem)):
        pltpu.make_async_copy(ref.at[seven], ref.at[seven], sems.at[1]).wait()
        pltpu.make_async_copy(ref.at[seven], ref.at[seven], sems.at[0]).wait()

    inner = lax.broadcasted_iota(jnp.int32, (256, 128), 0).astype(F32).astype(BF16)
    one, nil = jnp.ones((), BF16), jnp.zeros((), BF16)

    def spread(row, times):
        return jnp.concatenate([jnp.broadcast_to(row, (16, 128)).astype(BF16)] * times, axis=0)

    def step(o, _):
        zone = zone_in[o]
        value = sens[o] * draw_in[o].astype(F32)
        outer = ((zone + 0.5) * (1.0 / INNER)).astype(jnp.int32).astype(F32)
        place = zone - outer * INNER
        left, right = [], []
        for r in range(2 * NZ):
            row = slice(r, r + 1)
            right.append(jnp.where(inner == spread(outer[row], 16), spread(value[row], 16), nil))
            left.append(
                jnp.concatenate(
                    [
                        jnp.where(inner == spread(place[row], 16), one, nil),
                        jnp.where(
                            inner[0 : INNER - 256]
                            == spread(place[row] - 256.0, (INNER - 256) // 16),
                            one,
                            nil,
                        ),
                    ],
                    axis=0,
                )
            )
        acc[...] += lax.dot_general(
            jnp.concatenate(left, axis=1),
            jnp.concatenate(right, axis=1),
            NT,
            preferred_element_type=F32,
        )
        return 0

    acc[...] = jnp.zeros_like(acc)
    lax.fori_loop(0, N_GX, step, 0)

    turned = acc[...].T
    for dev in range(DEVICES):
        send_a[dev % N_GY, dev // N_GY] = turned[2 * dev : 2 * dev + 2, :]

    def row_copy(k):
        dev = lax.rem(gy + k, N_GY)
        return pltpu.make_async_remote_copy(
            src_ref=send_a.at[dev],
            dst_ref=recv_a.at[gy],
            send_sem=a_sem.at[0],
            recv_sem=a_sem.at[1],
            device_id=(gx, dev),
            device_id_type=MESH,
        )

    for k in range(1, N_GY):
        row_copy(k).start()
    recv_a[gy] = send_a[gy]
    rest = pl.ds(0, N_GY - 1)
    pltpu.make_async_copy(recv_a.at[rest], recv_a.at[rest], a_sem.at[1]).wait()
    for o in range(N_GX):
        total = recv_a[0, o]
        for n in range(1, N_GY):
            total = total + recv_a[n, o]
        send_b[o] = total
    for k in range(1, N_GX):
        to_column(k, lambda dev: send_b.at[dev], recv_b.at[gx], b_sem).start()
    recv_b[gx] = send_b[gx]
    pltpu.make_async_copy(recv_b.at[seven], recv_b.at[seven], b_sem.at[1]).wait()
    for t in range(TESTS):
        total = (recv_b[t] + recv_b[TESTS + t]).astype(BF16).astype(F32)
        for n in range(2):
            mine[t : t + 1, INNER * n : INNER * n + INNER] = total[n : n + 1]

    def put_out(n, dev, place):
        return pltpu.make_async_remote_copy(
            src_ref=mine,
            dst_ref=out_ref.at[place, member],
            send_sem=put_sem.at[n],
            recv_sem=got_sem.at[place, member],
            device_id=dev,
            device_id_type=MESH,
        )

    for n, (dev, place) in enumerate(takers):
        taker_is_me = dev[0] * N_GY + dev[1] == me

        @pl.when(jnp.logical_not(taker_is_me))
        def _():
            put_out(n, dev, place).start()

        @pl.when(taker_is_me)
        def _():
            out_ref[place, member] = mine[...]

    pltpu.make_async_copy(send_a.at[rest], send_a.at[rest], a_sem.at[0]).wait()
    pltpu.make_async_copy(send_b.at[seven], send_b.at[seven], b_sem.at[0]).wait()
    for place, held in ((0, low_group), (1, high_group)):
        for m in range(MEMBERS):

            @pl.when(held * MEMBERS + m != me)
            def _():
                pltpu.make_async_copy(
                    out_ref.at[place, m], out_ref.at[place, m], got_sem.at[place, m]
                ).wait()

    for n, (dev, place) in enumerate(takers):

        @pl.when(dev[0] * N_GY + dev[1] != me)
        def _():
            put_out(n, dev, place).wait_send()


def main_call(cond, source, zone, drawdown):
    return pl.pallas_call(
        main_kernel,
        out_shape=jax.ShapeDtypeStruct((2, MEMBERS, TESTS, SHARE), F32),
        in_specs=[VMEM] * 4,
        out_specs=VMEM,
        scratch_shapes=[
            pltpu.VMEM(FIELD, F32),
            pltpu.VMEM(FIELD, F32),
            pltpu.VMEM(FIELD, F32),
            pltpu.VMEM(FIELD, F32),
            pltpu.VMEM((2,) + FIELD, F32),
            pltpu.VMEM(FIELD, F32),
            pltpu.VMEM(FIELD, F32),
            pltpu.VMEM((XL + 1, YL, NZ, 128), F32),
            pltpu.VMEM((2, 2 * NZ, 128), F32),
            pltpu.VMEM((N_GX, 2 * NZ, 128), BF16),
            pltpu.VMEM((N_GX, 2 * NZ, 128), F32),
            pltpu.VMEM((N_GX, 2 * NZ, 128), BF16),
            pltpu.VMEM((N_GX, 2 * NZ, 128), F32),
            pltpu.VMEM((INNER, 256), F32),
            pltpu.VMEM((N_GY, N_GX, 2, INNER), F32),
            pltpu.VMEM((N_GY, N_GX, 2, INNER), F32),
            pltpu.VMEM((N_GX, 2, INNER), F32),
            pltpu.VMEM((N_GX, 2, INNER), F32),
            pltpu.VMEM((TESTS, SHARE), F32),
            pltpu.SemaphoreType.DMA((2,)),
            pltpu.SemaphoreType.DMA((2,)),
            pltpu.SemaphoreType.DMA((2,)),
            pltpu.SemaphoreType.DMA((2,)),
            pltpu.SemaphoreType.DMA((2, MEMBERS)),
            pltpu.SemaphoreType.DMA((16,)),
        ],
        compiler_params=pltpu.CompilerParams(
            collective_id=1, has_side_effects=True, vmem_limit_bytes=48 * MIB
        ),
    )(cond, source, zone, drawdown)


ROWS, COLS = 1024, 512
TERMS = 128


def pieces(value):
    out = []
    for _ in range(3):
        piece = value.astype(BF16).astype(F32)
        out.append(piece)
        value = value - piece
    return out


def terms(pts, as_rows):
    sub = lax.broadcasted_iota(jnp.int32, pts.shape, 0)
    norm = pieces(jnp.broadcast_to(jnp.sum(pts * pts, axis=0, keepdims=True), pts.shape))
    parts = pieces(pts)
    first = 0 if as_rows else 3
    rest = jnp.where((sub < 6) & ((sub >= 3) if as_rows else (sub < 3)), 1.0, 0.0)
    for n in range(3):
        rest = jnp.where(sub == first + n, norm[n], rest)
    blocks = [
        -2.0 * parts[i] if as_rows else parts[j] for i in range(3) for j in range(3)
    ]
    return jnp.concatenate(blocks + [rest], axis=0)


def cov_kernel(
    diag_ref, pts_ref, sums_ref, out_ref, z_ref, z_turned, row_terms, col_terms, near, total
):
    diag = diag_ref[0]
    out_ref[...] = jnp.zeros_like(out_ref)
    for g in range(2):
        for m in range(MEMBERS):
            both = jnp.concatenate([sums_ref[g, m], jnp.zeros((TESTS, SHARE), F32)], axis=0)
            z_ref[g, :, SHARE * m : SHARE * m + SHARE] = both.astype(BF16)

    def phase(rg, _):
        cg = jnp.where(diag == 1, rg, 1)
        for i in range(GROUP // ROWS):
            at = slice(ROWS * i, ROWS * i + ROWS)
            row_terms[0:80, at] = terms(pts_ref[rg, :, at], True)
            row_terms[80:TERMS, at] = jnp.zeros((TERMS - 80, ROWS), F32)
            col_terms[0:80, at] = terms(pts_ref[cg, :, at], False).astype(BF16)
            col_terms[80:TERMS, at] = jnp.zeros((TERMS - 80, ROWS), BF16)
            wide = jnp.concatenate(
                [z_ref[cg, :, at].astype(F32), jnp.zeros((120, ROWS), F32)], axis=0
            )
            z_turned[at, :] = wide.T.astype(BF16)

        def row_block(r, _):
            rs = pl.ds(pl.multiple_of(r * ROWS, ROWS), ROWS)
            near[...] = row_terms[:, rs].T.astype(BF16)
            total[...] = jnp.zeros_like(total)
            z_row = z_ref[rg, :, rs]

            def at_cols(c):
                return pl.ds(pl.multiple_of(c * COLS, COLS), COLS)

            def tile(c, rows):
                squared = jnp.dot(
                    near[rows, :], col_terms[:, at_cols(c)], preferred_element_type=F32
                )
                squared = jnp.maximum(squared, 1e-30)
                return jnp.exp2(squared * (-lax.rsqrt(squared))).astype(BF16)

            def for_rows(c, rows, held):
                total[rows, :] += jnp.dot(
                    held, z_turned[at_cols(c), :], preferred_element_type=F32
                )

            def for_cols(c, weights, held):
                out_ref[cg, :, at_cols(c)] += jnp.dot(
                    weights, held, preferred_element_type=F32
                )

            every, lower = slice(0, ROWS), slice(COLS, ROWS)

            @pl.when(diag == 1)
            def _():
                held = tile(2 * r, every)
                for_rows(2 * r, every, held)
                for_cols(2 * r, z_row[:, COLS:], held[COLS:])
                for_rows(2 * r + 1, lower, tile(2 * r + 1, lower))

            def two(p, _):
                for c in (2 * p, 2 * p + 1):
                    held = tile(c, every)
                    for_rows(c, every, held)
                    for_cols(c, z_row, held)
                return 0

            lax.fori_loop(jnp.where(diag == 1, r + 1, 0), GROUP // ROWS, two, 0)
            out_ref[rg, :, rs] += total[...].T[0:8]
            return 0

        lax.fori_loop(0, GROUP // ROWS, row_block, 0)
        return 0

    lax.fori_loop(0, 1 + diag, phase, 0)


def cov_call(diag, pts, sums):
    return pl.pallas_call(
        cov_kernel,
        out_shape=jax.ShapeDtypeStruct((2, 8, GROUP), F32),
        in_specs=[pl.BlockSpec(memory_space=pltpu.SMEM), VMEM, VMEM],
        out_specs=VMEM,
        scratch_shapes=[
            pltpu.VMEM((2, 8, GROUP), BF16),
            pltpu.VMEM((GROUP, 128), BF16),
            pltpu.VMEM((TERMS, GROUP), F32),
            pltpu.VMEM((TERMS, GROUP), BF16),
            pltpu.VMEM((ROWS, TERMS), BF16),
            pltpu.VMEM((ROWS, 128), F32),
        ],
        compiler_params=pltpu.CompilerParams(vmem_limit_bytes=48 * MIB),
    )(diag, pts, sums)


def reduce_kernel(part_ref, out_ref, send, recv, send_sem, recv_sem):
    me = my_index()
    gx, gy = lax.axis_index("gx"), lax.axis_index("gy")
    low, high, diag = groups_of(gx, gy)
    group, member = me // MEMBERS, me % MEMBERS
    for g in range(2):
        for m in range(MEMBERS):
            send[g, m] = part_ref[g, 0:TESTS, SHARE * m : SHARE * m + SHARE]

    takers = takers_of(group)
    barrier = pltpu.get_barrier_semaphore()
    for place, held in ((0, low), (1, high)):
        for m in range(MEMBERS):
            owner = held * MEMBERS + m

            @pl.when(owner != me)
            def _():
                pl.semaphore_signal(barrier, inc=1, device_id=coords(owner), device_id_type=MESH)

    for dev, _ in takers:

        @pl.when(dev[0] * N_GY + dev[1] != me)
        def _():
            pl.semaphore_signal(barrier, inc=1, device_id=dev, device_id_type=MESH)

    self_here = (low == group) | (high == group)
    pl.semaphore_wait(barrier, 32 - 2 * self_here.astype(jnp.int32))

    def put(place, m, held, slot):
        return pltpu.make_async_remote_copy(
            src_ref=send.at[place, m],
            dst_ref=recv.at[slot],
            send_sem=send_sem.at[place, m],
            recv_sem=recv_sem.at[slot],
            device_id=coords(held * MEMBERS + m),
            device_id_type=MESH,
        )

    sides = (
        (0, low, jnp.where(diag, low, high)),
        (1, high, jnp.where(diag, high, low)),
    )
    for place, held, slot in sides:
        for m in range(MEMBERS):

            @pl.when(held * MEMBERS + m != me)
            def _():
                put(place, m, held, slot).start()

            @pl.when(held * MEMBERS + m == me)
            def _():
                recv[slot] = send[place, m]

    own_slot = jnp.where(
        low == group, jnp.where(diag, low, high), jnp.where(diag, high, low)
    )
    for slot in range(GROUPS):

        @pl.when(jnp.logical_not(self_here & (own_slot == slot)))
        def _():
            pltpu.make_async_copy(recv.at[slot], recv.at[slot], recv_sem.at[slot]).wait()

    total = recv[0]
    for slot in range(1, GROUPS):
        total = total + recv[slot]
    out_ref[...] = total.astype(BF16)
    for place, held, slot in sides:
        for m in range(MEMBERS):

            @pl.when(held * MEMBERS + m != me)
            def _():
                put(place, m, held, slot).wait_send()


def reduce_call(parts):
    return pl.pallas_call(
        reduce_kernel,
        out_shape=jax.ShapeDtypeStruct((TESTS, SHARE), BF16),
        in_specs=[VMEM],
        out_specs=VMEM,
        scratch_shapes=[
            pltpu.VMEM((2, MEMBERS, TESTS, SHARE), F32),
            pltpu.VMEM((GROUPS, TESTS, SHARE), F32),
            pltpu.SemaphoreType.DMA((2, MEMBERS)),
            pltpu.SemaphoreType.DMA((GROUPS,)),
        ],
        compiler_params=pltpu.CompilerParams(
            collective_id=2, has_side_effects=True, vmem_limit_bytes=32 * MIB
        ),
    )(parts)


def per_device(
    well_cell, well_test, well_value, cond_class, class_value, zone_id, drawdown, centroid
):
    gx, gy = lax.axis_index("gx"), lax.axis_index("gy")
    low, high, diag = groups_of(gx, gy)
    pts = jnp.stack(
        [lax.dynamic_slice_in_dim(centroid, held * GROUP, GROUP, 1) for held in (low, high)]
    )
    pts = jnp.pad((pts - 0.5) * (LOG2E / corr_len), ((0, 0), (0, 5), (0, 0)))
    wells, classes, edges = share_call(
        well_cell[None], well_test[None], well_value[None], cond_class
    )
    cond, source = source_call(wells, classes, edges, class_value)
    rows = CX * NZ
    sums = main_call(
        cond, source, zone_id.reshape(rows, CY), drawdown.reshape(TESTS, rows, CY)
    )
    parts = cov_call(diag.astype(jnp.int32)[None], pts, sums)
    return reduce_call(parts)


def solution(mesh):
    return jax.shard_map(
        per_device,
        mesh=mesh,
        in_specs=(
            P(("gx", "gy")),
            P(("gx", "gy")),
            P(("gx", "gy")),
            P("gx", None, "gy"),
            P(),
            P("gx", None, "gy"),
            P(None, "gx", None, "gy"),
            P(),
        ),
        out_specs=P(None, ("gx", "gy")),
        check_vma=False,
    )
```

```python
import functools

import jax
import jax.numpy as jnp
from jax import lax
from jax.experimental import pallas as pl
from jax.experimental.pallas import tpu as pltpu
from jax.sharding import PartitionSpec as P

MESH = pl.DeviceIdType.MESH
NT = (((1,), (1,)), ((), ()))
VMEM = pl.BlockSpec(memory_space=pltpu.VMEM)
F32 = jnp.float32
BF16 = jnp.bfloat16
MIB = 2**20

SWEEPS = 12
TESTS = 4
CX, NZ, CY = 4, 64, 128
N_GX, N_GY = 8, 16
DEVICES = N_GX * N_GY
NCLASS = 16
CAP = 16
ZONES = 98304
SHARE = ZONES // DEVICES
GROUPS = 16
MEMBERS = DEVICES // GROUPS
GROUP = ZONES // GROUPS
HALF = CY // 2
RIM = 16
XL, YL = 8, 3
HIGHS = 4 * YL * NZ
SLOTS = 16 * CAP
FIELD = (XL, YL, NZ, 128)

storage = 0.02
lam_low = 0.02
lam_high = 36.02
corr_len = 0.1
LOG2E = 1.4426950408889634


def cheb_setup():
    middle = 0.5 * (lam_high + lam_low)
    spread = 0.5 * (lam_high - lam_low)
    ratio_mid = middle / spread
    current = 1.0 / ratio_mid
    factors = []
    for counter in range(SWEEPS - 1):
        updated = 1.0 / (2.0 * ratio_mid - current)
        factors.append((updated * current, 2.0 * updated / spread))
        current = updated
    return (middle, factors)


def my_index():
    return lax.axis_index("gx") * N_GY + lax.axis_index("gy")


def coords(dev):
    return (dev // N_GY, dev % N_GY)


def greet(devs):
    barrier = pltpu.get_barrier_semaphore()
    for dev in devs:
        pl.semaphore_signal(barrier, inc=1, device_id=dev, device_id_type=MESH)
    pl.semaphore_wait(barrier, len(devs))


def for_others(act):
    gx, gy = lax.axis_index("gx"), lax.axis_index("gy")
    for b in range(1, N_GY):
        act((gx, lax.rem(gy + b, N_GY)))

    def each(a, _):
        other = lax.rem(gx + a, N_GX)
        for b in range(N_GY):
            act((other, lax.rem(gy + b, N_GY)))
        return 0

    lax.fori_loop(1, N_GX, each, 0)


def tile(j):
    return slice(8 * j, 8 * j + 8)


def share_kernel(
    cell_ref,
    test_ref,
    value_ref,
    class_ref,
    class_value_ref,
    wells_ref,
    cond,
    cls_ref,
    edge_ref,
    plane,
    rows,
    send,
    mine,
    edges,
    wells_sem,
    cls_sem,
    edge_sem,
):
    me = my_index()
    gx, gy = lax.axis_index("gx"), lax.axis_index("gy")
    edge_ref[...] = jnp.zeros_like(edge_ref)
    barrier = pltpu.get_barrier_semaphore()
    for_others(
        lambda dev: pl.semaphore_signal(barrier, inc=1, device_id=dev, device_id_type=MESH)
    )
    lane = lax.broadcasted_iota(jnp.int32, (32, 128), 1)
    classes = class_ref[...].reshape(CX * NZ, CY).astype(F32)
    mine[...] = classes.astype(BF16)
    for side, first in ((0, 0), (1, CY - RIM)):
        pack = jnp.zeros((32, 128), F32)
        for g in range(8):
            here = (lane >= RIM * g) & (lane < RIM * g + RIM)
            pack = jnp.where(here, roll_to(classes[32 * g : 32 * g + 32], RIM * g - first), pack)
        edges[side] = pack.astype(BF16)

    cell, test, value = cell_ref[...], test_ref[...], value_ref[...]
    n_rows = 2 * cell.shape[1]
    y = cell % (CY * N_GY)
    z = cell // (CY * N_GY) % NZ
    x = cell // (CY * N_GY * NZ)
    block = y // HALF
    within = y % HALF
    step = jnp.where(within < RIM, -1, jnp.where(within >= HALF - RIM, 1, 0))
    other = block + step
    valid = (step != 0) & (other >= 0) & (other < 2 * N_GY)

    def twice(first, second):
        return jnp.concatenate([first, second], axis=1)

    block, y, z, x = twice(block, other), twice(y, y), twice(z, z), twice(x, x)
    test, value = twice(test, test), twice(value, value)
    owner = (block % 2 * 4 + test) * N_GY + block // 2
    owner = twice(owner[:, : n_rows // 2], jnp.where(valid, owner[:, n_rows // 2 :], -1))
    y_loc = y - (block * HALF - RIM)
    x_low = x % XL
    high = ((x_low % 4 * YL + y_loc % YL) * 8 + z % 8) * 8 + z // 8
    low = x_low // 4 * 128 + x // XL * 32 + y_loc // YL
    code = (high * 256 + low).astype(F32)
    hot = jnp.where(
        lax.broadcasted_iota(jnp.int32, (DEVICES, n_rows), 0) == owner, 1.0, 0.0
    )
    earlier = jnp.where(
        lax.broadcasted_iota(jnp.int32, (n_rows, n_rows), 0)
        < lax.broadcasted_iota(jnp.int32, (n_rows, n_rows), 1),
        1.0,
        0.0,
    )
    hot16 = hot.astype(BF16)
    count = jnp.dot(hot16, earlier.astype(BF16), preferred_element_type=F32)
    rank = jnp.sum(hot * count, axis=0, keepdims=True).astype(jnp.int32)
    slot = lax.broadcasted_iota(jnp.int32, (SLOTS, n_rows), 0)
    part = jnp.concatenate(
        [jnp.where(slot == rank, code, 0.0), jnp.where(slot == rank, value, 0.0)], axis=0
    )
    total = None
    for _ in range(3):
        piece = part.astype(BF16)
        part = part - piece.astype(F32)
        term = lax.dot_general(hot16, piece, NT, preferred_element_type=F32)
        total = term if total is None else total + term
    for k in range(4):
        rows[k] = total[:, 128 * k : 128 * k + 128]
    for dev in range(DEVICES):
        for k in range(4):
            send[dev, k : k + 1, :] = rows[k, dev : dev + 1, :]

    pl.semaphore_wait(barrier, DEVICES - 1)

    def cls_copy(k):
        return pltpu.make_async_remote_copy(
            src_ref=mine,
            dst_ref=cls_ref.at[gx],
            send_sem=cls_sem.at[0],
            recv_sem=cls_sem.at[1],
            device_id=(lax.rem(gx + k, N_GX), gy),
            device_id_type=MESH,
        )

    for k in range(1, N_GX):
        cls_copy(k).start()

    def edge_copy(side, k):
        return pltpu.make_async_remote_copy(
            src_ref=edges.at[side],
            dst_ref=edge_ref.at[gx],
            send_sem=edge_sem.at[side],
            recv_sem=edge_sem.at[2],
            device_id=(k + 4 * (1 - side), lax.rem(gy + N_GY - 1 + 2 * side, N_GY)),
            device_id_type=MESH,
        )

    @pl.when(gy > 0)
    def _():
        for k in range(4):
            edge_copy(0, k).start()

    @pl.when(gy < N_GY - 1)
    def _():
        for k in range(4):
            edge_copy(1, k).start()

    cls_ref[gx] = mine[...]

    def send_rows(dev):
        pltpu.make_async_remote_copy(
            src_ref=send.at[dev[0] * N_GY + dev[1]],
            dst_ref=wells_ref.at[me],
            send_sem=wells_sem.at[0],
            recv_sem=wells_sem.at[1],
            device_id=dev,
            device_id_type=MESH,
        ).start()

    for_others(send_rows)
    wells_ref[me] = send[me]
    seven = pl.ds(0, N_GX - 1)
    pltpu.make_async_copy(cls_ref.at[seven], cls_ref.at[seven], cls_sem.at[1]).wait()
    half = gx // 4

    @pl.when(((half == 1) & (gy < N_GY - 1)) | ((half == 0) & (gy > 0)))
    def _():
        pltpu.make_async_copy(edge_ref, edge_ref, edge_sem.at[2]).wait()

    from_lane = lax.broadcasted_iota(jnp.int32, (128, 128), 0)
    to_lane = lax.broadcasted_iota(jnp.int32, (128, 128), 1)
    local = (from_lane + jnp.where(half == 0, RIM, HALF + RIM)) % 128
    picks = [
        jnp.where(local == YL * (to_lane % 32) + low, 1.0, 0.0).astype(BF16) for low in range(YL)
    ]
    lane32 = lax.broadcasted_iota(jnp.int32, (32, 128), 1)
    rim_at = jnp.where(half == 0, CY - RIM, 0)
    in_rim = (lane32 >= rim_at) & (lane32 < rim_at + RIM)
    group64 = lax.broadcasted_iota(jnp.int32, (NZ, 128), 1) // 32

    def whole(x):
        o = x // CX
        own = cls_ref[o, NZ * (x % CX) : NZ * (x % CX) + NZ, :].astype(F32)
        side = edge_ref[o].astype(F32)
        parts = []
        for g in (2 * (x % CX), 2 * (x % CX) + 1):
            moved = pltpu.roll(side, lax.rem(rim_at + 128 - RIM * g, 128), 1)
            parts.append(jnp.where(in_rim, moved, own[32 * (g % 2) : 32 * (g % 2) + 32]))
        return jnp.concatenate(parts, axis=0).astype(BF16)

    for x_low in range(XL):
        blocks = jnp.concatenate([whole(XL * h + x_low) for h in range(4)], axis=0)
        for y_low in range(YL):
            moved = jnp.dot(blocks, picks[y_low], preferred_element_type=F32)
            merged = moved[0:NZ]
            for h in range(1, 4):
                merged = jnp.where(group64 == h, moved[NZ * h : NZ * h + NZ], merged)
            value = jnp.zeros((NZ, 128), F32)
            for k in range(NCLASS):
                value = jnp.where(merged == float(k), class_value_ref[k], value)
            plane[...] = value
            for j in range(8):
                cond[x_low, y_low, tile(j), :] = plane[pl.ds(j, 8, stride=8), :]

    rest = pl.ds(0, DEVICES - 1)
    pltpu.make_async_copy(wells_ref.at[rest], wells_ref.at[rest], wells_sem.at[1]).wait()
    pltpu.make_async_copy(send.at[rest], send.at[rest], wells_sem.at[0]).wait()
    pltpu.make_async_copy(cls_ref.at[seven], cls_ref.at[seven], cls_sem.at[0]).wait()
    four = pl.ds(0, 4)

    @pl.when(gy > 0)
    def _():
        pltpu.make_async_copy(edge_ref.at[four], edge_ref.at[four], edge_sem.at[0]).wait()

    @pl.when(gy < N_GY - 1)
    def _():
        pltpu.make_async_copy(edge_ref.at[four], edge_ref.at[four], edge_sem.at[1]).wait()


def share_call(cell, test, value, classes, class_value):
    return pl.pallas_call(
        share_kernel,
        out_shape=(
            jax.ShapeDtypeStruct((DEVICES, 4, 128), F32),
            jax.ShapeDtypeStruct(FIELD, F32),
        ),
        in_specs=[VMEM] * 4 + [pl.BlockSpec(memory_space=pltpu.SMEM)],
        out_specs=(VMEM,) * 2,
        scratch_shapes=[
            pltpu.VMEM((N_GX, CX * NZ, CY), BF16),
            pltpu.VMEM((N_GX, 32, 128), BF16),
            pltpu.VMEM((NZ, 128), F32),
            pltpu.VMEM((4, DEVICES, 128), F32),
            pltpu.VMEM((DEVICES, 4, 128), F32),
            pltpu.VMEM((CX * NZ, CY), BF16),
            pltpu.VMEM((2, 32, 128), BF16),
            pltpu.SemaphoreType.DMA((2,)),
            pltpu.SemaphoreType.DMA((2,)),
            pltpu.SemaphoreType.DMA((3,)),
        ],
        compiler_params=pltpu.CompilerParams(
            collective_id=0, has_side_effects=True, vmem_limit_bytes=48 * MIB
        ),
    )(cell, test, value, classes, class_value)


def roll_to(value, shift):
    shift = shift % 128
    return pltpu.roll(value, shift, 1) if shift else value


def source_kernel(wells_ref, src_ref, rows, acc):
    for dev in range(DEVICES):
        for k in range(4):
            rows[k, dev : dev + 1, :] = wells_ref[dev, k : k + 1, :]
    lane16 = lax.broadcasted_iota(jnp.int32, (16, 128), 1)
    row_high = lax.broadcasted_iota(jnp.int32, (HIGHS, 128), 0)
    row_low = lax.broadcasted_iota(jnp.int32, (256, 128), 0)
    acc[...] = jnp.zeros_like(acc)

    def level(n, _):
        row, at = n // 8, n % 8 * CAP
        codes = jnp.zeros((16, 128), F32)
        values = jnp.zeros((16, 128), F32)
        for g in range(8):
            here = lane16 // CAP == g
            turn = lax.rem(CAP * g + 128 - at, 128)
            block = rows[row, 16 * g : 16 * g + 16, :]
            codes = jnp.where(here, pltpu.roll(block, turn, 1), codes)
            block = rows[2 + row, 16 * g : 16 * g + 16, :]
            values = jnp.where(here, pltpu.roll(block, turn, 1), values)

        @pl.when(jnp.max(jnp.abs(values)) > 0.0)
        def _():
            whole_codes = codes.astype(jnp.int32)
            highs, lows = whole_codes // 256, whole_codes % 256
            first = values.astype(BF16).astype(F32)
            second = values - first
            left, right_a, right_b = [], [], []
            for r in range(16):
                left.append(jnp.where(row_high == highs[r : r + 1], 1.0, 0.0).astype(BF16))
                same = row_low == lows[r : r + 1]
                right_a.append(jnp.where(same, first[r : r + 1], 0.0).astype(BF16))
                right_b.append(jnp.where(same, second[r : r + 1], 0.0).astype(BF16))
            left = jnp.concatenate(left, axis=1)
            acc[...] += lax.dot_general(
                left, jnp.concatenate(right_a, axis=1), NT, preferred_element_type=F32
            ) + lax.dot_general(
                left, jnp.concatenate(right_b, axis=1), NT, preferred_element_type=F32
            )

        return 0

    lax.fori_loop(0, SLOTS // CAP, level, 0)

    for x_low in range(XL):
        for y_low in range(YL):
            at = NZ * (x_low % 4 * YL + y_low)
            src_ref[x_low, y_low] = acc[at : at + NZ, x_low // 4 * 128 : x_low // 4 * 128 + 128]


def source_call(wells):
    return pl.pallas_call(
        source_kernel,
        out_shape=jax.ShapeDtypeStruct(FIELD, F32),
        in_specs=[VMEM],
        out_specs=VMEM,
        scratch_shapes=[pltpu.VMEM((4, DEVICES, 128), F32), pltpu.VMEM((HIGHS, 256), F32)],
        compiler_params=pltpu.CompilerParams(vmem_limit_bytes=48 * MIB),
    )(wells)


def groups_of(gx, gy):
    tail = gx == N_GX - 1
    low = jnp.where(tail, gy % 8, gy)
    high = jnp.where(tail, gy % 8 + 8, (gy + gx + 1) % GROUPS)
    return low, high, tail & (gy >= 8)


def takers_of(group):
    out = []
    for k in range(N_GX - 1):
        out.append(((k, group), 0))
        out.append(((k, (group + GROUPS - k - 1) % GROUPS), 1))
    place = group // 8
    out.append(((N_GX - 1, group % 8), place))
    out.append(((N_GX - 1, group % 8 + 8), place))
    return out


INNER = SHARE // 2


def main_kernel(
    cond,
    src_ref,
    zone_ref,
    draw_ref,
    out_ref,
    face_x,
    face_y,
    face_z,
    extra,
    dirs,
    resid,
    sol,
    flux,
    zone_out,
    draw_out,
    zone_in,
    draw_in,
    sens,
    acc,
    send_a,
    recv_a,
    send_b,
    recv_b,
    mine,
    zone_sem,
    draw_sem,
    a_sem,
    b_sem,
    got_sem,
    put_sem,
):
    me = my_index()
    gx, gy = lax.axis_index("gx"), lax.axis_index("gy")
    half = gx // 4
    lane = lax.broadcasted_iota(jnp.int32, (8, 128), 1)
    sub = lax.broadcasted_iota(jnp.int32, (8, 128), 0)
    x_high, y_high = lane // 32, lane % 32
    left_half = lax.broadcasted_iota(jnp.int32, (NZ, 128), 1) < HALF

    group, member = me // MEMBERS, me % MEMBERS
    low_group, high_group, _ = groups_of(gx, gy)
    takers = takers_of(group)
    barrier = pltpu.get_barrier_semaphore()
    for k in range(1, N_GX):
        pl.semaphore_signal(
            barrier, inc=1, device_id=(lax.rem(gx + k, N_GX), gy), device_id_type=MESH
        )
    for k in range(1, N_GY):
        pl.semaphore_signal(
            barrier, inc=1, device_id=(gx, lax.rem(gy + k, N_GY)), device_id_type=MESH
        )
    for held in (low_group, high_group):
        for m in range(MEMBERS):
            owner = held * MEMBERS + m

            @pl.when(owner != me)
            def _():
                pl.semaphore_signal(barrier, inc=1, device_id=coords(owner), device_id_type=MESH)

    for dev, _ in takers:

        @pl.when(dev[0] * N_GY + dev[1] != me)
        def _():
            pl.semaphore_signal(barrier, inc=1, device_id=dev, device_id_type=MESH)

    def packed(fields, side, n):
        a, b = fields[n], fields[n + 2]
        if side == 0:
            return jnp.where(left_half, a, pltpu.roll(b, HALF, 1))
        return jnp.where(left_half, pltpu.roll(a, HALF, 1), b)

    zones = [zone_ref[NZ * x : NZ * x + NZ, :].astype(F32) for x in range(CX)]
    for side in range(2):
        for n in range(2):
            zone_out[side, NZ * n : NZ * n + NZ, :] = packed(zones, side, n)
    for t in range(TESTS):
        draws = [draw_ref[t, NZ * x : NZ * x + NZ, :].astype(F32) for x in range(CX)]
        for side in range(2):
            for n in range(2):
                draw_out[TESTS * side + t, NZ * n : NZ * n + NZ, :] = packed(
                    draws, side, n
                ).astype(BF16)

    self_here = (low_group == group) | (high_group == group)
    pl.semaphore_wait(barrier, N_GX + N_GY - 2 + 32 - 2 * self_here.astype(jnp.int32))

    def to_column(k, src, dst, sems):
        dev = lax.rem(gx + k, N_GX)
        return pltpu.make_async_remote_copy(
            src_ref=src(dev),
            dst_ref=dst,
            send_sem=sems[0],
            recv_sem=sems[1],
            device_id=(dev, gy),
            device_id_type=MESH,
        )

    for k in range(1, N_GX):
        to_column(k, lambda dev: zone_out.at[dev // TESTS], zone_in.at[gx], (zone_sem.at[N_GX], zone_sem.at[gx])).start()
        to_column(k, lambda dev: draw_out.at[dev], draw_in.at[gx], (draw_sem.at[N_GX], draw_sem.at[gx])).start()
    zone_in[gx] = zone_out[half]
    draw_in[gx] = draw_out[gx]

    zero = jnp.zeros((8, 128), F32)
    first_y = jnp.where((gy == 0) & (half == 0), RIM, -1)
    last_y = jnp.where((gy == N_GY - 1) & (half == 1), RIM + HALF - 1, -2)

    def faces(x_low, _):
        for y_low in range(YL):
            y_loc = YL * y_high + y_low
            for j in range(8):
                c = cond[x_low, y_low, tile(j), :]
                more = jnp.full((8, 128), storage, F32)
                end = x_low == XL - 1
                near = cond[jnp.where(end, 0, x_low + 1), y_low, tile(j), :]
                near = jnp.where(end, pltpu.roll(near, 96, 1), near)
                off = end & (x_high == 3)
                face_x[x_low, y_low, tile(j), :] = jnp.where(off, zero, 0.5 * (c + near))
                more = more + jnp.where(off, 0.5 * c, zero)
                more = more + jnp.where((x_low == 0) & (x_high == 0), 0.5 * c, zero)
                if y_low < YL - 1:
                    near = cond[x_low, y_low + 1, tile(j), :]
                    off = y_loc + 1 == first_y
                else:
                    near = pltpu.roll(cond[x_low, 0, tile(j), :], 127, 1)
                    off = (y_loc + 1 == first_y) | (y_high == 31)
                off = off | (y_loc == last_y)
                face_y[x_low, y_low, tile(j), :] = jnp.where(off, zero, 0.5 * (c + near))
                more = more + jnp.where((y_loc == first_y) | (y_loc == last_y), 0.5 * c, zero)
                if j < 7:
                    face_z[x_low, y_low, tile(j), :] = 0.5 * (c + cond[x_low, y_low, tile(j + 1), :])
                else:
                    near = pltpu.roll(cond[x_low, y_low, tile(0), :], 7, 0)
                    face_z[x_low, y_low, tile(j), :] = jnp.where(sub == 7, zero, 0.5 * (c + near))
                    more = more + jnp.where(sub == 7, 0.5 * c, zero)
                if j == 0:
                    more = more + jnp.where(sub == 0, 0.5 * c, zero)
                extra[x_low, y_low, tile(j), :] = more
        return 0

    lax.fori_loop(0, XL, faces, 0)

    middle, factors = cheb_setup()
    for x_low in range(XL):
        for y_low in range(YL):
            value = src_ref[x_low, y_low]
            resid[x_low, y_low] = value
            dirs[0, x_low, y_low] = value / middle
            sol[x_low, y_low] = jnp.zeros((NZ, 128), F32)

    keeps = [pair[0] for pair in factors]
    news = [pair[1] for pair in factors]

    def sweep(k, _):
        par = lax.rem(k, 2)
        nxt = 1 - par
        keep, new = jnp.float32(keeps[0]), jnp.float32(news[0])
        for n in range(1, SWEEPS - 1):
            keep = jnp.where(k == n, jnp.float32(keeps[n]), keep)
            new = jnp.where(k == n, jnp.float32(news[n]), new)
        for y_low in range(YL):
            for j in range(8):
                over = face_x[XL - 1, y_low, tile(j), :] * (
                    pltpu.roll(dirs[par, 0, y_low, tile(j), :], 96, 1)
                    - dirs[par, XL - 1, y_low, tile(j), :]
                )
                flux[XL - 1, y_low, tile(j), :] = over
                flux[XL, y_low, tile(j), :] = pltpu.roll(over, 32, 1)
        for x_low in range(XL):
            behind = XL if x_low == 0 else x_low - 1
            v = [[dirs[par, x_low, y_low, tile(j), :] for y_low in range(YL)] for j in range(8)]
            z_old = []
            for y_low in range(YL):
                z_old.append(
                    pltpu.roll(
                        face_z[x_low, y_low, tile(7), :]
                        * (pltpu.roll(v[0][y_low], 7, 0) - v[7][y_low]),
                        1,
                        0,
                    )
                )
            for j in range(8):
                fy = [
                    face_y[x_low, y_low, tile(j), :]
                    * (
                        (v[j][y_low + 1] if y_low < YL - 1 else pltpu.roll(v[j][0], 127, 1))
                        - v[j][y_low]
                    )
                    for y_low in range(YL)
                ]
                for y_low in range(YL):
                    here = v[j][y_low]
                    at = (x_low, y_low, tile(j))
                    if x_low < XL - 1:
                        fx = face_x[at] * (dirs[par, x_low + 1, y_low, tile(j), :] - here)
                        flux[at] = fx
                    else:
                        fx = flux[at]
                    above = v[j + 1][y_low] if j < 7 else pltpu.roll(v[0][y_low], 7, 0)
                    fz = face_z[at] * (above - here)
                    fy_old = fy[y_low - 1] if y_low else pltpu.roll(fy[YL - 1], 1, 1)
                    gain = (fx - flux[behind, y_low, tile(j), :]) + (fy[y_low] - fy_old)
                    gain = gain + (fz - z_old[y_low])
                    z_old[y_low] = fz
                    left = resid[at] + (gain - extra[at] * here)
                    resid[at] = left
                    sol[at] = sol[at] + here
                    dirs[nxt, x_low, y_low, tile(j), :] = keep * here + new * left
        return 0

    lax.fori_loop(0, SWEEPS - 1, sweep, 0)
    last = (SWEEPS - 1) % 2

    row = lax.broadcasted_iota(jnp.int32, (YL * 128, 256), 0)
    col = lax.broadcasted_iota(jnp.int32, (YL * 128, 256), 1)
    put = jnp.where(
        (row % 128 // 32 == col // HALF)
        & (YL * (row % 32) + row // 128 == col % HALF + RIM),
        1.0,
        0.0,
    ).astype(BF16)
    for odd in range(2):
        wide = []
        for x_low in range(4 * odd, 4 * odd + 4):
            field = jnp.concatenate(
                [
                    cond[x_low, y_low] * (sol[x_low, y_low] + dirs[last, x_low, y_low])
                    for y_low in range(YL)
                ], axis=1
            )
            first = field.astype(BF16)
            second = (field - first.astype(F32)).astype(BF16)
            wide.append(
                jnp.dot(first, put, preferred_element_type=F32)
                + jnp.dot(second, put, preferred_element_type=F32)
            )
        for h in range(4):
            lanes = slice(128 * (h // 2), 128 * (h // 2) + 128)
            for n in range(2):
                a, b = wide[n][:, lanes], wide[n + 2][:, lanes]
                if h % 2 == 0:
                    both = jnp.where(left_half, a, pltpu.roll(b, 64, 1))
                else:
                    both = jnp.where(left_half, pltpu.roll(a, 64, 1), b)
                for j in range(8):
                    sens[2 * h + odd, pl.ds(NZ * n + j, 8, stride=8), :] = both[tile(j)]


    seven = pl.ds(0, N_GX - 1)

    inner = lax.broadcasted_iota(jnp.int32, (256, 128), 0).astype(F32).astype(BF16)
    one, nil = jnp.ones((), BF16), jnp.zeros((), BF16)

    def spread(row, times):
        return jnp.concatenate([jnp.broadcast_to(row, (16, 128)).astype(BF16)] * times, axis=0)

    def step(k, _):
        o = lax.rem(gx + k, N_GX)

        @pl.when(k > 0)
        def _():
            for ref, sems in ((zone_in, zone_sem), (draw_in, draw_sem)):
                pltpu.make_async_copy(ref.at[o], ref.at[o], sems.at[o]).wait()

        zone = zone_in[o]
        value = sens[o] * draw_in[o].astype(F32)
        outer = ((zone + 0.5) * (1.0 / INNER)).astype(jnp.int32)
        place = zone - outer.astype(F32) * INNER
        outer = outer // 2 % N_GY * 16 + outer // 32 * 2 + outer % 2
        outer = outer.astype(F32)
        left, right = [], []
        for r in range(2 * NZ):
            row = slice(r, r + 1)
            right.append(jnp.where(inner == spread(outer[row], 16), spread(value[row], 16), nil))
            left.append(
                jnp.concatenate(
                    [
                        jnp.where(inner == spread(place[row], 16), one, nil),
                        jnp.where(
                            inner[0 : INNER - 256]
                            == spread(place[row] - 256.0, (INNER - 256) // 16),
                            one,
                            nil,
                        ),
                    ],
                    axis=0,
                )
            )
        acc[...] += lax.dot_general(
            jnp.concatenate(left, axis=1),
            jnp.concatenate(right, axis=1),
            NT,
            preferred_element_type=F32,
        )
        return 0

    acc[...] = jnp.zeros_like(acc)
    lax.fori_loop(0, N_GX, step, 0)

    send_a[...] = acc[...].T.astype(BF16).reshape(N_GY, 16, INNER)

    def row_copy(k):
        dev = lax.rem(gy + k, N_GY)
        return pltpu.make_async_remote_copy(
            src_ref=send_a.at[dev],
            dst_ref=recv_a.at[gy],
            send_sem=a_sem.at[0],
            recv_sem=a_sem.at[1],
            device_id=(gx, dev),
            device_id_type=MESH,
        )

    for k in range(1, N_GY):
        row_copy(k).start()
    recv_a[gy] = send_a[gy]
    rest = pl.ds(0, N_GY - 1)
    pltpu.make_async_copy(recv_a.at[rest], recv_a.at[rest], a_sem.at[1]).wait()
    total = recv_a[0].astype(F32)
    for n in range(1, N_GY):
        total = total + recv_a[n].astype(F32)
    for o in range(N_GX):
        send_b[o] = total[2 * o : 2 * o + 2, :]
    for k in range(1, N_GX):
        to_column(k, lambda dev: send_b.at[dev], recv_b.at[gx], (b_sem.at[0], b_sem.at[1])).start()
    recv_b[gx] = send_b[gx]
    pltpu.make_async_copy(recv_b.at[seven], recv_b.at[seven], b_sem.at[1]).wait()
    for t in range(TESTS):
        total = (recv_b[t] + recv_b[TESTS + t]).astype(BF16).astype(F32)
        for n in range(2):
            mine[t : t + 1, INNER * n : INNER * n + INNER] = total[n : n + 1]

    def put_out(n, dev, place):
        return pltpu.make_async_remote_copy(
            src_ref=mine,
            dst_ref=out_ref.at[place, member],
            send_sem=put_sem.at[n],
            recv_sem=got_sem.at[place, member],
            device_id=dev,
            device_id_type=MESH,
        )

    for n, (dev, place) in enumerate(takers):
        taker_is_me = dev[0] * N_GY + dev[1] == me

        @pl.when(jnp.logical_not(taker_is_me))
        def _():
            put_out(n, dev, place).start()

        @pl.when(taker_is_me)
        def _():
            out_ref[place, member] = mine[...]

    pltpu.make_async_copy(send_a.at[rest], send_a.at[rest], a_sem.at[0]).wait()
    pltpu.make_async_copy(send_b.at[seven], send_b.at[seven], b_sem.at[0]).wait()
    pltpu.make_async_copy(zone_in.at[seven], zone_in.at[seven], zone_sem.at[N_GX]).wait()
    pltpu.make_async_copy(draw_in.at[seven], draw_in.at[seven], draw_sem.at[N_GX]).wait()
    for place, held in ((0, low_group), (1, high_group)):
        for m in range(MEMBERS):

            @pl.when(held * MEMBERS + m != me)
            def _():
                pltpu.make_async_copy(
                    out_ref.at[place, m], out_ref.at[place, m], got_sem.at[place, m]
                ).wait()

    for n, (dev, place) in enumerate(takers):

        @pl.when(dev[0] * N_GY + dev[1] != me)
        def _():
            put_out(n, dev, place).wait_send()


def main_call(cond, source, zone, drawdown):
    return pl.pallas_call(
        main_kernel,
        out_shape=jax.ShapeDtypeStruct((2, MEMBERS, TESTS, SHARE), F32),
        in_specs=[VMEM] * 4,
        out_specs=VMEM,
        scratch_shapes=[
            pltpu.VMEM(FIELD, F32),
            pltpu.VMEM(FIELD, F32),
            pltpu.VMEM(FIELD, F32),
            pltpu.VMEM(FIELD, F32),
            pltpu.VMEM((2,) + FIELD, F32),
            pltpu.VMEM(FIELD, F32),
            pltpu.VMEM(FIELD, F32),
            pltpu.VMEM((XL + 1, YL, NZ, 128), F32),
            pltpu.VMEM((2, 2 * NZ, 128), F32),
            pltpu.VMEM((N_GX, 2 * NZ, 128), BF16),
            pltpu.VMEM((N_GX, 2 * NZ, 128), F32),
            pltpu.VMEM((N_GX, 2 * NZ, 128), BF16),
            pltpu.VMEM((N_GX, 2 * NZ, 128), F32),
            pltpu.VMEM((INNER, 256), F32),
            pltpu.VMEM((N_GY, 16, INNER), BF16),
            pltpu.VMEM((N_GY, 16, INNER), BF16),
            pltpu.VMEM((N_GX, 2, INNER), F32),
            pltpu.VMEM((N_GX, 2, INNER), F32),
            pltpu.VMEM((TESTS, SHARE), F32),
            pltpu.SemaphoreType.DMA((N_GX + 1,)),
            pltpu.SemaphoreType.DMA((N_GX + 1,)),
            pltpu.SemaphoreType.DMA((2,)),
            pltpu.SemaphoreType.DMA((2,)),
            pltpu.SemaphoreType.DMA((2, MEMBERS)),
            pltpu.SemaphoreType.DMA((16,)),
        ],
        compiler_params=pltpu.CompilerParams(
            collective_id=1, has_side_effects=True, vmem_limit_bytes=48 * MIB
        ),
    )(cond, source, zone, drawdown)


ROWS, COLS = 1024, 512
TERMS = 128


def pieces(value):
    out = []
    for _ in range(3):
        piece = value.astype(BF16).astype(F32)
        out.append(piece)
        value = value - piece
    return out


def terms(pts, as_rows):
    sub = lax.broadcasted_iota(jnp.int32, pts.shape, 0)
    norm = pieces(jnp.broadcast_to(jnp.sum(pts * pts, axis=0, keepdims=True), pts.shape))
    parts = pieces(pts)
    first = 0 if as_rows else 3
    rest = jnp.where((sub < 6) & ((sub >= 3) if as_rows else (sub < 3)), 1.0, 0.0)
    for n in range(3):
        rest = jnp.where(sub == first + n, norm[n], rest)
    blocks = [
        -2.0 * parts[i] if as_rows else parts[j] for i in range(3) for j in range(3)
    ]
    return jnp.concatenate(blocks + [rest], axis=0)


def cov_kernel(
    diag_ref, pts_ref, sums_ref, out_ref, z_ref, z_turned, row_terms, col_terms, near, total
):
    diag = diag_ref[0]
    out_ref[...] = jnp.zeros_like(out_ref)
    for g in range(2):
        for m in range(MEMBERS):
            both = jnp.concatenate([sums_ref[g, m], jnp.zeros((TESTS, SHARE), F32)], axis=0)
            z_ref[g, :, SHARE * m : SHARE * m + SHARE] = both.astype(BF16)

    def phase(rg, _):
        cg = jnp.where(diag == 1, rg, 1)
        for i in range(GROUP // ROWS):
            at = slice(ROWS * i, ROWS * i + ROWS)
            row_terms[0:80, at] = terms(pts_ref[rg, :, at], True)
            row_terms[80:TERMS, at] = jnp.zeros((TERMS - 80, ROWS), F32)
            col_terms[0:80, at] = terms(pts_ref[cg, :, at], False).astype(BF16)
            col_terms[80:TERMS, at] = jnp.zeros((TERMS - 80, ROWS), BF16)
            wide = jnp.concatenate(
                [z_ref[cg, :, at].astype(F32), jnp.zeros((120, ROWS), F32)], axis=0
            )
            z_turned[at, :] = wide.T.astype(BF16)

        def row_block(r, _):
            rs = pl.ds(pl.multiple_of(r * ROWS, ROWS), ROWS)
            near[...] = row_terms[:, rs].T.astype(BF16)
            total[...] = jnp.zeros_like(total)
            z_row = z_ref[rg, :, rs]

            def at_cols(c):
                return pl.ds(pl.multiple_of(c * COLS, COLS), COLS)

            def tile(c, rows):
                squared = jnp.dot(
                    near[rows, :], col_terms[:, at_cols(c)], preferred_element_type=F32
                )
                squared = jnp.maximum(squared, 1e-30)
                return jnp.exp2(squared * (-lax.rsqrt(squared))).astype(BF16)

            def for_rows(c, rows, held):
                total[rows, :] += jnp.dot(
                    held, z_turned[at_cols(c), :], preferred_element_type=F32
                )

            def for_cols(c, weights, held):
                out_ref[cg, :, at_cols(c)] += jnp.dot(
                    weights, held, preferred_element_type=F32
                )

            every, lower = slice(0, ROWS), slice(COLS, ROWS)

            @pl.when(diag == 1)
            def _():
                held = tile(2 * r, every)
                for_rows(2 * r, every, held)
                for_cols(2 * r, z_row[:, COLS:], held[COLS:])
                for_rows(2 * r + 1, lower, tile(2 * r + 1, lower))

            def two(p, _):
                for c in (2 * p, 2 * p + 1):
                    held = tile(c, every)
                    for_rows(c, every, held)
                    for_cols(c, z_row, held)
                return 0

            lax.fori_loop(jnp.where(diag == 1, r + 1, 0), GROUP // ROWS, two, 0)
            out_ref[rg, :, rs] += total[...].T[0:8]
            return 0

        lax.fori_loop(0, GROUP // ROWS, row_block, 0)
        return 0

    lax.fori_loop(0, 1 + diag, phase, 0)


def cov_call(diag, pts, sums):
    return pl.pallas_call(
        cov_kernel,
        out_shape=jax.ShapeDtypeStruct((2, 8, GROUP), F32),
        in_specs=[pl.BlockSpec(memory_space=pltpu.SMEM), VMEM, VMEM],
        out_specs=VMEM,
        scratch_shapes=[
            pltpu.VMEM((2, 8, GROUP), BF16),
            pltpu.VMEM((GROUP, 128), BF16),
            pltpu.VMEM((TERMS, GROUP), F32),
            pltpu.VMEM((TERMS, GROUP), BF16),
            pltpu.VMEM((ROWS, TERMS), BF16),
            pltpu.VMEM((ROWS, 128), F32),
        ],
        compiler_params=pltpu.CompilerParams(vmem_limit_bytes=48 * MIB),
    )(diag, pts, sums)


def reduce_kernel(part_ref, out_ref, send, recv, send_sem, recv_sem):
    me = my_index()
    gx, gy = lax.axis_index("gx"), lax.axis_index("gy")
    low, high, diag = groups_of(gx, gy)
    group, member = me // MEMBERS, me % MEMBERS
    for g in range(2):
        for m in range(MEMBERS):
            send[g, m] = part_ref[g, 0:TESTS, SHARE * m : SHARE * m + SHARE]

    takers = takers_of(group)
    barrier = pltpu.get_barrier_semaphore()
    for place, held in ((0, low), (1, high)):
        for m in range(MEMBERS):
            owner = held * MEMBERS + m

            @pl.when(owner != me)
            def _():
                pl.semaphore_signal(barrier, inc=1, device_id=coords(owner), device_id_type=MESH)

    for dev, _ in takers:

        @pl.when(dev[0] * N_GY + dev[1] != me)
        def _():
            pl.semaphore_signal(barrier, inc=1, device_id=dev, device_id_type=MESH)

    self_here = (low == group) | (high == group)
    pl.semaphore_wait(barrier, 32 - 2 * self_here.astype(jnp.int32))

    def put(place, m, held, slot):
        return pltpu.make_async_remote_copy(
            src_ref=send.at[place, m],
            dst_ref=recv.at[slot],
            send_sem=send_sem.at[place, m],
            recv_sem=recv_sem.at[slot],
            device_id=coords(held * MEMBERS + m),
            device_id_type=MESH,
        )

    sides = (
        (0, low, jnp.where(diag, low, high)),
        (1, high, jnp.where(diag, high, low)),
    )
    for place, held, slot in sides:
        for m in range(MEMBERS):

            @pl.when(held * MEMBERS + m != me)
            def _():
                put(place, m, held, slot).start()

            @pl.when(held * MEMBERS + m == me)
            def _():
                recv[slot] = send[place, m]

    own_slot = jnp.where(
        low == group, jnp.where(diag, low, high), jnp.where(diag, high, low)
    )
    for slot in range(GROUPS):

        @pl.when(jnp.logical_not(self_here & (own_slot == slot)))
        def _():
            pltpu.make_async_copy(recv.at[slot], recv.at[slot], recv_sem.at[slot]).wait()

    total = recv[0]
    for slot in range(1, GROUPS):
        total = total + recv[slot]
    out_ref[...] = total.astype(BF16)
    for place, held, slot in sides:
        for m in range(MEMBERS):

            @pl.when(held * MEMBERS + m != me)
            def _():
                put(place, m, held, slot).wait_send()


def reduce_call(parts):
    return pl.pallas_call(
        reduce_kernel,
        out_shape=jax.ShapeDtypeStruct((TESTS, SHARE), BF16),
        in_specs=[VMEM],
        out_specs=VMEM,
        scratch_shapes=[
            pltpu.VMEM((2, MEMBERS, TESTS, SHARE), F32),
            pltpu.VMEM((GROUPS, TESTS, SHARE), F32),
            pltpu.SemaphoreType.DMA((2, MEMBERS)),
            pltpu.SemaphoreType.DMA((GROUPS,)),
        ],
        compiler_params=pltpu.CompilerParams(
            collective_id=2, has_side_effects=True, vmem_limit_bytes=32 * MIB
        ),
    )(parts)


def per_device(
    well_cell, well_test, well_value, cond_class, class_value, zone_id, drawdown, centroid
):
    gx, gy = lax.axis_index("gx"), lax.axis_index("gy")
    low, high, diag = groups_of(gx, gy)
    pts = jnp.stack(
        [lax.dynamic_slice_in_dim(centroid, held * GROUP, GROUP, 1) for held in (low, high)]
    )
    pts = jnp.pad((pts - 0.5) * (LOG2E / corr_len), ((0, 0), (0, 5), (0, 0)))
    wells, cond = share_call(
        well_cell[None], well_test[None], well_value[None], cond_class, class_value
    )
    source = source_call(wells)
    rows = CX * NZ
    sums = main_call(
        cond, source, zone_id.reshape(rows, CY), drawdown.reshape(TESTS, rows, CY)
    )
    parts = cov_call(diag.astype(jnp.int32)[None], pts, sums)
    return reduce_call(parts)


def solution(mesh):
    return jax.shard_map(
        per_device,
        mesh=mesh,
        in_specs=(
            P(("gx", "gy")),
            P(("gx", "gy")),
            P(("gx", "gy")),
            P("gx", None, "gy"),
            P(),
            P("gx", None, "gy"),
            P(None, "gx", None, "gy"),
            P(),
        ),
        out_specs=P(None, ("gx", "gy")),
        check_vma=False,
    )
```

```python
import functools

import jax
import jax.numpy as jnp
from jax import lax
from jax.experimental import pallas as pl
from jax.experimental.pallas import tpu as pltpu
from jax.sharding import PartitionSpec as P

MESH = pl.DeviceIdType.MESH
NT = (((1,), (1,)), ((), ()))
VMEM = pl.BlockSpec(memory_space=pltpu.VMEM)
F32 = jnp.float32
BF16 = jnp.bfloat16
MIB = 2**20

SWEEPS = 12
TESTS = 4
CX, NZ, CY = 4, 64, 128
N_GX, N_GY = 8, 16
DEVICES = N_GX * N_GY
NCLASS = 16
CAP = 16
ZONES = 98304
SHARE = ZONES // DEVICES
GROUPS = 16
MEMBERS = DEVICES // GROUPS
GROUP = ZONES // GROUPS
HALF = CY // 2
RIM = 16
XL, YL = 8, 3
HIGHS = 4 * YL * NZ
SLOTS = 16 * CAP
FIELD = (XL, YL, NZ, 128)

storage = 0.02
lam_low = 0.02
lam_high = 36.02
corr_len = 0.1
LOG2E = 1.4426950408889634


def cheb_setup():
    middle = 0.5 * (lam_high + lam_low)
    spread = 0.5 * (lam_high - lam_low)
    ratio_mid = middle / spread
    current = 1.0 / ratio_mid
    factors = []
    for counter in range(SWEEPS - 1):
        updated = 1.0 / (2.0 * ratio_mid - current)
        factors.append((updated * current, 2.0 * updated / spread))
        current = updated
    return (middle, factors)


def my_index():
    return lax.axis_index("gx") * N_GY + lax.axis_index("gy")


def coords(dev):
    return (dev // N_GY, dev % N_GY)


def for_others(act):
    gx, gy = lax.axis_index("gx"), lax.axis_index("gy")
    for b in range(1, N_GY):
        act((gx, lax.rem(gy + b, N_GY)))

    def each(a, _):
        other = lax.rem(gx + a, N_GX)
        for b in range(N_GY):
            act((other, lax.rem(gy + b, N_GY)))
        return 0

    lax.fori_loop(1, N_GX, each, 0)


def tile(j):
    return slice(8 * j, 8 * j + 8)


def share_kernel(
    cell_ref,
    test_ref,
    value_ref,
    class_ref,
    class_value_ref,
    wells_ref,
    cond,
    cls_ref,
    edge_ref,
    plane,
    rows,
    send,
    mine,
    edges,
    wells_sem,
    cls_sem,
    edge_sem,
):
    me = my_index()
    gx, gy = lax.axis_index("gx"), lax.axis_index("gy")
    edge_ref[...] = jnp.zeros_like(edge_ref)
    barrier = pltpu.get_barrier_semaphore()
    for_others(
        lambda dev: pl.semaphore_signal(barrier, inc=1, device_id=dev, device_id_type=MESH)
    )
    lane = lax.broadcasted_iota(jnp.int32, (32, 128), 1)
    classes = class_ref[...].reshape(CX * NZ, CY).astype(F32)
    mine[...] = classes.astype(BF16)
    for side, first in ((0, 0), (1, CY - RIM)):
        pack = jnp.zeros((32, 128), F32)
        for g in range(8):
            here = (lane >= RIM * g) & (lane < RIM * g + RIM)
            pack = jnp.where(here, roll_to(classes[32 * g : 32 * g + 32], RIM * g - first), pack)
        edges[side] = pack.astype(BF16)

    cell, test, value = cell_ref[...], test_ref[...], value_ref[...]
    n_rows = 2 * cell.shape[1]
    y = cell % (CY * N_GY)
    z = cell // (CY * N_GY) % NZ
    x = cell // (CY * N_GY * NZ)
    block = y // HALF
    within = y % HALF
    step = jnp.where(within < RIM, -1, jnp.where(within >= HALF - RIM, 1, 0))
    other = block + step
    valid = (step != 0) & (other >= 0) & (other < 2 * N_GY)

    def twice(first, second):
        return jnp.concatenate([first, second], axis=1)

    block, y, z, x = twice(block, other), twice(y, y), twice(z, z), twice(x, x)
    test, value = twice(test, test), twice(value, value)
    owner = (block % 2 * 4 + test) * N_GY + block // 2
    owner = twice(owner[:, : n_rows // 2], jnp.where(valid, owner[:, n_rows // 2 :], -1))
    y_loc = y - (block * HALF - RIM)
    x_low = x % XL
    high = ((x_low % 4 * YL + y_loc % YL) * 8 + z % 8) * 8 + z // 8
    low = x_low // 4 * 128 + x // XL * 32 + y_loc // YL
    code = (high * 256 + low).astype(F32)
    hot = jnp.where(
        lax.broadcasted_iota(jnp.int32, (DEVICES, n_rows), 0) == owner, 1.0, 0.0
    )
    earlier = jnp.where(
        lax.broadcasted_iota(jnp.int32, (n_rows, n_rows), 0)
        < lax.broadcasted_iota(jnp.int32, (n_rows, n_rows), 1),
        1.0,
        0.0,
    )
    hot16 = hot.astype(BF16)
    count = jnp.dot(hot16, earlier.astype(BF16), preferred_element_type=F32)
    rank = jnp.sum(hot * count, axis=0, keepdims=True).astype(jnp.int32)
    slot = lax.broadcasted_iota(jnp.int32, (SLOTS, n_rows), 0)
    part = jnp.concatenate(
        [jnp.where(slot == rank, code, 0.0), jnp.where(slot == rank, value, 0.0)], axis=0
    )
    total = None
    for _ in range(3):
        piece = part.astype(BF16)
        part = part - piece.astype(F32)
        term = lax.dot_general(hot16, piece, NT, preferred_element_type=F32)
        total = term if total is None else total + term
    for k in range(4):
        rows[k] = total[:, 128 * k : 128 * k + 128]
    for dev in range(DEVICES):
        for k in range(4):
            send[dev, k : k + 1, :] = rows[k, dev : dev + 1, :]

    pl.semaphore_wait(barrier, DEVICES - 1)

    def cls_copy(k):
        return pltpu.make_async_remote_copy(
            src_ref=mine,
            dst_ref=cls_ref.at[gx],
            send_sem=cls_sem.at[0],
            recv_sem=cls_sem.at[1],
            device_id=(lax.rem(gx + k, N_GX), gy),
            device_id_type=MESH,
        )

    for k in range(1, N_GX):
        cls_copy(k).start()

    def edge_copy(side, k):
        return pltpu.make_async_remote_copy(
            src_ref=edges.at[side],
            dst_ref=edge_ref.at[gx],
            send_sem=edge_sem.at[side],
            recv_sem=edge_sem.at[2],
            device_id=(k + 4 * (1 - side), lax.rem(gy + N_GY - 1 + 2 * side, N_GY)),
            device_id_type=MESH,
        )

    @pl.when(gy > 0)
    def _():
        for k in range(4):
            edge_copy(0, k).start()

    @pl.when(gy < N_GY - 1)
    def _():
        for k in range(4):
            edge_copy(1, k).start()

    cls_ref[gx] = mine[...]

    def send_rows(dev):
        pltpu.make_async_remote_copy(
            src_ref=send.at[dev[0] * N_GY + dev[1]],
            dst_ref=wells_ref.at[me],
            send_sem=wells_sem.at[0],
            recv_sem=wells_sem.at[1],
            device_id=dev,
            device_id_type=MESH,
        ).start()

    for_others(send_rows)
    wells_ref[me] = send[me]
    seven = pl.ds(0, N_GX - 1)
    pltpu.make_async_copy(cls_ref.at[seven], cls_ref.at[seven], cls_sem.at[1]).wait()
    half = gx // 4

    @pl.when(((half == 1) & (gy < N_GY - 1)) | ((half == 0) & (gy > 0)))
    def _():
        pltpu.make_async_copy(edge_ref, edge_ref, edge_sem.at[2]).wait()

    from_lane = lax.broadcasted_iota(jnp.int32, (128, 128), 0)
    to_lane = lax.broadcasted_iota(jnp.int32, (128, 128), 1)
    local = (from_lane + jnp.where(half == 0, RIM, HALF + RIM)) % 128
    picks = [
        jnp.where(local == YL * (to_lane % 32) + low, 1.0, 0.0).astype(BF16) for low in range(YL)
    ]
    lane32 = lax.broadcasted_iota(jnp.int32, (32, 128), 1)
    rim_at = jnp.where(half == 0, CY - RIM, 0)
    in_rim = (lane32 >= rim_at) & (lane32 < rim_at + RIM)
    group64 = lax.broadcasted_iota(jnp.int32, (NZ, 128), 1) // 32

    def whole(x):
        o = x // CX
        own = cls_ref[o, NZ * (x % CX) : NZ * (x % CX) + NZ, :].astype(F32)
        side = edge_ref[o].astype(F32)
        parts = []
        for g in (2 * (x % CX), 2 * (x % CX) + 1):
            moved = pltpu.roll(side, lax.rem(rim_at + 128 - RIM * g, 128), 1)
            parts.append(jnp.where(in_rim, moved, own[32 * (g % 2) : 32 * (g % 2) + 32]))
        return jnp.concatenate(parts, axis=0).astype(BF16)

    for x_low in range(XL):
        blocks = jnp.concatenate([whole(XL * h + x_low) for h in range(4)], axis=0)
        for y_low in range(YL):
            moved = jnp.dot(blocks, picks[y_low], preferred_element_type=F32)
            merged = moved[0:NZ]
            for h in range(1, 4):
                merged = jnp.where(group64 == h, moved[NZ * h : NZ * h + NZ], merged)
            value = jnp.zeros((NZ, 128), F32)
            for k in range(NCLASS):
                value = jnp.where(merged == float(k), class_value_ref[k], value)
            plane[...] = value
            for j in range(8):
                cond[x_low, y_low, tile(j), :] = plane[pl.ds(j, 8, stride=8), :]

    rest = pl.ds(0, DEVICES - 1)
    pltpu.make_async_copy(wells_ref.at[rest], wells_ref.at[rest], wells_sem.at[1]).wait()
    pltpu.make_async_copy(send.at[rest], send.at[rest], wells_sem.at[0]).wait()
    pltpu.make_async_copy(cls_ref.at[seven], cls_ref.at[seven], cls_sem.at[0]).wait()
    four = pl.ds(0, 4)

    @pl.when(gy > 0)
    def _():
        pltpu.make_async_copy(edge_ref.at[four], edge_ref.at[four], edge_sem.at[0]).wait()

    @pl.when(gy < N_GY - 1)
    def _():
        pltpu.make_async_copy(edge_ref.at[four], edge_ref.at[four], edge_sem.at[1]).wait()


def share_call(cell, test, value, classes, class_value):
    return pl.pallas_call(
        share_kernel,
        out_shape=(
            jax.ShapeDtypeStruct((DEVICES, 4, 128), F32),
            jax.ShapeDtypeStruct(FIELD, F32),
        ),
        in_specs=[VMEM] * 4 + [pl.BlockSpec(memory_space=pltpu.SMEM)],
        out_specs=(VMEM,) * 2,
        scratch_shapes=[
            pltpu.VMEM((N_GX, CX * NZ, CY), BF16),
            pltpu.VMEM((N_GX, 32, 128), BF16),
            pltpu.VMEM((NZ, 128), F32),
            pltpu.VMEM((4, DEVICES, 128), F32),
            pltpu.VMEM((DEVICES, 4, 128), F32),
            pltpu.VMEM((CX * NZ, CY), BF16),
            pltpu.VMEM((2, 32, 128), BF16),
            pltpu.SemaphoreType.DMA((2,)),
            pltpu.SemaphoreType.DMA((2,)),
            pltpu.SemaphoreType.DMA((3,)),
        ],
        compiler_params=pltpu.CompilerParams(
            collective_id=0, has_side_effects=True, vmem_limit_bytes=48 * MIB
        ),
    )(cell, test, value, classes, class_value)


def roll_to(value, shift):
    shift = shift % 128
    return pltpu.roll(value, shift, 1) if shift else value


def source_kernel(wells_ref, src_ref, rows, acc):
    for dev in range(DEVICES):
        for k in range(4):
            rows[k, dev : dev + 1, :] = wells_ref[dev, k : k + 1, :]
    lane16 = lax.broadcasted_iota(jnp.int32, (16, 128), 1)
    row_high = lax.broadcasted_iota(jnp.int32, (HIGHS, 128), 0)
    row_low = lax.broadcasted_iota(jnp.int32, (256, 128), 0)
    acc[...] = jnp.zeros_like(acc)

    def level(n, _):
        row, at = n // 8, n % 8 * CAP
        codes = jnp.zeros((16, 128), F32)
        values = jnp.zeros((16, 128), F32)
        for g in range(8):
            here = lane16 // CAP == g
            turn = lax.rem(CAP * g + 128 - at, 128)
            block = rows[row, 16 * g : 16 * g + 16, :]
            codes = jnp.where(here, pltpu.roll(block, turn, 1), codes)
            block = rows[2 + row, 16 * g : 16 * g + 16, :]
            values = jnp.where(here, pltpu.roll(block, turn, 1), values)

        @pl.when(jnp.max(jnp.abs(values)) > 0.0)
        def _():
            whole_codes = codes.astype(jnp.int32)
            highs, lows = whole_codes // 256, whole_codes % 256
            first = values.astype(BF16).astype(F32)
            second = values - first
            left, right_a, right_b = [], [], []
            for r in range(16):
                left.append(jnp.where(row_high == highs[r : r + 1], 1.0, 0.0).astype(BF16))
                same = row_low == lows[r : r + 1]
                right_a.append(jnp.where(same, first[r : r + 1], 0.0).astype(BF16))
                right_b.append(jnp.where(same, second[r : r + 1], 0.0).astype(BF16))
            left = jnp.concatenate(left, axis=1)
            acc[...] += lax.dot_general(
                left, jnp.concatenate(right_a, axis=1), NT, preferred_element_type=F32
            ) + lax.dot_general(
                left, jnp.concatenate(right_b, axis=1), NT, preferred_element_type=F32
            )

        return 0

    lax.fori_loop(0, SLOTS // CAP, level, 0)

    for x_low in range(XL):
        for y_low in range(YL):
            at = NZ * (x_low % 4 * YL + y_low)
            src_ref[x_low, y_low] = acc[at : at + NZ, x_low // 4 * 128 : x_low // 4 * 128 + 128]


def source_call(wells):
    return pl.pallas_call(
        source_kernel,
        out_shape=jax.ShapeDtypeStruct(FIELD, F32),
        in_specs=[VMEM],
        out_specs=VMEM,
        scratch_shapes=[pltpu.VMEM((4, DEVICES, 128), F32), pltpu.VMEM((HIGHS, 256), F32)],
        compiler_params=pltpu.CompilerParams(vmem_limit_bytes=48 * MIB),
    )(wells)


def groups_of(gx, gy):
    tail = gx == N_GX - 1
    low = jnp.where(tail, gy % 8, gy)
    high = jnp.where(tail, gy % 8 + 8, (gy + gx + 1) % GROUPS)
    return low, high, tail & (gy >= 8)


def takers_of(group):
    out = []
    for k in range(N_GX - 1):
        out.append(((k, group), 0))
        out.append(((k, (group + GROUPS - k - 1) % GROUPS), 1))
    place = group // 8
    out.append(((N_GX - 1, group % 8), place))
    out.append(((N_GX - 1, group % 8 + 8), place))
    return out


INNER = SHARE // 2


def main_kernel(
    cond,
    src_ref,
    zone_ref,
    draw_ref,
    out_ref,
    face_x,
    face_y,
    face_z,
    extra,
    dirs,
    resid,
    sol,
    flux,
    zone_out,
    draw_out,
    zone_in,
    draw_in,
    sens,
    acc,
    send_a,
    recv_a,
    send_b,
    recv_b,
    mine,
    zone_sem,
    draw_sem,
    a_sem,
    b_sem,
    got_sem,
    put_sem,
):
    me = my_index()
    gx, gy = lax.axis_index("gx"), lax.axis_index("gy")
    half = gx // 4
    lane = lax.broadcasted_iota(jnp.int32, (8, 128), 1)
    sub = lax.broadcasted_iota(jnp.int32, (8, 128), 0)
    x_high, y_high = lane // 32, lane % 32
    left_half = lax.broadcasted_iota(jnp.int32, (NZ, 128), 1) < HALF

    group, member = me // MEMBERS, me % MEMBERS
    low_group, high_group, _ = groups_of(gx, gy)
    takers = takers_of(group)
    barrier = pltpu.get_barrier_semaphore()
    for k in range(1, N_GX):
        pl.semaphore_signal(
            barrier, inc=1, device_id=(lax.rem(gx + k, N_GX), gy), device_id_type=MESH
        )
    for k in range(1, N_GY):
        pl.semaphore_signal(
            barrier, inc=1, device_id=(gx, lax.rem(gy + k, N_GY)), device_id_type=MESH
        )
    for held in (low_group, high_group):
        for m in range(MEMBERS):
            owner = held * MEMBERS + m

            @pl.when(owner != me)
            def _():
                pl.semaphore_signal(barrier, inc=1, device_id=coords(owner), device_id_type=MESH)

    for dev, _ in takers:

        @pl.when(dev[0] * N_GY + dev[1] != me)
        def _():
            pl.semaphore_signal(barrier, inc=1, device_id=dev, device_id_type=MESH)

    def packed(fields, side, n):
        a, b = fields[n], fields[n + 2]
        if side == 0:
            return jnp.where(left_half, a, pltpu.roll(b, HALF, 1))
        return jnp.where(left_half, pltpu.roll(a, HALF, 1), b)

    zones = [zone_ref[NZ * x : NZ * x + NZ, :].astype(F32) for x in range(CX)]
    for side in range(2):
        for n in range(2):
            zone_out[side, NZ * n : NZ * n + NZ, :] = packed(zones, side, n)
    for t in range(TESTS):
        draws = [draw_ref[t, NZ * x : NZ * x + NZ, :].astype(F32) for x in range(CX)]
        for side in range(2):
            for n in range(2):
                draw_out[TESTS * side + t, NZ * n : NZ * n + NZ, :] = packed(
                    draws, side, n
                ).astype(BF16)

    self_here = (low_group == group) | (high_group == group)
    pl.semaphore_wait(barrier, N_GX + N_GY - 2 + 32 - 2 * self_here.astype(jnp.int32))

    def to_column(k, src, dst, sems):
        dev = lax.rem(gx + k, N_GX)
        return pltpu.make_async_remote_copy(
            src_ref=src(dev),
            dst_ref=dst,
            send_sem=sems[0],
            recv_sem=sems[1],
            device_id=(dev, gy),
            device_id_type=MESH,
        )

    for k in range(1, N_GX):
        to_column(k, lambda dev: zone_out.at[dev // TESTS], zone_in.at[gx], (zone_sem.at[N_GX], zone_sem.at[gx])).start()
        to_column(k, lambda dev: draw_out.at[dev], draw_in.at[gx], (draw_sem.at[N_GX], draw_sem.at[gx])).start()
    zone_in[gx] = zone_out[half]
    draw_in[gx] = draw_out[gx]

    zero = jnp.zeros((8, 128), F32)
    first_y = jnp.where((gy == 0) & (half == 0), RIM, -1)
    last_y = jnp.where((gy == N_GY - 1) & (half == 1), RIM + HALF - 1, -2)

    def faces(x_low, _):
        for y_low in range(YL):
            y_loc = YL * y_high + y_low
            for j in range(8):
                c = cond[x_low, y_low, tile(j), :]
                more = jnp.full((8, 128), storage, F32)
                end = x_low == XL - 1
                near = cond[jnp.where(end, 0, x_low + 1), y_low, tile(j), :]
                near = jnp.where(end, pltpu.roll(near, 96, 1), near)
                off = end & (x_high == 3)
                face_x[x_low, y_low, tile(j), :] = jnp.where(off, zero, 0.5 * (c + near))
                more = more + jnp.where(off, 0.5 * c, zero)
                more = more + jnp.where((x_low == 0) & (x_high == 0), 0.5 * c, zero)
                if y_low < YL - 1:
                    near = cond[x_low, y_low + 1, tile(j), :]
                    off = y_loc + 1 == first_y
                else:
                    near = pltpu.roll(cond[x_low, 0, tile(j), :], 127, 1)
                    off = (y_loc + 1 == first_y) | (y_high == 31)
                off = off | (y_loc == last_y)
                face_y[x_low, y_low, tile(j), :] = jnp.where(off, zero, 0.5 * (c + near))
                more = more + jnp.where((y_loc == first_y) | (y_loc == last_y), 0.5 * c, zero)
                if j < 7:
                    face_z[x_low, y_low, tile(j), :] = 0.5 * (c + cond[x_low, y_low, tile(j + 1), :])
                else:
                    near = pltpu.roll(cond[x_low, y_low, tile(0), :], 7, 0)
                    face_z[x_low, y_low, tile(j), :] = jnp.where(sub == 7, zero, 0.5 * (c + near))
                    more = more + jnp.where(sub == 7, 0.5 * c, zero)
                if j == 0:
                    more = more + jnp.where(sub == 0, 0.5 * c, zero)
                extra[x_low, y_low, tile(j), :] = more
        return 0

    lax.fori_loop(0, XL, faces, 0)

    middle, factors = cheb_setup()
    for x_low in range(XL):
        for y_low in range(YL):
            value = src_ref[x_low, y_low]
            resid[x_low, y_low] = value
            dirs[0, x_low, y_low] = value / middle
            sol[x_low, y_low] = jnp.zeros((NZ, 128), F32)

    keeps = [pair[0] for pair in factors]
    news = [pair[1] for pair in factors]

    def sweep(k, _):
        par = lax.rem(k, 2)
        nxt = 1 - par
        keep, new = jnp.float32(keeps[0]), jnp.float32(news[0])
        for n in range(1, SWEEPS - 1):
            keep = jnp.where(k == n, jnp.float32(keeps[n]), keep)
            new = jnp.where(k == n, jnp.float32(news[n]), new)
        for y_low in range(YL):
            for j in range(8):
                over = face_x[XL - 1, y_low, tile(j), :] * (
                    pltpu.roll(dirs[par, 0, y_low, tile(j), :], 96, 1)
                    - dirs[par, XL - 1, y_low, tile(j), :]
                )
                flux[XL - 1, y_low, tile(j), :] = over
                flux[XL, y_low, tile(j), :] = pltpu.roll(over, 32, 1)
        for x_low in range(XL):
            behind = XL if x_low == 0 else x_low - 1
            v = [[dirs[par, x_low, y_low, tile(j), :] for y_low in range(YL)] for j in range(8)]
            z_old = []
            for y_low in range(YL):
                z_old.append(
                    pltpu.roll(
                        face_z[x_low, y_low, tile(7), :]
                        * (pltpu.roll(v[0][y_low], 7, 0) - v[7][y_low]),
                        1,
                        0,
                    )
                )
            for j in range(8):
                fy = [
                    face_y[x_low, y_low, tile(j), :]
                    * (
                        (v[j][y_low + 1] if y_low < YL - 1 else pltpu.roll(v[j][0], 127, 1))
                        - v[j][y_low]
                    )
                    for y_low in range(YL)
                ]
                for y_low in range(YL):
                    here = v[j][y_low]
                    at = (x_low, y_low, tile(j))
                    if x_low < XL - 1:
                        fx = face_x[at] * (dirs[par, x_low + 1, y_low, tile(j), :] - here)
                        flux[at] = fx
                    else:
                        fx = flux[at]
                    above = v[j + 1][y_low] if j < 7 else pltpu.roll(v[0][y_low], 7, 0)
                    fz = face_z[at] * (above - here)
                    fy_old = fy[y_low - 1] if y_low else pltpu.roll(fy[YL - 1], 1, 1)
                    gain = (fx - flux[behind, y_low, tile(j), :]) + (fy[y_low] - fy_old)
                    gain = gain + (fz - z_old[y_low])
                    z_old[y_low] = fz
                    left = resid[at] + (gain - extra[at] * here)
                    resid[at] = left
                    sol[at] = sol[at] + here
                    dirs[nxt, x_low, y_low, tile(j), :] = keep * here + new * left
        return 0

    lax.fori_loop(0, SWEEPS - 1, sweep, 0)
    last = (SWEEPS - 1) % 2

    row = lax.broadcasted_iota(jnp.int32, (YL * 128, 256), 0)
    col = lax.broadcasted_iota(jnp.int32, (YL * 128, 256), 1)
    put = jnp.where(
        (row % 128 // 32 == col // HALF)
        & (YL * (row % 32) + row // 128 == col % HALF + RIM),
        1.0,
        0.0,
    ).astype(BF16)
    for odd in range(2):
        wide = []
        for x_low in range(4 * odd, 4 * odd + 4):
            field = jnp.concatenate(
                [
                    cond[x_low, y_low] * (sol[x_low, y_low] + dirs[last, x_low, y_low])
                    for y_low in range(YL)
                ], axis=1
            )
            first = field.astype(BF16)
            second = (field - first.astype(F32)).astype(BF16)
            wide.append(
                jnp.dot(first, put, preferred_element_type=F32)
                + jnp.dot(second, put, preferred_element_type=F32)
            )
        for h in range(4):
            lanes = slice(128 * (h // 2), 128 * (h // 2) + 128)
            for n in range(2):
                a, b = wide[n][:, lanes], wide[n + 2][:, lanes]
                if h % 2 == 0:
                    both = jnp.where(left_half, a, pltpu.roll(b, 64, 1))
                else:
                    both = jnp.where(left_half, pltpu.roll(a, 64, 1), b)
                for j in range(8):
                    sens[2 * h + odd, pl.ds(NZ * n + j, 8, stride=8), :] = both[tile(j)]


    seven = pl.ds(0, N_GX - 1)

    inner = lax.broadcasted_iota(jnp.int32, (256, 128), 0).astype(F32).astype(BF16)
    one, nil = jnp.ones((), BF16), jnp.zeros((), BF16)

    def spread(row, times):
        return jnp.concatenate([jnp.broadcast_to(row, (16, 128)).astype(BF16)] * times, axis=0)

    def step(k, _):
        o = lax.rem(gx + k, N_GX)

        @pl.when(k > 0)
        def _():
            for ref, sems in ((zone_in, zone_sem), (draw_in, draw_sem)):
                pltpu.make_async_copy(ref.at[o], ref.at[o], sems.at[o]).wait()

        zone = zone_in[o]
        value = sens[o] * draw_in[o].astype(F32)
        outer = ((zone + 0.5) * (1.0 / INNER)).astype(jnp.int32)
        place = zone - outer.astype(F32) * INNER
        outer = outer // 2 % N_GY * 16 + outer // 32 * 2 + outer % 2
        outer = outer.astype(F32)
        left, right = [], []
        for r in range(2 * NZ):
            row = slice(r, r + 1)
            right.append(jnp.where(inner == spread(outer[row], 16), spread(value[row], 16), nil))
            left.append(
                jnp.concatenate(
                    [
                        jnp.where(inner == spread(place[row], 16), one, nil),
                        jnp.where(
                            inner[0 : INNER - 256]
                            == spread(place[row] - 256.0, (INNER - 256) // 16),
                            one,
                            nil,
                        ),
                    ],
                    axis=0,
                )
            )
        acc[...] += lax.dot_general(
            jnp.concatenate(left, axis=1),
            jnp.concatenate(right, axis=1),
            NT,
            preferred_element_type=F32,
        )
        return 0

    acc[...] = jnp.zeros_like(acc)
    lax.fori_loop(0, N_GX, step, 0)

    send_a[...] = acc[...].T.astype(BF16).reshape(N_GY, 16, INNER)

    def row_copy(k):
        dev = lax.rem(gy + k, N_GY)
        return pltpu.make_async_remote_copy(
            src_ref=send_a.at[dev],
            dst_ref=recv_a.at[gy],
            send_sem=a_sem.at[0],
            recv_sem=a_sem.at[1],
            device_id=(gx, dev),
            device_id_type=MESH,
        )

    for k in range(1, N_GY):
        row_copy(k).start()
    recv_a[gy] = send_a[gy]
    rest = pl.ds(0, N_GY - 1)
    pltpu.make_async_copy(recv_a.at[rest], recv_a.at[rest], a_sem.at[1]).wait()
    total = recv_a[0].astype(F32)
    for n in range(1, N_GY):
        total = total + recv_a[n].astype(F32)
    for o in range(N_GX):
        send_b[o] = total[2 * o : 2 * o + 2, :]
    for k in range(1, N_GX):
        to_column(k, lambda dev: send_b.at[dev], recv_b.at[gx], (b_sem.at[0], b_sem.at[1])).start()
    recv_b[gx] = send_b[gx]
    pltpu.make_async_copy(recv_b.at[seven], recv_b.at[seven], b_sem.at[1]).wait()
    for t in range(TESTS):
        total = (recv_b[t] + recv_b[TESTS + t]).astype(BF16).astype(F32)
        for n in range(2):
            mine[t : t + 1, INNER * n : INNER * n + INNER] = total[n : n + 1]

    def put_out(n, dev, place):
        return pltpu.make_async_remote_copy(
            src_ref=mine,
            dst_ref=out_ref.at[place, member],
            send_sem=put_sem.at[n],
            recv_sem=got_sem.at[place, member],
            device_id=dev,
            device_id_type=MESH,
        )

    for n, (dev, place) in enumerate(takers):
        taker_is_me = dev[0] * N_GY + dev[1] == me

        @pl.when(jnp.logical_not(taker_is_me))
        def _():
            put_out(n, dev, place).start()

        @pl.when(taker_is_me)
        def _():
            out_ref[place, member] = mine[...]

    pltpu.make_async_copy(send_a.at[rest], send_a.at[rest], a_sem.at[0]).wait()
    pltpu.make_async_copy(send_b.at[seven], send_b.at[seven], b_sem.at[0]).wait()
    pltpu.make_async_copy(zone_in.at[seven], zone_in.at[seven], zone_sem.at[N_GX]).wait()
    pltpu.make_async_copy(draw_in.at[seven], draw_in.at[seven], draw_sem.at[N_GX]).wait()
    for place, held in ((0, low_group), (1, high_group)):
        for m in range(MEMBERS):

            @pl.when(held * MEMBERS + m != me)
            def _():
                pltpu.make_async_copy(
                    out_ref.at[place, m], out_ref.at[place, m], got_sem.at[place, m]
                ).wait()

    for n, (dev, place) in enumerate(takers):

        @pl.when(dev[0] * N_GY + dev[1] != me)
        def _():
            put_out(n, dev, place).wait_send()


def main_call(cond, source, zone, drawdown):
    return pl.pallas_call(
        main_kernel,
        out_shape=jax.ShapeDtypeStruct((2, MEMBERS, TESTS, SHARE), F32),
        in_specs=[VMEM] * 4,
        out_specs=VMEM,
        scratch_shapes=[
            pltpu.VMEM(FIELD, F32),
            pltpu.VMEM(FIELD, F32),
            pltpu.VMEM(FIELD, F32),
            pltpu.VMEM(FIELD, F32),
            pltpu.VMEM((2,) + FIELD, F32),
            pltpu.VMEM(FIELD, F32),
            pltpu.VMEM(FIELD, F32),
            pltpu.VMEM((XL + 1, YL, NZ, 128), F32),
            pltpu.VMEM((2, 2 * NZ, 128), F32),
            pltpu.VMEM((N_GX, 2 * NZ, 128), BF16),
            pltpu.VMEM((N_GX, 2 * NZ, 128), F32),
            pltpu.VMEM((N_GX, 2 * NZ, 128), BF16),
            pltpu.VMEM((N_GX, 2 * NZ, 128), F32),
            pltpu.VMEM((INNER, 256), F32),
            pltpu.VMEM((N_GY, 16, INNER), BF16),
            pltpu.VMEM((N_GY, 16, INNER), BF16),
            pltpu.VMEM((N_GX, 2, INNER), F32),
            pltpu.VMEM((N_GX, 2, INNER), F32),
            pltpu.VMEM((TESTS, SHARE), F32),
            pltpu.SemaphoreType.DMA((N_GX + 1,)),
            pltpu.SemaphoreType.DMA((N_GX + 1,)),
            pltpu.SemaphoreType.DMA((2,)),
            pltpu.SemaphoreType.DMA((2,)),
            pltpu.SemaphoreType.DMA((2, MEMBERS)),
            pltpu.SemaphoreType.DMA((16,)),
        ],
        compiler_params=pltpu.CompilerParams(
            collective_id=1, has_side_effects=True, vmem_limit_bytes=48 * MIB
        ),
    )(cond, source, zone, drawdown)


ROWS, COLS = 1024, 512
TERMS = 128
HELP = 4


def pieces(value):
    out = []
    for _ in range(3):
        piece = value.astype(BF16).astype(F32)
        out.append(piece)
        value = value - piece
    return out


def terms(pts, as_rows):
    sub = lax.broadcasted_iota(jnp.int32, pts.shape, 0)
    norm = pieces(jnp.broadcast_to(jnp.sum(pts * pts, axis=0, keepdims=True), pts.shape))
    parts = pieces(pts)
    first = 0 if as_rows else 3
    rest = jnp.where((sub < 6) & ((sub >= 3) if as_rows else (sub < 3)), 1.0, 0.0)
    for n in range(3):
        rest = jnp.where(sub == first + n, norm[n], rest)
    blocks = [
        -2.0 * parts[i] if as_rows else parts[j] for i in range(3) for j in range(3)
    ]
    return jnp.concatenate(blocks + [rest], axis=0)


def cov_kernel(
    pts_ref,
    sums_ref,
    out_ref,
    products,
    z_ref,
    z_turned,
    row_terms,
    col_terms,
    near,
    total,
    send_c,
    recv_c,
    give_sem,
    take_sem,
):
    me = my_index()
    gx, gy = lax.axis_index("gx"), lax.axis_index("gy")
    low_group, high_group, is_diag = groups_of(gx, gy)
    group, member = me // MEMBERS, me % MEMBERS
    mode = is_diag.astype(jnp.int32) + 2 * ((gx == N_GX - 1) & (gy < 8)).astype(jnp.int32)
    takers = takers_of(group)
    barrier = pltpu.get_barrier_semaphore()
    for held in (low_group, high_group):
        for m in range(MEMBERS):
            owner = held * MEMBERS + m

            @pl.when(owner != me)
            def _():
                pl.semaphore_signal(barrier, inc=1, device_id=coords(owner), device_id_type=MESH)

    for dev, _ in takers:

        @pl.when(dev[0] * N_GY + dev[1] != me)
        def _():
            pl.semaphore_signal(barrier, inc=1, device_id=dev, device_id_type=MESH)

    products[...] = jnp.zeros_like(products)
    for g in range(2):
        for m in range(MEMBERS):
            both = jnp.concatenate([sums_ref[g, m], jnp.zeros((TESTS, SHARE), F32)], axis=0)
            z_ref[g, :, SHARE * m : SHARE * m + SHARE] = both.astype(BF16)

    def phase(rg, _):
        square = (mode == 1) | (rg == 1)
        cg = jnp.where(square, rg, 1)
        for i in range(GROUP // ROWS):
            at = slice(ROWS * i, ROWS * i + ROWS)
            row_terms[0:80, at] = terms(pts_ref[rg, :, at], True)
            row_terms[80:TERMS, at] = jnp.zeros((TERMS - 80, ROWS), F32)

        @pl.when((mode == 1) | (rg == 0))
        def _():
            for i in range(GROUP // ROWS):
                at = slice(ROWS * i, ROWS * i + ROWS)
                col_terms[0:80, at] = terms(pts_ref[cg, :, at], False).astype(BF16)
                col_terms[80:TERMS, at] = jnp.zeros((TERMS - 80, ROWS), BF16)
                wide = jnp.concatenate(
                    [z_ref[cg, :, at].astype(F32), jnp.zeros((120, ROWS), F32)], axis=0
                )
                z_turned[at, :] = wide.T.astype(BF16)

        def row_block(r, _):
            rs = pl.ds(pl.multiple_of(r * ROWS, ROWS), ROWS)
            near[...] = row_terms[:, rs].T.astype(BF16)
            total[...] = jnp.zeros_like(total)
            z_row = z_ref[rg, :, rs]

            def at_cols(c):
                return pl.ds(pl.multiple_of(c * COLS, COLS), COLS)

            def tile(c, rows):
                squared = jnp.dot(
                    near[rows, :], col_terms[:, at_cols(c)], preferred_element_type=F32
                )
                squared = jnp.maximum(squared, 1e-30)
                return jnp.exp2(squared * (-lax.rsqrt(squared))).astype(BF16)

            def for_rows(c, rows, held):
                total[rows, :] += jnp.dot(
                    held, z_turned[at_cols(c), :], preferred_element_type=F32
                )

            def for_cols(c, weights, held):
                products[cg, :, at_cols(c)] += jnp.dot(
                    weights, held, preferred_element_type=F32
                )

            every, lower = slice(0, ROWS), slice(COLS, ROWS)

            @pl.when(square)
            def _():
                held = tile(2 * r, every)
                for_rows(2 * r, every, held)
                for_cols(2 * r, z_row[:, COLS:], held[COLS:])
                for_rows(2 * r + 1, lower, tile(2 * r + 1, lower))

            def two(p, _):
                for c in (2 * p, 2 * p + 1):
                    held = tile(c, every)
                    for_rows(c, every, held)
                    for_cols(c, z_row, held)
                return 0

            lax.fori_loop(jnp.where(square, r + 1, 0), GROUP // ROWS, two, 0)
            products[rg, :, rs] += total[...].T[0:8]
            return 0

        begin = jnp.where((mode == 2) & (rg == 1), HELP, 0)
        end = jnp.where((mode == 1) & (rg == 1), HELP, GROUP // ROWS)
        lax.fori_loop(begin, end, row_block, 0)
        return 0

    lax.fori_loop(0, jnp.where(mode == 0, 1, 2), phase, 0)

    for g in range(2):
        for m in range(MEMBERS):
            send_c[g, m] = products[g, 0:TESTS, SHARE * m : SHARE * m + SHARE]

    self_here = (low_group == group) | (high_group == group)
    pl.semaphore_wait(barrier, 32 - 2 * self_here.astype(jnp.int32))

    def give(place, m, held, slot):
        return pltpu.make_async_remote_copy(
            src_ref=send_c.at[place, m],
            dst_ref=recv_c.at[slot],
            send_sem=give_sem.at[place, m],
            recv_sem=take_sem.at[slot],
            device_id=coords(held * MEMBERS + m),
            device_id_type=MESH,
        )

    sides = (
        (0, low_group, jnp.where(is_diag, low_group, high_group)),
        (1, high_group, jnp.where(is_diag, high_group, low_group)),
    )
    for place, held, slot in sides:
        for m in range(MEMBERS):

            @pl.when(held * MEMBERS + m != me)
            def _():
                give(place, m, held, slot).start()

            @pl.when(held * MEMBERS + m == me)
            def _():
                recv_c[slot] = send_c[place, m]

    own_slot = jnp.where(low_group == group, sides[0][2], sides[1][2])
    for slot in range(GROUPS):

        @pl.when(jnp.logical_not(self_here & (own_slot == slot)))
        def _():
            pltpu.make_async_copy(recv_c.at[slot], recv_c.at[slot], take_sem.at[slot]).wait()

    final = recv_c[0]
    for slot in range(1, GROUPS):
        final = final + recv_c[slot]
    out_ref[...] = final.astype(BF16)
    for place, held, slot in sides:
        for m in range(MEMBERS):

            @pl.when(held * MEMBERS + m != me)
            def _():
                give(place, m, held, slot).wait_send()


def cov_call(pts, sums):
    return pl.pallas_call(
        cov_kernel,
        out_shape=jax.ShapeDtypeStruct((TESTS, SHARE), BF16),
        in_specs=[VMEM, VMEM],
        out_specs=VMEM,
        scratch_shapes=[
            pltpu.VMEM((2, 8, GROUP), F32),
            pltpu.VMEM((2, 8, GROUP), BF16),
            pltpu.VMEM((GROUP, 128), BF16),
            pltpu.VMEM((TERMS, GROUP), F32),
            pltpu.VMEM((TERMS, GROUP), BF16),
            pltpu.VMEM((ROWS, TERMS), BF16),
            pltpu.VMEM((ROWS, 128), F32),
            pltpu.VMEM((2, MEMBERS, TESTS, SHARE), F32),
            pltpu.VMEM((GROUPS, TESTS, SHARE), F32),
            pltpu.SemaphoreType.DMA((2, MEMBERS)),
            pltpu.SemaphoreType.DMA((GROUPS,)),
        ],
        compiler_params=pltpu.CompilerParams(
            collective_id=2, has_side_effects=True, vmem_limit_bytes=48 * MIB
        ),
    )(pts, sums)


def per_device(
    well_cell, well_test, well_value, cond_class, class_value, zone_id, drawdown, centroid
):
    gx, gy = lax.axis_index("gx"), lax.axis_index("gy")
    low, high, _ = groups_of(gx, gy)
    pts = jnp.stack(
        [lax.dynamic_slice_in_dim(centroid, held * GROUP, GROUP, 1) for held in (low, high)]
    )
    pts = jnp.pad((pts - 0.5) * (LOG2E / corr_len), ((0, 0), (0, 5), (0, 0)))
    wells, cond = share_call(
        well_cell[None], well_test[None], well_value[None], cond_class, class_value
    )
    source = source_call(wells)
    rows = CX * NZ
    sums = main_call(
        cond, source, zone_id.reshape(rows, CY), drawdown.reshape(TESTS, rows, CY)
    )
    return cov_call(pts, sums)


def solution(mesh):
    return jax.shard_map(
        per_device,
        mesh=mesh,
        in_specs=(
            P(("gx", "gy")),
            P(("gx", "gy")),
            P(("gx", "gy")),
            P("gx", None, "gy"),
            P(),
            P("gx", None, "gy"),
            P(None, "gx", None, "gy"),
            P(),
        ),
        out_specs=P(None, ("gx", "gy")),
        check_vma=False,
    )
```

```python
import functools

import jax
import jax.numpy as jnp
from jax import lax
from jax.experimental import pallas as pl
from jax.experimental.pallas import tpu as pltpu
from jax.sharding import PartitionSpec as P

MESH = pl.DeviceIdType.MESH
NT = (((1,), (1,)), ((), ()))
VMEM = pl.BlockSpec(memory_space=pltpu.VMEM)
F32 = jnp.float32
BF16 = jnp.bfloat16
MIB = 2**20

SWEEPS = 12
TESTS = 4
CX, NZ, CY = 4, 64, 128
N_GX, N_GY = 8, 16
DEVICES = N_GX * N_GY
NCLASS = 16
CAP = 16
ZONES = 98304
SHARE = ZONES // DEVICES
GROUPS = 16
MEMBERS = DEVICES // GROUPS
GROUP = ZONES // GROUPS
HALF = CY // 2
RIM = 16
XL, YL = 8, 3
HIGHS = 4 * YL * NZ
SLOTS = 16 * CAP
FIELD = (XL, YL, NZ, 128)

storage = 0.02
lam_low = 0.02
lam_high = 36.02
corr_len = 0.1
LOG2E = 1.4426950408889634


def cheb_setup():
    middle = 0.5 * (lam_high + lam_low)
    spread = 0.5 * (lam_high - lam_low)
    ratio_mid = middle / spread
    current = 1.0 / ratio_mid
    factors = []
    for counter in range(SWEEPS - 1):
        updated = 1.0 / (2.0 * ratio_mid - current)
        factors.append((updated * current, 2.0 * updated / spread))
        current = updated
    return (middle, factors)


def my_index():
    return lax.axis_index("gx") * N_GY + lax.axis_index("gy")


def coords(dev):
    return (dev // N_GY, dev % N_GY)


def for_others(act):
    gx, gy = lax.axis_index("gx"), lax.axis_index("gy")
    for b in range(1, N_GY):
        act((gx, lax.rem(gy + b, N_GY)))

    def each(a, _):
        other = lax.rem(gx + a, N_GX)
        for b in range(N_GY):
            act((other, lax.rem(gy + b, N_GY)))
        return 0

    lax.fori_loop(1, N_GX, each, 0)


def tile(j):
    return slice(8 * j, 8 * j + 8)


def share_kernel(
    cell_in,
    test_in,
    value_in,
    class_in,
    class_value_ref,
    wells_ref,
    cond,
    cls_ref,
    edge_ref,
    plane,
    rows,
    send,
    mine,
    edges,
    wells_sem,
    cls_sem,
    edge_sem,
    cell_ref,
    test_ref,
    value_ref,
    class_ref,
    in_sem,
):
    inputs = [
        pltpu.make_async_copy(src, dst, in_sem.at[n])
        for n, (src, dst) in enumerate(
            (
                (cell_in, cell_ref),
                (test_in, test_ref),
                (value_in, value_ref),
                (class_in, class_ref),
            )
        )
    ]
    for copy in inputs:
        copy.start()
    me = my_index()
    gx, gy = lax.axis_index("gx"), lax.axis_index("gy")
    edge_ref[...] = jnp.zeros_like(edge_ref)
    barrier = pltpu.get_barrier_semaphore()
    for_others(
        lambda dev: pl.semaphore_signal(barrier, inc=1, device_id=dev, device_id_type=MESH)
    )
    for copy in inputs:
        copy.wait()
    lane = lax.broadcasted_iota(jnp.int32, (32, 128), 1)
    classes = class_ref[...].reshape(CX * NZ, CY).astype(F32)
    mine[...] = classes.astype(BF16)
    for side, first in ((0, 0), (1, CY - RIM)):
        pack = jnp.zeros((32, 128), F32)
        for g in range(8):
            here = (lane >= RIM * g) & (lane < RIM * g + RIM)
            pack = jnp.where(here, roll_to(classes[32 * g : 32 * g + 32], RIM * g - first), pack)
        edges[side] = pack.astype(BF16)

    cell, test, value = cell_ref[...], test_ref[...], value_ref[...]
    n_rows = 2 * cell.shape[1]
    y = cell % (CY * N_GY)
    z = cell // (CY * N_GY) % NZ
    x = cell // (CY * N_GY * NZ)
    block = y // HALF
    within = y % HALF
    step = jnp.where(within < RIM, -1, jnp.where(within >= HALF - RIM, 1, 0))
    other = block + step
    valid = (step != 0) & (other >= 0) & (other < 2 * N_GY)

    def twice(first, second):
        return jnp.concatenate([first, second], axis=1)

    block, y, z, x = twice(block, other), twice(y, y), twice(z, z), twice(x, x)
    test, value = twice(test, test), twice(value, value)
    owner = (block % 2 * 4 + test) * N_GY + block // 2
    owner = twice(owner[:, : n_rows // 2], jnp.where(valid, owner[:, n_rows // 2 :], -1))
    y_loc = y - (block * HALF - RIM)
    x_low = x % XL
    high = ((x_low % 4 * YL + y_loc % YL) * 8 + z % 8) * 8 + z // 8
    low = x_low // 4 * 128 + x // XL * 32 + y_loc // YL
    code = (high * 256 + low).astype(F32)
    hot = jnp.where(
        lax.broadcasted_iota(jnp.int32, (DEVICES, n_rows), 0) == owner, 1.0, 0.0
    )
    earlier = jnp.where(
        lax.broadcasted_iota(jnp.int32, (n_rows, n_rows), 0)
        < lax.broadcasted_iota(jnp.int32, (n_rows, n_rows), 1),
        1.0,
        0.0,
    )
    hot16 = hot.astype(BF16)
    count = jnp.dot(hot16, earlier.astype(BF16), preferred_element_type=F32)
    rank = jnp.sum(hot * count, axis=0, keepdims=True).astype(jnp.int32)
    slot = lax.broadcasted_iota(jnp.int32, (SLOTS, n_rows), 0)
    part = jnp.concatenate(
        [jnp.where(slot == rank, code, 0.0), jnp.where(slot == rank, value, 0.0)], axis=0
    )
    total = None
    for _ in range(3):
        piece = part.astype(BF16)
        part = part - piece.astype(F32)
        term = lax.dot_general(hot16, piece, NT, preferred_element_type=F32)
        total = term if total is None else total + term
    for k in range(4):
        rows[k] = total[:, 128 * k : 128 * k + 128]
    for dev in range(DEVICES):
        for k in range(4):
            send[dev, k : k + 1, :] = rows[k, dev : dev + 1, :]

    pl.semaphore_wait(barrier, DEVICES - 1)

    def cls_copy(k):
        return pltpu.make_async_remote_copy(
            src_ref=mine,
            dst_ref=cls_ref.at[gx],
            send_sem=cls_sem.at[0],
            recv_sem=cls_sem.at[1],
            device_id=(lax.rem(gx + k, N_GX), gy),
            device_id_type=MESH,
        )

    for k in range(1, N_GX):
        cls_copy(k).start()

    def edge_copy(side, k):
        return pltpu.make_async_remote_copy(
            src_ref=edges.at[side],
            dst_ref=edge_ref.at[gx],
            send_sem=edge_sem.at[side],
            recv_sem=edge_sem.at[2],
            device_id=(k + 4 * (1 - side), lax.rem(gy + N_GY - 1 + 2 * side, N_GY)),
            device_id_type=MESH,
        )

    @pl.when(gy > 0)
    def _():
        for k in range(4):
            edge_copy(0, k).start()

    @pl.when(gy < N_GY - 1)
    def _():
        for k in range(4):
            edge_copy(1, k).start()

    cls_ref[gx] = mine[...]

    def send_rows(dev):
        pltpu.make_async_remote_copy(
            src_ref=send.at[dev[0] * N_GY + dev[1]],
            dst_ref=wells_ref.at[me],
            send_sem=wells_sem.at[0],
            recv_sem=wells_sem.at[1],
            device_id=dev,
            device_id_type=MESH,
        ).start()

    for_others(send_rows)
    wells_ref[me] = send[me]
    seven = pl.ds(0, N_GX - 1)
    pltpu.make_async_copy(cls_ref.at[seven], cls_ref.at[seven], cls_sem.at[1]).wait()
    half = gx // 4

    @pl.when(((half == 1) & (gy < N_GY - 1)) | ((half == 0) & (gy > 0)))
    def _():
        pltpu.make_async_copy(edge_ref, edge_ref, edge_sem.at[2]).wait()

    from_lane = lax.broadcasted_iota(jnp.int32, (128, 128), 0)
    to_lane = lax.broadcasted_iota(jnp.int32, (128, 128), 1)
    local = (from_lane + jnp.where(half == 0, RIM, HALF + RIM)) % 128
    picks = [
        jnp.where(local == YL * (to_lane % 32) + low, 1.0, 0.0).astype(BF16) for low in range(YL)
    ]
    lane32 = lax.broadcasted_iota(jnp.int32, (32, 128), 1)
    rim_at = jnp.where(half == 0, CY - RIM, 0)
    in_rim = (lane32 >= rim_at) & (lane32 < rim_at + RIM)
    group64 = lax.broadcasted_iota(jnp.int32, (NZ, 128), 1) // 32

    def whole(x):
        o = x // CX
        own = cls_ref[o, NZ * (x % CX) : NZ * (x % CX) + NZ, :].astype(F32)
        side = edge_ref[o].astype(F32)
        parts = []
        for g in (2 * (x % CX), 2 * (x % CX) + 1):
            moved = pltpu.roll(side, lax.rem(rim_at + 128 - RIM * g, 128), 1)
            parts.append(jnp.where(in_rim, moved, own[32 * (g % 2) : 32 * (g % 2) + 32]))
        return jnp.concatenate(parts, axis=0).astype(BF16)

    for x_low in range(XL):
        blocks = jnp.concatenate([whole(XL * h + x_low) for h in range(4)], axis=0)
        for y_low in range(YL):
            moved = jnp.dot(blocks, picks[y_low], preferred_element_type=F32)
            merged = moved[0:NZ]
            for h in range(1, 4):
                merged = jnp.where(group64 == h, moved[NZ * h : NZ * h + NZ], merged)
            value = jnp.zeros((NZ, 128), F32)
            for k in range(NCLASS):
                value = jnp.where(merged == float(k), class_value_ref[k], value)
            plane[...] = value
            for j in range(8):
                cond[x_low, y_low, tile(j), :] = plane[pl.ds(j, 8, stride=8), :]

    rest = pl.ds(0, DEVICES - 1)
    pltpu.make_async_copy(wells_ref.at[rest], wells_ref.at[rest], wells_sem.at[1]).wait()
    pltpu.make_async_copy(send.at[rest], send.at[rest], wells_sem.at[0]).wait()
    pltpu.make_async_copy(cls_ref.at[seven], cls_ref.at[seven], cls_sem.at[0]).wait()
    four = pl.ds(0, 4)

    @pl.when(gy > 0)
    def _():
        pltpu.make_async_copy(edge_ref.at[four], edge_ref.at[four], edge_sem.at[0]).wait()

    @pl.when(gy < N_GY - 1)
    def _():
        pltpu.make_async_copy(edge_ref.at[four], edge_ref.at[four], edge_sem.at[1]).wait()


def share_call(cell, test, value, classes, class_value):
    return pl.pallas_call(
        share_kernel,
        out_shape=(
            jax.ShapeDtypeStruct((DEVICES, 4, 128), F32),
            jax.ShapeDtypeStruct(FIELD, F32),
        ),
        in_specs=[pl.BlockSpec(memory_space=pl.ANY)] * 4
        + [pl.BlockSpec(memory_space=pltpu.SMEM)],
        out_specs=(VMEM,) * 2,
        scratch_shapes=[
            pltpu.VMEM((N_GX, CX * NZ, CY), BF16),
            pltpu.VMEM((N_GX, 32, 128), BF16),
            pltpu.VMEM((NZ, 128), F32),
            pltpu.VMEM((4, DEVICES, 128), F32),
            pltpu.VMEM((DEVICES, 4, 128), F32),
            pltpu.VMEM((CX * NZ, CY), BF16),
            pltpu.VMEM((2, 32, 128), BF16),
            pltpu.SemaphoreType.DMA((2,)),
            pltpu.SemaphoreType.DMA((2,)),
            pltpu.SemaphoreType.DMA((3,)),
            pltpu.VMEM(cell.shape, jnp.int32),
            pltpu.VMEM(test.shape, jnp.int32),
            pltpu.VMEM(value.shape, F32),
            pltpu.VMEM(classes.shape, jnp.int32),
            pltpu.SemaphoreType.DMA((4,)),
        ],
        compiler_params=pltpu.CompilerParams(
            collective_id=0, has_side_effects=True, vmem_limit_bytes=48 * MIB
        ),
    )(cell, test, value, classes, class_value)


def roll_to(value, shift):
    shift = shift % 128
    return pltpu.roll(value, shift, 1) if shift else value


def source_kernel(wells_ref, src_ref, rows, acc):
    for dev in range(DEVICES):
        for k in range(4):
            rows[k, dev : dev + 1, :] = wells_ref[dev, k : k + 1, :]
    lane16 = lax.broadcasted_iota(jnp.int32, (16, 128), 1)
    row_high = lax.broadcasted_iota(jnp.int32, (HIGHS, 128), 0)
    row_low = lax.broadcasted_iota(jnp.int32, (256, 128), 0)
    acc[...] = jnp.zeros_like(acc)

    def level(n, _):
        row, at = n // 8, n % 8 * CAP
        codes = jnp.zeros((16, 128), F32)
        values = jnp.zeros((16, 128), F32)
        for g in range(8):
            here = lane16 // CAP == g
            turn = lax.rem(CAP * g + 128 - at, 128)
            block = rows[row, 16 * g : 16 * g + 16, :]
            codes = jnp.where(here, pltpu.roll(block, turn, 1), codes)
            block = rows[2 + row, 16 * g : 16 * g + 16, :]
            values = jnp.where(here, pltpu.roll(block, turn, 1), values)

        @pl.when(jnp.max(jnp.abs(values)) > 0.0)
        def _():
            whole_codes = codes.astype(jnp.int32)
            highs, lows = whole_codes // 256, whole_codes % 256
            first = values.astype(BF16).astype(F32)
            second = values - first
            left, right_a, right_b = [], [], []
            for r in range(16):
                left.append(jnp.where(row_high == highs[r : r + 1], 1.0, 0.0).astype(BF16))
                same = row_low == lows[r : r + 1]
                right_a.append(jnp.where(same, first[r : r + 1], 0.0).astype(BF16))
                right_b.append(jnp.where(same, second[r : r + 1], 0.0).astype(BF16))
            left = jnp.concatenate(left, axis=1)
            acc[...] += lax.dot_general(
                left, jnp.concatenate(right_a, axis=1), NT, preferred_element_type=F32
            ) + lax.dot_general(
                left, jnp.concatenate(right_b, axis=1), NT, preferred_element_type=F32
            )

        return 0

    lax.fori_loop(0, SLOTS // CAP, level, 0)

    for x_low in range(XL):
        for y_low in range(YL):
            at = NZ * (x_low % 4 * YL + y_low)
            src_ref[x_low, y_low] = acc[at : at + NZ, x_low // 4 * 128 : x_low // 4 * 128 + 128]


def source_call(wells):
    return pl.pallas_call(
        source_kernel,
        out_shape=jax.ShapeDtypeStruct(FIELD, F32),
        in_specs=[VMEM],
        out_specs=VMEM,
        scratch_shapes=[pltpu.VMEM((4, DEVICES, 128), F32), pltpu.VMEM((HIGHS, 256), F32)],
        compiler_params=pltpu.CompilerParams(vmem_limit_bytes=48 * MIB),
    )(wells)


def groups_of(gx, gy):
    tail = gx == N_GX - 1
    low = jnp.where(tail, gy % 8, gy)
    high = jnp.where(tail, gy % 8 + 8, (gy + gx + 1) % GROUPS)
    return low, high, tail & (gy >= 8)


def takers_of(group):
    out = []
    for k in range(N_GX - 1):
        out.append(((k, group), 0))
        out.append(((k, (group + GROUPS - k - 1) % GROUPS), 1))
    place = group // 8
    out.append(((N_GX - 1, group % 8), place))
    out.append(((N_GX - 1, group % 8 + 8), place))
    return out


INNER = SHARE // 2


def main_kernel(
    cond,
    src_ref,
    zone_ref,
    draw_ref,
    out_ref,
    face_x,
    face_y,
    face_z,
    extra,
    dirs,
    resid,
    sol,
    flux,
    zone_out,
    draw_out,
    zone_in,
    draw_in,
    sens,
    acc,
    send_a,
    recv_a,
    send_b,
    recv_b,
    mine,
    zone_sem,
    draw_sem,
    a_sem,
    b_sem,
    got_sem,
    put_sem,
):
    me = my_index()
    gx, gy = lax.axis_index("gx"), lax.axis_index("gy")
    half = gx // 4
    lane = lax.broadcasted_iota(jnp.int32, (8, 128), 1)
    sub = lax.broadcasted_iota(jnp.int32, (8, 128), 0)
    x_high, y_high = lane // 32, lane % 32
    left_half = lax.broadcasted_iota(jnp.int32, (NZ, 128), 1) < HALF

    group, member = me // MEMBERS, me % MEMBERS
    low_group, high_group, _ = groups_of(gx, gy)
    takers = takers_of(group)
    barrier = pltpu.get_barrier_semaphore()
    for k in range(1, N_GX):
        pl.semaphore_signal(
            barrier, inc=1, device_id=(lax.rem(gx + k, N_GX), gy), device_id_type=MESH
        )
    for k in range(1, N_GY):
        pl.semaphore_signal(
            barrier, inc=1, device_id=(gx, lax.rem(gy + k, N_GY)), device_id_type=MESH
        )
    for held in (low_group, high_group):
        for m in range(MEMBERS):
            owner = held * MEMBERS + m

            @pl.when(owner != me)
            def _():
                pl.semaphore_signal(barrier, inc=1, device_id=coords(owner), device_id_type=MESH)

    for dev, _ in takers:

        @pl.when(dev[0] * N_GY + dev[1] != me)
        def _():
            pl.semaphore_signal(barrier, inc=1, device_id=dev, device_id_type=MESH)

    def packed(fields, side, n):
        a, b = fields[n], fields[n + 2]
        if side == 0:
            return jnp.where(left_half, a, pltpu.roll(b, HALF, 1))
        return jnp.where(left_half, pltpu.roll(a, HALF, 1), b)

    zones = [zone_ref[NZ * x : NZ * x + NZ, :].astype(F32) for x in range(CX)]
    for side in range(2):
        for n in range(2):
            zone_out[side, NZ * n : NZ * n + NZ, :] = packed(zones, side, n)
    for t in range(TESTS):
        draws = [draw_ref[t, NZ * x : NZ * x + NZ, :].astype(F32) for x in range(CX)]
        for side in range(2):
            for n in range(2):
                draw_out[TESTS * side + t, NZ * n : NZ * n + NZ, :] = packed(
                    draws, side, n
                ).astype(BF16)

    self_here = (low_group == group) | (high_group == group)
    pl.semaphore_wait(barrier, N_GX + N_GY - 2 + 32 - 2 * self_here.astype(jnp.int32))

    def to_column(k, src, dst, sems):
        dev = lax.rem(gx + k, N_GX)
        return pltpu.make_async_remote_copy(
            src_ref=src(dev),
            dst_ref=dst,
            send_sem=sems[0],
            recv_sem=sems[1],
            device_id=(dev, gy),
            device_id_type=MESH,
        )

    for k in range(1, N_GX):
        to_column(k, lambda dev: zone_out.at[dev // TESTS], zone_in.at[gx], (zone_sem.at[N_GX], zone_sem.at[gx])).start()
        to_column(k, lambda dev: draw_out.at[dev], draw_in.at[gx], (draw_sem.at[N_GX], draw_sem.at[gx])).start()
    zone_in[gx] = zone_out[half]
    draw_in[gx] = draw_out[gx]

    zero = jnp.zeros((8, 128), F32)
    first_y = jnp.where((gy == 0) & (half == 0), RIM, -1)
    last_y = jnp.where((gy == N_GY - 1) & (half == 1), RIM + HALF - 1, -2)

    def faces(x_low, _):
        for y_low in range(YL):
            y_loc = YL * y_high + y_low
            for j in range(8):
                c = cond[x_low, y_low, tile(j), :]
                more = jnp.full((8, 128), storage, F32)
                end = x_low == XL - 1
                near = cond[jnp.where(end, 0, x_low + 1), y_low, tile(j), :]
                near = jnp.where(end, pltpu.roll(near, 96, 1), near)
                off = end & (x_high == 3)
                face_x[x_low, y_low, tile(j), :] = jnp.where(off, zero, 0.5 * (c + near))
                more = more + jnp.where(off, 0.5 * c, zero)
                more = more + jnp.where((x_low == 0) & (x_high == 0), 0.5 * c, zero)
                if y_low < YL - 1:
                    near = cond[x_low, y_low + 1, tile(j), :]
                    off = y_loc + 1 == first_y
                else:
                    near = pltpu.roll(cond[x_low, 0, tile(j), :], 127, 1)
                    off = (y_loc + 1 == first_y) | (y_high == 31)
                off = off | (y_loc == last_y)
                face_y[x_low, y_low, tile(j), :] = jnp.where(off, zero, 0.5 * (c + near))
                more = more + jnp.where((y_loc == first_y) | (y_loc == last_y), 0.5 * c, zero)
                if j < 7:
                    face_z[x_low, y_low, tile(j), :] = 0.5 * (c + cond[x_low, y_low, tile(j + 1), :])
                else:
                    near = pltpu.roll(cond[x_low, y_low, tile(0), :], 7, 0)
                    face_z[x_low, y_low, tile(j), :] = jnp.where(sub == 7, zero, 0.5 * (c + near))
                    more = more + jnp.where(sub == 7, 0.5 * c, zero)
                if j == 0:
                    more = more + jnp.where(sub == 0, 0.5 * c, zero)
                extra[x_low, y_low, tile(j), :] = more
        return 0

    lax.fori_loop(0, XL, faces, 0)

    middle, factors = cheb_setup()
    for x_low in range(XL):
        for y_low in range(YL):
            value = src_ref[x_low, y_low]
            resid[x_low, y_low] = value
            dirs[0, x_low, y_low] = value / middle
            sol[x_low, y_low] = jnp.zeros((NZ, 128), F32)

    keeps = [pair[0] for pair in factors]
    news = [pair[1] for pair in factors]

    def sweep(k, _):
        par = lax.rem(k, 2)
        nxt = 1 - par
        keep, new = jnp.float32(keeps[0]), jnp.float32(news[0])
        for n in range(1, SWEEPS - 1):
            keep = jnp.where(k == n, jnp.float32(keeps[n]), keep)
            new = jnp.where(k == n, jnp.float32(news[n]), new)
        for y_low in range(YL):
            for j in range(8):
                over = face_x[XL - 1, y_low, tile(j), :] * (
                    pltpu.roll(dirs[par, 0, y_low, tile(j), :], 96, 1)
                    - dirs[par, XL - 1, y_low, tile(j), :]
                )
                flux[XL - 1, y_low, tile(j), :] = over
                flux[XL, y_low, tile(j), :] = pltpu.roll(over, 32, 1)
        for x_low in range(XL):
            behind = XL if x_low == 0 else x_low - 1
            v = [[dirs[par, x_low, y_low, tile(j), :] for y_low in range(YL)] for j in range(8)]
            z_old = []
            for y_low in range(YL):
                z_old.append(
                    pltpu.roll(
                        face_z[x_low, y_low, tile(7), :]
                        * (pltpu.roll(v[0][y_low], 7, 0) - v[7][y_low]),
                        1,
                        0,
                    )
                )
            for j in range(8):
                fy = [
                    face_y[x_low, y_low, tile(j), :]
                    * (
                        (v[j][y_low + 1] if y_low < YL - 1 else pltpu.roll(v[j][0], 127, 1))
                        - v[j][y_low]
                    )
                    for y_low in range(YL)
                ]
                for y_low in range(YL):
                    here = v[j][y_low]
                    at = (x_low, y_low, tile(j))
                    if x_low < XL - 1:
                        fx = face_x[at] * (dirs[par, x_low + 1, y_low, tile(j), :] - here)
                        flux[at] = fx
                    else:
                        fx = flux[at]
                    above = v[j + 1][y_low] if j < 7 else pltpu.roll(v[0][y_low], 7, 0)
                    fz = face_z[at] * (above - here)
                    fy_old = fy[y_low - 1] if y_low else pltpu.roll(fy[YL - 1], 1, 1)
                    gain = (fx - flux[behind, y_low, tile(j), :]) + (fy[y_low] - fy_old)
                    gain = gain + (fz - z_old[y_low])
                    z_old[y_low] = fz
                    left = resid[at] + (gain - extra[at] * here)
                    resid[at] = left
                    sol[at] = sol[at] + here
                    dirs[nxt, x_low, y_low, tile(j), :] = keep * here + new * left
        return 0

    lax.fori_loop(0, SWEEPS - 1, sweep, 0)
    last = (SWEEPS - 1) % 2

    row = lax.broadcasted_iota(jnp.int32, (YL * 128, 256), 0)
    col = lax.broadcasted_iota(jnp.int32, (YL * 128, 256), 1)
    put = jnp.where(
        (row % 128 // 32 == col // HALF)
        & (YL * (row % 32) + row // 128 == col % HALF + RIM),
        1.0,
        0.0,
    ).astype(BF16)
    for odd in range(2):
        wide = []
        for x_low in range(4 * odd, 4 * odd + 4):
            field = jnp.concatenate(
                [
                    cond[x_low, y_low] * (sol[x_low, y_low] + dirs[last, x_low, y_low])
                    for y_low in range(YL)
                ], axis=1
            )
            first = field.astype(BF16)
            second = (field - first.astype(F32)).astype(BF16)
            wide.append(
                jnp.dot(first, put, preferred_element_type=F32)
                + jnp.dot(second, put, preferred_element_type=F32)
            )
        for h in range(4):
            lanes = slice(128 * (h // 2), 128 * (h // 2) + 128)
            for n in range(2):
                a, b = wide[n][:, lanes], wide[n + 2][:, lanes]
                if h % 2 == 0:
                    both = jnp.where(left_half, a, pltpu.roll(b, 64, 1))
                else:
                    both = jnp.where(left_half, pltpu.roll(a, 64, 1), b)
                for j in range(8):
                    sens[2 * h + odd, pl.ds(NZ * n + j, 8, stride=8), :] = both[tile(j)]


    seven = pl.ds(0, N_GX - 1)

    inner = lax.broadcasted_iota(jnp.int32, (256, 128), 0).astype(F32).astype(BF16)
    one, nil = jnp.ones((), BF16), jnp.zeros((), BF16)

    def spread(row, times):
        return jnp.concatenate([jnp.broadcast_to(row, (16, 128)).astype(BF16)] * times, axis=0)

    def step(k, _):
        o = lax.rem(gx + k, N_GX)

        @pl.when(k > 0)
        def _():
            for ref, sems in ((zone_in, zone_sem), (draw_in, draw_sem)):
                pltpu.make_async_copy(ref.at[o], ref.at[o], sems.at[o]).wait()

        zone = zone_in[o]
        value = sens[o] * draw_in[o].astype(F32)
        outer = ((zone + 0.5) * (1.0 / INNER)).astype(jnp.int32)
        place = zone - outer.astype(F32) * INNER
        outer = outer // 2 % N_GY * 16 + outer // 32 * 2 + outer % 2
        outer = outer.astype(F32)
        left, right = [], []
        for r in range(2 * NZ):
            row = slice(r, r + 1)
            right.append(jnp.where(inner == spread(outer[row], 16), spread(value[row], 16), nil))
            left.append(
                jnp.concatenate(
                    [
                        jnp.where(inner == spread(place[row], 16), one, nil),
                        jnp.where(
                            inner[0 : INNER - 256]
                            == spread(place[row] - 256.0, (INNER - 256) // 16),
                            one,
                            nil,
                        ),
                    ],
                    axis=0,
                )
            )
        acc[...] += lax.dot_general(
            jnp.concatenate(left, axis=1),
            jnp.concatenate(right, axis=1),
            NT,
            preferred_element_type=F32,
        )
        return 0

    acc[...] = jnp.zeros_like(acc)
    lax.fori_loop(0, N_GX, step, 0)

    send_a[...] = acc[...].T.astype(BF16).reshape(N_GY, 16, INNER)

    def row_copy(k):
        dev = lax.rem(gy + k, N_GY)
        return pltpu.make_async_remote_copy(
            src_ref=send_a.at[dev],
            dst_ref=recv_a.at[gy],
            send_sem=a_sem.at[0],
            recv_sem=a_sem.at[1],
            device_id=(gx, dev),
            device_id_type=MESH,
        )

    for k in range(1, N_GY):
        row_copy(k).start()
    recv_a[gy] = send_a[gy]
    rest = pl.ds(0, N_GY - 1)
    pltpu.make_async_copy(recv_a.at[rest], recv_a.at[rest], a_sem.at[1]).wait()
    total = recv_a[0].astype(F32)
    for n in range(1, N_GY):
        total = total + recv_a[n].astype(F32)
    for o in range(N_GX):
        send_b[o] = total[2 * o : 2 * o + 2, :]
    for k in range(1, N_GX):
        to_column(k, lambda dev: send_b.at[dev], recv_b.at[gx], (b_sem.at[0], b_sem.at[1])).start()
    recv_b[gx] = send_b[gx]
    pltpu.make_async_copy(recv_b.at[seven], recv_b.at[seven], b_sem.at[1]).wait()
    for t in range(TESTS):
        total = (recv_b[t] + recv_b[TESTS + t]).astype(BF16).astype(F32)
        for n in range(2):
            mine[t : t + 1, INNER * n : INNER * n + INNER] = total[n : n + 1]

    def put_out(n, dev, place):
        return pltpu.make_async_remote_copy(
            src_ref=mine,
            dst_ref=out_ref.at[place, member],
            send_sem=put_sem.at[n],
            recv_sem=got_sem.at[place, member],
            device_id=dev,
            device_id_type=MESH,
        )

    for n, (dev, place) in enumerate(takers):
        taker_is_me = dev[0] * N_GY + dev[1] == me

        @pl.when(jnp.logical_not(taker_is_me))
        def _():
            put_out(n, dev, place).start()

        @pl.when(taker_is_me)
        def _():
            out_ref[place, member] = mine[...]

    pltpu.make_async_copy(send_a.at[rest], send_a.at[rest], a_sem.at[0]).wait()
    pltpu.make_async_copy(send_b.at[seven], send_b.at[seven], b_sem.at[0]).wait()
    pltpu.make_async_copy(zone_in.at[seven], zone_in.at[seven], zone_sem.at[N_GX]).wait()
    pltpu.make_async_copy(draw_in.at[seven], draw_in.at[seven], draw_sem.at[N_GX]).wait()
    for place, held in ((0, low_group), (1, high_group)):
        for m in range(MEMBERS):

            @pl.when(held * MEMBERS + m != me)
            def _():
                pltpu.make_async_copy(
                    out_ref.at[place, m], out_ref.at[place, m], got_sem.at[place, m]
                ).wait()

    for n, (dev, place) in enumerate(takers):

        @pl.when(dev[0] * N_GY + dev[1] != me)
        def _():
            put_out(n, dev, place).wait_send()


def main_call(cond, source, zone, drawdown):
    return pl.pallas_call(
        main_kernel,
        out_shape=jax.ShapeDtypeStruct((2, MEMBERS, TESTS, SHARE), F32),
        in_specs=[VMEM] * 4,
        out_specs=VMEM,
        scratch_shapes=[
            pltpu.VMEM(FIELD, F32),
            pltpu.VMEM(FIELD, F32),
            pltpu.VMEM(FIELD, F32),
            pltpu.VMEM(FIELD, F32),
            pltpu.VMEM((2,) + FIELD, F32),
            pltpu.VMEM(FIELD, F32),
            pltpu.VMEM(FIELD, F32),
            pltpu.VMEM((XL + 1, YL, NZ, 128), F32),
            pltpu.VMEM((2, 2 * NZ, 128), F32),
            pltpu.VMEM((N_GX, 2 * NZ, 128), BF16),
            pltpu.VMEM((N_GX, 2 * NZ, 128), F32),
            pltpu.VMEM((N_GX, 2 * NZ, 128), BF16),
            pltpu.VMEM((N_GX, 2 * NZ, 128), F32),
            pltpu.VMEM((INNER, 256), F32),
            pltpu.VMEM((N_GY, 16, INNER), BF16),
            pltpu.VMEM((N_GY, 16, INNER), BF16),
            pltpu.VMEM((N_GX, 2, INNER), F32),
            pltpu.VMEM((N_GX, 2, INNER), F32),
            pltpu.VMEM((TESTS, SHARE), F32),
            pltpu.SemaphoreType.DMA((N_GX + 1,)),
            pltpu.SemaphoreType.DMA((N_GX + 1,)),
            pltpu.SemaphoreType.DMA((2,)),
            pltpu.SemaphoreType.DMA((2,)),
            pltpu.SemaphoreType.DMA((2, MEMBERS)),
            pltpu.SemaphoreType.DMA((16,)),
        ],
        compiler_params=pltpu.CompilerParams(
            collective_id=1, has_side_effects=True, vmem_limit_bytes=48 * MIB
        ),
    )(cond, source, zone, drawdown)


ROWS, COLS = 1024, 512
TERMS = 128
HELP = 4


def pieces(value):
    out = []
    for _ in range(3):
        piece = value.astype(BF16).astype(F32)
        out.append(piece)
        value = value - piece
    return out


def terms(pts, as_rows):
    sub = lax.broadcasted_iota(jnp.int32, pts.shape, 0)
    norm = pieces(jnp.broadcast_to(jnp.sum(pts * pts, axis=0, keepdims=True), pts.shape))
    parts = pieces(pts)
    first = 0 if as_rows else 3
    rest = jnp.where((sub < 6) & ((sub >= 3) if as_rows else (sub < 3)), 1.0, 0.0)
    for n in range(3):
        rest = jnp.where(sub == first + n, norm[n], rest)
    blocks = [
        -2.0 * parts[i] if as_rows else parts[j] for i in range(3) for j in range(3)
    ]
    return jnp.concatenate(blocks + [rest], axis=0)


def cov_kernel(
    pts_ref,
    sums_ref,
    out_ref,
    products,
    z_ref,
    z_turned,
    row_terms,
    col_terms,
    near,
    total,
    send_c,
    recv_c,
    give_sem,
    take_sem,
):
    me = my_index()
    gx, gy = lax.axis_index("gx"), lax.axis_index("gy")
    low_group, high_group, is_diag = groups_of(gx, gy)
    group, member = me // MEMBERS, me % MEMBERS
    mode = is_diag.astype(jnp.int32) + 2 * ((gx == N_GX - 1) & (gy < 8)).astype(jnp.int32)
    takers = takers_of(group)
    barrier = pltpu.get_barrier_semaphore()
    for held in (low_group, high_group):
        for m in range(MEMBERS):
            owner = held * MEMBERS + m

            @pl.when(owner != me)
            def _():
                pl.semaphore_signal(barrier, inc=1, device_id=coords(owner), device_id_type=MESH)

    for dev, _ in takers:

        @pl.when(dev[0] * N_GY + dev[1] != me)
        def _():
            pl.semaphore_signal(barrier, inc=1, device_id=dev, device_id_type=MESH)

    products[...] = jnp.zeros_like(products)
    for g in range(2):
        for m in range(MEMBERS):
            both = jnp.concatenate([sums_ref[g, m], jnp.zeros((TESTS, SHARE), F32)], axis=0)
            z_ref[g, :, SHARE * m : SHARE * m + SHARE] = both.astype(BF16)

    def phase(rg, _):
        square = (mode == 1) | (rg == 1)
        cg = jnp.where(square, rg, 1)
        for i in range(GROUP // ROWS):
            at = slice(ROWS * i, ROWS * i + ROWS)
            row_terms[0:80, at] = terms(pts_ref[rg, :, at], True)
            row_terms[80:TERMS, at] = jnp.zeros((TERMS - 80, ROWS), F32)

        @pl.when((mode == 1) | (rg == 0))
        def _():
            for i in range(GROUP // ROWS):
                at = slice(ROWS * i, ROWS * i + ROWS)
                col_terms[0:80, at] = terms(pts_ref[cg, :, at], False).astype(BF16)
                col_terms[80:TERMS, at] = jnp.zeros((TERMS - 80, ROWS), BF16)
                wide = jnp.concatenate(
                    [z_ref[cg, :, at].astype(F32), jnp.zeros((120, ROWS), F32)], axis=0
                )
                z_turned[at, :] = wide.T.astype(BF16)

        def row_block(r, _):
            rs = pl.ds(pl.multiple_of(r * ROWS, ROWS), ROWS)
            near[...] = row_terms[:, rs].T.astype(BF16)
            total[...] = jnp.zeros_like(total)
            z_row = z_ref[rg, :, rs]

            def at_cols(c):
                return pl.ds(pl.multiple_of(c * COLS, COLS), COLS)

            def tile(c, rows):
                squared = jnp.dot(
                    near[rows, :], col_terms[:, at_cols(c)], preferred_element_type=F32
                )
                squared = jnp.maximum(squared, 1e-30)
                return jnp.exp2(squared * (-lax.rsqrt(squared))).astype(BF16)

            def for_rows(c, rows, held):
                total[rows, :] += jnp.dot(
                    held, z_turned[at_cols(c), :], preferred_element_type=F32
                )

            def for_cols(c, weights, held):
                products[cg, :, at_cols(c)] += jnp.dot(
                    weights, held, preferred_element_type=F32
                )

            every, lower = slice(0, ROWS), slice(COLS, ROWS)

            @pl.when(square)
            def _():
                held = tile(2 * r, every)
                for_rows(2 * r, every, held)
                for_cols(2 * r, z_row[:, COLS:], held[COLS:])
                for_rows(2 * r + 1, lower, tile(2 * r + 1, lower))

            def two(p, _):
                for c in (2 * p, 2 * p + 1):
                    held = tile(c, every)
                    for_rows(c, every, held)
                    for_cols(c, z_row, held)
                return 0

            lax.fori_loop(jnp.where(square, r + 1, 0), GROUP // ROWS, two, 0)
            products[rg, :, rs] += total[...].T[0:8]
            return 0

        begin = jnp.where((mode == 2) & (rg == 1), HELP, 0)
        end = jnp.where((mode == 1) & (rg == 1), HELP, GROUP // ROWS)
        lax.fori_loop(begin, end, row_block, 0)
        return 0

    lax.fori_loop(0, jnp.where(mode == 0, 1, 2), phase, 0)

    for g in range(2):
        for m in range(MEMBERS):
            send_c[g, m] = products[g, 0:TESTS, SHARE * m : SHARE * m + SHARE]

    self_here = (low_group == group) | (high_group == group)
    pl.semaphore_wait(barrier, 32 - 2 * self_here.astype(jnp.int32))

    def give(place, m, held, slot):
        return pltpu.make_async_remote_copy(
            src_ref=send_c.at[place, m],
            dst_ref=recv_c.at[slot],
            send_sem=give_sem.at[place, m],
            recv_sem=take_sem.at[slot],
            device_id=coords(held * MEMBERS + m),
            device_id_type=MESH,
        )

    sides = (
        (0, low_group, jnp.where(is_diag, low_group, high_group)),
        (1, high_group, jnp.where(is_diag, high_group, low_group)),
    )
    for place, held, slot in sides:
        for m in range(MEMBERS):

            @pl.when(held * MEMBERS + m != me)
            def _():
                give(place, m, held, slot).start()

            @pl.when(held * MEMBERS + m == me)
            def _():
                recv_c[slot] = send_c[place, m]

    own_slot = jnp.where(low_group == group, sides[0][2], sides[1][2])
    for slot in range(GROUPS):

        @pl.when(jnp.logical_not(self_here & (own_slot == slot)))
        def _():
            pltpu.make_async_copy(recv_c.at[slot], recv_c.at[slot], take_sem.at[slot]).wait()

    final = recv_c[0]
    for slot in range(1, GROUPS):
        final = final + recv_c[slot]
    out_ref[...] = final.astype(BF16)
    for place, held, slot in sides:
        for m in range(MEMBERS):

            @pl.when(held * MEMBERS + m != me)
            def _():
                give(place, m, held, slot).wait_send()


def cov_call(pts, sums):
    return pl.pallas_call(
        cov_kernel,
        out_shape=jax.ShapeDtypeStruct((TESTS, SHARE), BF16),
        in_specs=[VMEM, VMEM],
        out_specs=VMEM,
        scratch_shapes=[
            pltpu.VMEM((2, 8, GROUP), F32),
            pltpu.VMEM((2, 8, GROUP), BF16),
            pltpu.VMEM((GROUP, 128), BF16),
            pltpu.VMEM((TERMS, GROUP), F32),
            pltpu.VMEM((TERMS, GROUP), BF16),
            pltpu.VMEM((ROWS, TERMS), BF16),
            pltpu.VMEM((ROWS, 128), F32),
            pltpu.VMEM((2, MEMBERS, TESTS, SHARE), F32),
            pltpu.VMEM((GROUPS, TESTS, SHARE), F32),
            pltpu.SemaphoreType.DMA((2, MEMBERS)),
            pltpu.SemaphoreType.DMA((GROUPS,)),
        ],
        compiler_params=pltpu.CompilerParams(
            collective_id=2, has_side_effects=True, vmem_limit_bytes=48 * MIB
        ),
    )(pts, sums)


def per_device(
    well_cell, well_test, well_value, cond_class, class_value, zone_id, drawdown, centroid
):
    gx, gy = lax.axis_index("gx"), lax.axis_index("gy")
    low, high, _ = groups_of(gx, gy)
    pts = jnp.stack(
        [lax.dynamic_slice_in_dim(centroid, held * GROUP, GROUP, 1) for held in (low, high)]
    )
    pts = jnp.pad((pts - 0.5) * (LOG2E / corr_len), ((0, 0), (0, 5), (0, 0)))
    wells, cond = share_call(
        well_cell[None], well_test[None], well_value[None], cond_class, class_value
    )
    source = source_call(wells)
    rows = CX * NZ
    sums = main_call(
        cond, source, zone_id.reshape(rows, CY), drawdown.reshape(TESTS, rows, CY)
    )
    return cov_call(pts, sums)


def solution(mesh):
    return jax.shard_map(
        per_device,
        mesh=mesh,
        in_specs=(
            P(("gx", "gy")),
            P(("gx", "gy")),
            P(("gx", "gy")),
            P("gx", None, "gy"),
            P(),
            P("gx", None, "gy"),
            P(None, "gx", None, "gy"),
            P(),
        ),
        out_specs=P(None, ("gx", "gy")),
        check_vma=False,
    )
```
